32 devices in a mesh: seq: 4 (over y, x), batch: 8 (over z, core).
Axes of the slice: x: 2, y: 2, z: 4, core: 2. Of those that a mesh axis runs over, the one named last changes fastest.
Arguments:
- inputs: bfloat16 [512, 64, 768], P('seq', 'batch'), may hold values from -6 to 6
- lengths: int32 [64], P('batch'), may hold values from 128 to 512, as said below
- norm1_gain: float32 [768], replicated, may hold values from 0.1 to 1.9
- in_weight: bfloat16 [768, 2304], replicated, may hold values from -0.21875 to 0.21875
- short_taps: float32 [3, 2304], replicated, may hold values from -3 to 3
- static_kernel: float32 [512, 768], replicated, may hold values from -0.25 to 0.25
- out_weight: bfloat16 [768, 768], replicated, may hold values from -0.21875 to 0.21875
- norm2_gain: float32 [768], replicated, may hold values from 0.1 to 1.9
- glu_weight: bfloat16 [768, 6144], replicated, may hold values from -0.21875 to 0.21875
- down_weight: bfloat16 [3072, 768], replicated, may hold values from -0.109375 to 0.109375
- cotangent: bfloat16 [512, 64, 768], P('seq', 'batch'), may hold values from -6 to 6
Outputs:
- output: bfloat16 [512, 64, 768], P('seq', 'batch')
- input_grad: float32 [512, 64, 768], P('seq', 'batch')
- norm1_gain_grad: float32 [768], replicated
- in_weight_grad: float32 [768, 2304], P('seq', 'batch')
- short_taps_grad: float32 [3, 2304], replicated
- static_kernel_grad: float32 [512, 768], P('seq', 'batch')
- out_weight_grad: float32 [768, 768], P('seq', 'batch')
- norm2_gain_grad: float32 [768], replicated
- glu_weight_grad: float32 [768, 6144], P('seq', 'batch')
- down_weight_grad: float32 [3072, 768], P('seq', 'batch')
The draws below stay inside these ranges and needn't reach their ends.
Inputs may be any that keep to these rules, and one draw needn't show every extreme that they name: `lengths`: each entry is 128 or 512; each aligned block of 8 slots holds at least one of length 512.
All inputs are finite; a program needn't handle non-finite values.
Results may differ from the reference program's by a relative error of at most 0.019.
Values may be sent and summed in bfloat16 or wider, within the bound.
No kernel may reach another device: no remote copies, remote signals or barrier semaphores. Data moves between devices by JAX's collectives and lax.ppermute only.
A program may use at most 256 MiB of HBM per device.

```python
import math
import jax
import jax.numpy as jnp
from jax import lax

D = 768
FF = 3072
NPOS = 512
SLOTS_DEV = 8
SLOTS = 64
N_BATCH = 8


def draw_lengths(key, part):
    key = jax.random.fold_in(key, 11)
    coin_key, pick_key = jax.random.split(key)
    coins = jax.random.randint(coin_key, (N_BATCH, SLOTS_DEV), 0, 2)
    picked = jax.random.randint(pick_key, (N_BATCH, 1), 0, SLOTS_DEV)
    slot_ids = jnp.arange(SLOTS_DEV, dtype=jnp.int32)[None, :]
    longer = (coins == 1) | (slot_ids == picked)
    return jnp.where(longer, NPOS, NPOS // 4).reshape(-1).astype(jnp.int32)


def strengthened(values, stream_key, source, target, parts, factor):
    def block_of(axis_at):
        return (jnp.arange(values.shape[axis_at]) // (values.shape[axis_at] // parts)).reshape((-1,) + (1,) * (values.ndim - 1 - axis_at))

    near = jax.random.permutation(stream_key, parts)[block_of(target)]
    other_side = (block_of(target) + parts // 2) % parts
    return jnp.where((block_of(source) == near) | (block_of(source) == other_side), factor * values, values)


def steps_of(own_key, extent, cuts, low, largest):
    loudness = 1.0
    for position, shards_of in cuts:
        steps = jax.random.uniform(jax.random.fold_in(jax.random.fold_in(own_key, 6), position), (shards_of,), jnp.float32, low / len(cuts), largest / len(cuts))
        loudness = loudness * jnp.repeat(jnp.exp(steps), extent[position] // shards_of).reshape((-1,) + (1,) * (len(extent) - 1 - position))
    return loudness


def noise(stream_key, shape, scale, bound, shards=(), kind=jnp.bfloat16):
    values = jax.random.normal(stream_key, shape, jnp.float32) * scale
    if len(shards) > 0:
        values = steps_of(stream_key, shape, shards, -0.22, 0.18) * values
    return jnp.clip(values, min=-bound, max=bound).astype(kind)


def bell_draw_with(stream_key, extent, scale, reach, shards, heavy, held_as=jnp.bfloat16):
    values = scale * jax.random.normal(stream_key, extent, jnp.float32)
    if shards:
        values = values * steps_of(stream_key, extent, shards, -0.22, 0.18)
    return jnp.clip(strengthened(values, jax.random.fold_in(stream_key, 3), *heavy), -reach, reach).astype(held_as)


def setup_inputs(seed: int = 0) -> dict:
    seeds = jax.random.split(jax.random.key(seed), 12)
    return {
        "inputs": noise(seeds[0], (NPOS, SLOTS, D), 1.0, 6.0, ((0, 4), (1, 8))),
        "lengths": draw_lengths(jax.random.fold_in(seeds[11], 71), 0),
        "norm1_gain": jnp.clip(1.0 + 0.18 * jax.random.normal(seeds[2], (D,), jnp.float32), 0.1, 1.9),
        "in_weight": noise(seeds[3], (D, 3 * D), D ** -0.5, 0.21875),
        "short_taps": noise(seeds[4], (3, 3 * D), 0.6, 3.0, (), jnp.float32),
        "static_kernel": noise(seeds[5], (NPOS, D), NPOS ** -0.5, 0.25, (), jnp.float32),
        "out_weight": noise(seeds[6], (D, D), D ** -0.5, 0.21875),
        "norm2_gain": jnp.clip(1.0 + 0.18 * jax.random.normal(seeds[7], (D,), jnp.float32), 0.1, 1.9),
        "glu_weight": noise(seeds[8], (D, 2 * FF), D ** -0.5, 0.21875),
        "down_weight": noise(seeds[9], (FF, D), FF ** -0.5, 0.109375),
        "cotangent": bell_draw_with(seeds[10], (NPOS, SLOTS, D), 1.0, 6.0, ((0, 4), (1, 8)), (1, 2, 8, 2.0)),
    }


@jax.custom_vjp
def low(v):
    return lax.optimization_barrier(v.astype(jnp.bfloat16)).astype(jnp.float32)

@jax.custom_vjp
def low_back(v):
    return v

def low_keep(v):
    return (low(v), None)

def low_pass(kept, grad):
    return (grad,)

def back_keep(v):
    return (v, None)

def back_low(kept, grad):
    return (low(grad),)
low.defvjp(low_keep, low_pass)
low_back.defvjp(back_keep, back_low)

def product(form, left, right):
    return jnp.einsum(form, left, right, precision=lax.Precision.HIGHEST)

def transform_table(count):
    steps = jnp.arange(count, dtype=jnp.int32)
    index = steps[:, None] * steps[None, :] % count
    angle = index.astype(jnp.float32) * (2.0 * math.pi / count)
    return jnp.concatenate([jnp.cos(angle), -jnp.sin(angle)], axis=0)

def normalize(values, gain_vec):
    centred = values - lax.optimization_barrier(jnp.mean(values, axis=-1, keepdims=True))
    inverse = lax.rsqrt(lax.optimization_barrier(jnp.mean(centred * centred, axis=-1, keepdims=True)) + 1e-05)
    return centred * inverse * gain_vec

def layer(values, live, gain_one, in_mat, taps, static, out_mat, gain_two, glu_mat, down_mat):
    count = values.shape[0]
    width = values.shape[2]
    hidden_width = down_mat.shape[0]
    table = transform_table(count)
    normed_one = normalize(values, gain_one)
    projected = low_back(low(product('psd,de->pse', low(normed_one), in_mat)))
    padded = jnp.pad(projected, ((1, 1), (0, 0), (0, 0)))
    mixed = taps[0] * padded[:-2] + taps[1] * padded[1:-1] + taps[2] * padded[2:]
    gate_in = mixed[..., :width]
    value_in = mixed[..., width:2 * width]
    cond_in = mixed[..., 2 * width:]
    live_cols = live[:, :, None]
    value_seq = low_back(low(live_cols * value_in))
    cond_seq = low_back(low(live_cols * jax.nn.gelu(cond_in)))
    value_spec = product('ft,tsd->fsd', table, value_seq)
    cond_spec = product('ft,tsd->fsd', table, cond_seq)
    static_spec = product('ft,td->fd', table, static)
    scale = count ** (-0.5)
    kern_re = static_spec[:count, None, :] + scale * cond_spec[:count]
    kern_im = static_spec[count:, None, :] + scale * cond_spec[count:]
    val_re = value_spec[:count]
    val_im = value_spec[count:]
    prod_spec = jnp.concatenate([val_re * kern_re - val_im * kern_im, val_re * kern_im + val_im * kern_re], axis=0)
    conv_out = low_back(low(product('ft,fsd->tsd', table, prod_spec) / count))
    gated = low(live_cols * gate_in * conv_out)
    residual = values + low_back(product('psd,de->pse', gated, out_mat))
    normed_two = normalize(residual, gain_two)
    gate_up = low_back(product('psd,df->psf', low(normed_two), glu_mat))
    hidden = low(jax.nn.gelu(gate_up[..., :hidden_width]) * gate_up[..., hidden_width:])
    return residual + low_back(product('psf,fd->psd', hidden, down_mat))

def reference(inputs, lengths, norm1_gain, in_weight, short_taps, static_kernel, out_weight, norm2_gain, glu_weight, down_weight, cotangent):
    weights = (norm1_gain, in_weight.astype(jnp.float32), short_taps, static_kernel, out_weight.astype(jnp.float32), norm2_gain, glu_weight.astype(jnp.float32), down_weight.astype(jnp.float32))
    groups = SLOTS // SLOTS_DEV
    grouped_in = inputs.reshape(NPOS, groups, SLOTS_DEV, D).transpose(1, 0, 2, 3)
    grouped_cot = cotangent.reshape(NPOS, groups, SLOTS_DEV, D).transpose(1, 0, 2, 3)
    grouped_len = lengths.reshape(groups, SLOTS_DEV)

    def group_step(totals, item):
        block_in, block_cot, block_len = item
        live = (jnp.arange(NPOS, dtype=jnp.int32)[:, None] < block_len[None, :]).astype(jnp.float32)

        def forward(values, *params):
            return layer(values, live, *params)
        result, pullback = jax.vjp(forward, block_in.astype(jnp.float32), *weights)
        grads = pullback(block_cot.astype(jnp.float32))
        totals = jax.tree.map(jnp.add, totals, tuple(grads[1:]))
        return (totals, (result.astype(jnp.bfloat16), grads[0]))
    zeros = jax.tree.map(jnp.zeros_like, weights)
    totals, (results, input_grads) = lax.scan(group_step, zeros, (grouped_in, grouped_cot, grouped_len))
    output = results.transpose(1, 0, 2, 3).reshape(NPOS, SLOTS, D)
    input_grad = input_grads.transpose(1, 0, 2, 3).reshape(NPOS, SLOTS, D)
    return (output, input_grad, totals[0], totals[1], totals[2], totals[3], totals[4], totals[5], totals[6], totals[7])
```

```python
import functools
import math

import jax
import jax.numpy as jnp
import numpy as np
from jax import lax
from jax.experimental import pallas as pl
from jax.experimental.pallas import tpu as pltpu
from jax.sharding import PartitionSpec as P

F32 = jnp.float32
LOW = jnp.bfloat16
CHUNKS = 3
LANES = 128
BLOCK = 256
ROOT = math.sqrt(2.0 / math.pi)
CUBE = 0.044715
MIB = 2**20


def half_table(count):
    steps = np.arange(count)
    angle = (np.arange(count // 2)[:, None] * steps[None, :] % count) * (2.0 * math.pi / count)
    low_rows = np.cos(angle)
    high_rows = -np.sin(angle)
    high_rows[0] = np.where(steps % 2 == 0, 1.0, -1.0)
    return np.concatenate([low_rows, high_rows], axis=0).astype(LOW)


def dot(a, b, ca=1, cb=0):
    return lax.dot_general(a, b, (((ca,), (cb,)), ((), ())), preferred_element_type=F32)


def gelu_parts(z):
    square = z * z
    tanh = jnp.tanh(z * (ROOT + (ROOT * CUBE) * square))
    plus = 0.5 + 0.5 * tanh
    act = z * plus
    return act, plus + act * (1.0 - tanh) * (ROOT + (3.0 * ROOT * CUBE) * square)


def gelu(z):
    return z * (0.5 + 0.5 * jnp.tanh(z * (ROOT + (ROOT * CUBE) * (z * z))))


def standardize(values):
    centred = values - jnp.mean(values, axis=-1, keepdims=True)
    inverse = lax.rsqrt(jnp.mean(centred * centred, axis=-1, keepdims=True) + 1e-05)
    return centred * inverse, inverse


def norm_back(grad_in, standard, inverse, gain_vec):
    scaled = grad_in * gain_vec
    inner = (
        scaled
        - jnp.mean(scaled, axis=-1, keepdims=True)
        - standard * jnp.mean(scaled * standard, axis=-1, keepdims=True)
    )
    return inverse * inner


def shifts(a):
    count = a.shape[0]
    row = lax.broadcasted_iota(jnp.int32, a.shape, 0)
    before = jnp.where(row == 0, 0.0, pltpu.roll(a, 1, 0))
    after = jnp.where(row == count - 1, 0.0, pltpu.roll(a, count - 1, 0))
    return before, after


def spectrum_product(a, b, sign):
    half = a.shape[0] // 2
    ar, ai, br, bi = a[:half], a[half:], b[:half], b[half:]
    first = lax.broadcasted_iota(jnp.int32, ar.shape, 0) == 0
    both = ai * bi
    re = ar * br - jnp.where(first, 0.0, sign * both)
    im = jnp.where(first, both, ai * br + sign * (ar * bi))
    return re, im


def weighted(re, im, scale):
    first = lax.broadcasted_iota(jnp.int32, re.shape, 0) == 0
    weight = jnp.where(first, scale, 2.0 * scale)
    return jnp.concatenate([(re * weight).astype(LOW), (im * weight).astype(LOW)], axis=0)


def live_mask(length, count):
    return (lax.broadcasted_iota(jnp.int32, (count, 1), 0) < length).astype(F32)


def pack_kernel(ids, glu_ref, down_ref, glu_out, down_out):
    for k in range(CHUNKS):
        glu_out[k] = glu_ref[:, k * LANES : (k + 1) * LANES]

    @pl.when(pl.program_id(0) < pl.num_programs(0) // 2)
    def _():
        for k in range(CHUNKS):
            down_out[k] = down_ref[k * LANES : (k + 1) * LANES]


def pack_weights(ids, glu_weight, down_weight, n_seq):
    width, share = glu_weight.shape[0], CHUNKS * LANES
    return pl.pallas_call(
        pack_kernel,
        grid_spec=pltpu.PrefetchScalarGridSpec(
            num_scalar_prefetch=1,
            grid=(2 * n_seq,),
            in_specs=[
                pl.BlockSpec((width, share), lambda i, ids: (0, 2 * i + ids[1])),
                pl.BlockSpec((share, width), lambda i, ids: (2 * jnp.minimum(i, n_seq - 1) + ids[1], 0)),
            ],
            out_specs=[
                pl.BlockSpec((CHUNKS, width, LANES), lambda i, ids: (0, 0, i)),
                pl.BlockSpec((CHUNKS, LANES, width), lambda i, ids: (0, jnp.minimum(i, n_seq - 1), 0)),
            ],
        ),
        out_shape=[
            jax.ShapeDtypeStruct((CHUNKS, width, 2 * n_seq * LANES), LOW),
            jax.ShapeDtypeStruct((CHUNKS, n_seq * LANES, width), LOW),
        ],
        compiler_params=pltpu.CompilerParams(vmem_limit_bytes=24 * MIB),
    )(ids, glu_weight, down_weight)


def mixer_kernel(
    ids, x0, x1, x2, x3, w_gate, w_value, w_cond, t_gate, t_value, t_cond, static, table, w_out, gain1, gain2,
    p_gate, p_value, p_cond, conv_ref, value_spec, kernel_spec, gated_ref, residual_ref, n2_ref,
    normed, total,
):
    j = pl.program_id(0)
    blocks = (x0, x1, x2, x3)
    slots, span = x0.shape[0], x0.shape[1]
    count = span * len(blocks)
    scale = count**-0.5

    @pl.when(j == 0)
    def _():
        for r, block in enumerate(blocks):
            at = pl.multiple_of((ids[0] ^ r) * span, span)
            for s in range(slots):
                wide = block[s].astype(F32)
                standard, _ = standardize(wide)
                normed[s, pl.ds(at, span), :] = (standard * gain1[...]).astype(LOW)
                total[s, pl.ds(at, span), :] = wide

    static_spec = dot(table[...], static[...].astype(LOW))

    def mix(low, taps):
        wide = low.astype(F32)
        before, after = shifts(wide)
        return taps[0:1] * before + taps[1:2] * wide + taps[2:3] * after

    for s in range(slots):
        live = live_mask(ids[2 + s], count)
        rows = normed[s]
        pg = dot(rows, w_gate[...]).astype(LOW)
        pv = dot(rows, w_value[...]).astype(LOW)
        pc = dot(rows, w_cond[...]).astype(LOW)
        p_gate[s], p_value[s], p_cond[s] = pg, pv, pc
        value = (live * mix(pv, t_value[...])).astype(LOW)
        cond = (live * gelu(mix(pc, t_cond[...]))).astype(LOW)
        vs = dot(table[...], value)
        ks = static_spec + scale * dot(table[...], cond)
        value_spec[s], kernel_spec[s] = vs.astype(LOW), ks.astype(LOW)
        re, im = spectrum_product(vs, ks, 1.0)
        conv = dot(table[...], weighted(re, im, 1.0 / count), 0, 0).astype(LOW)
        conv_ref[s] = conv
        gated = (live * mix(pg, t_gate[...]) * conv.astype(F32)).astype(LOW)
        gated_ref[s] = gated
        total[s] += dot(gated, w_out[...])

    @pl.when(j == pl.num_programs(0) - 1)
    def _():
        for r in range(len(blocks)):
            at = pl.multiple_of((ids[0] ^ r) * span, span)
            for s in range(slots):
                rows = total[s, pl.ds(at, span), :]
                residual_ref[r, s] = rows
                standard, _ = standardize(rows)
                n2_ref[r, s] = (standard * gain2[...]).astype(LOW)


def mixer_forward(ids, x_blocks, in_weight, taps, static_kernel, table, out_weight, gain1, gain2):
    slots, span, width = x_blocks[0].shape
    count = span * len(x_blocks)
    steps = width // BLOCK
    whole = lambda shape: pl.BlockSpec(shape, lambda j, ids: (0,) * len(shape))
    part = lambda rows, m: pl.BlockSpec((rows, BLOCK), lambda j, ids, m=m: (0, m * steps + j))
    seqs = pl.BlockSpec((slots, count, BLOCK), lambda j, ids: (0, 0, j))
    rel = (len(x_blocks), slots, span, width)
    return pl.pallas_call(
        mixer_kernel,
        grid_spec=pltpu.PrefetchScalarGridSpec(
            num_scalar_prefetch=1,
            grid=(steps,),
            in_specs=[whole((slots, span, width))] * len(x_blocks)
            + [part(width, m) for m in range(3)]
            + [part(3, m) for m in range(3)]
            + [
                part(count, 0),
                whole((count, count)),
                pl.BlockSpec((BLOCK, width), lambda j, ids: (j, 0)),
                whole((1, width)),
                whole((1, width)),
            ],
            out_specs=[seqs] * 7 + [whole(rel)] * 2,
            scratch_shapes=[pltpu.VMEM((slots, count, width), LOW), pltpu.VMEM((slots, count, width), F32)],
        ),
        out_shape=[jax.ShapeDtypeStruct((slots, count, width), LOW)] * 7
        + [jax.ShapeDtypeStruct(rel, F32), jax.ShapeDtypeStruct(rel, LOW)],
        compiler_params=pltpu.CompilerParams(vmem_limit_bytes=56 * MIB),
    )(
        ids, *x_blocks, in_weight, in_weight, in_weight, taps, taps, taps, static_kernel, table, out_weight,
        gain1, gain2,
    )


def glu_kernel(
    ids, n2_own, n2_other, ct_own, ct_other, w_gate, w_up, w_down,
    hidden_ref, gate_ref, up_ref, glu_keep, glu_send, down_keep, down_send,
):
    g_grad = u_grad = d_grad = None
    for h, (n2, ct) in enumerate(((n2_own, ct_own), (n2_other, ct_other))):
        gate = dot(n2[...], w_gate[0])
        up = dot(n2[...], w_up[0])
        hidden_grad = dot(ct[...], w_down[0], 1, 1)
        act, slope = gelu_parts(gate)
        hidden = (act * up).astype(LOW)
        gate_grad = (hidden_grad * up * slope).astype(LOW)
        up_grad = (hidden_grad * act).astype(LOW)
        hidden_ref[h], gate_ref[h], up_ref[h] = hidden, gate_grad, up_grad
        parts = dot(n2[...], gate_grad, 0, 0), dot(n2[...], up_grad, 0, 0), dot(ct[...], hidden, 0, 0)
        if h == 0:
            g_grad, u_grad, d_grad = parts
        else:
            g_grad, u_grad, d_grad = g_grad + parts[0], u_grad + parts[1], d_grad + parts[2]
    grad = jnp.concatenate([g_grad.astype(LOW), u_grad.astype(LOW)], axis=1)
    low = d_grad.astype(LOW)
    blocks = 4
    size = grad.shape[0] // blocks
    for q in range(blocks):
        for value, keep, send, at in ((grad, glu_keep, glu_send, ids[8 + q]), (low, down_keep, down_send, ids[12 + q])):
            rows = value[q * size : (q + 1) * size]

            @pl.when(at < 2)
            def _(rows=rows, keep=keep, at=at):
                keep[at] = rows

            @pl.when(at >= 2)
            def _(rows=rows, send=send, at=at):
                send[at - 2] = rows


def glu_chunk(ids, n2_own, n2_other, ct_own, ct_other, w_glu, w_down, k, n_seq):
    tokens, width = n2_own.shape
    units = n_seq * LANES
    steps = units // BLOCK
    whole = pl.BlockSpec((tokens, width), lambda i, ids: (0, 0))
    cols = pl.BlockSpec((2, tokens, BLOCK), lambda i, ids: (0, 0, i))
    size = width // 4
    return pl.pallas_call(
        glu_kernel,
        grid_spec=pltpu.PrefetchScalarGridSpec(
            num_scalar_prefetch=1,
            grid=(steps,),
            in_specs=[whole] * 4
            + [
                pl.BlockSpec((1, width, BLOCK), lambda i, ids: (k, 0, i)),
                pl.BlockSpec((1, width, BLOCK), lambda i, ids: (k, 0, steps + i)),
                pl.BlockSpec((1, BLOCK, width), lambda i, ids: (k, i, 0)),
            ],
            out_specs=[cols] * 3
            + [pl.BlockSpec((2, size, 2 * BLOCK), lambda i, ids: (0, 0, i))] * 2
            + [pl.BlockSpec((2, size, BLOCK), lambda i, ids: (0, 0, i))] * 2,
        ),
        out_shape=[jax.ShapeDtypeStruct((2, tokens, units), LOW)] * 3
        + [jax.ShapeDtypeStruct((2, size, 2 * units), LOW)] * 2
        + [jax.ShapeDtypeStruct((2, size, units), LOW)] * 2,
        compiler_params=pltpu.CompilerParams(vmem_limit_bytes=56 * MIB),
    )(ids, n2_own, n2_other, ct_own, ct_other, w_glu, w_glu, w_down)


def n2_grad_kernel(*refs):
    gates, ups, w_glu, own, other = refs[:CHUNKS], refs[CHUNKS : 2 * CHUNKS], refs[-3], refs[-2], refs[-1]
    units = gates[0].shape[2]
    result = None
    for k in range(CHUNKS):
        part = dot(gates[k][0], w_glu[k, :, :units], 1, 1) + dot(ups[k][0], w_glu[k, :, units:], 1, 1)
        result = part if result is None else result + part

    @pl.when(pl.program_id(0) < pl.num_programs(0) // 2)
    def _():
        other[...] = result.astype(LOW)

    @pl.when(pl.program_id(0) >= pl.num_programs(0) // 2)
    def _():
        own[...] = result


def out_kernel(*refs):
    hiddens, w_down, own, other = refs[:CHUNKS], refs[-3], refs[-2], refs[-1]
    result = None
    for k in range(CHUNKS):
        part = dot(hiddens[k][0], w_down[k])
        result = part if result is None else result + part

    @pl.when(pl.program_id(0) < pl.num_programs(0) // 2)
    def _():
        other[...] = result.astype(LOW)

    @pl.when(pl.program_id(0) >= pl.num_programs(0) // 2)
    def _():
        own[...] = result


def token_call(body, arrays, weights, width, rows=256):
    tokens = arrays[0].shape[1]
    per = tokens // rows
    block = lambda a: pl.BlockSpec((1, rows, a.shape[2]), lambda i: (1 - i // per, i % per, 0))
    return pl.pallas_call(
        body,
        grid=(2 * per,),
        in_specs=[block(a) for a in arrays] + [pl.BlockSpec(weights.shape, lambda i: (0, 0, 0))],
        out_specs=[
            pl.BlockSpec((rows, width), lambda i: (jnp.maximum(i - per, 0), 0)),
            pl.BlockSpec((rows, width), lambda i: (jnp.minimum(i, per - 1), 0)),
        ],
        out_shape=[jax.ShapeDtypeStruct((tokens, width), F32), jax.ShapeDtypeStruct((tokens, width), LOW)],
        compiler_params=pltpu.CompilerParams(vmem_limit_bytes=56 * MIB),
    )(*arrays, weights)


def mixer_back_kernel(
    ids, x0, x1, x2, x3, n2g_own, n2g_other, cot, residual, w_gate, w_value, w_cond, t_gate, t_value, t_cond,
    table, w_out, gain1, gain2, p_gate, p_value, p_cond, conv_ref, value_spec, kernel_spec, gated_ref,
    out_grad, in_gate, in_value, in_cond, static_grad, taps_gate, taps_value, taps_cond, gains_grad, input_grad,
    normed, residual_grad, branch, total,
):
    j = pl.program_id(0)
    blocks = (x0, x1, x2, x3)
    slots, span = x0.shape[0], x0.shape[1]
    count = span * len(blocks)
    scale = count**-0.5

    @pl.when(j == 0)
    def _():
        gain_grad = jnp.zeros((1, x0.shape[2]), F32)
        for r, block in enumerate(blocks):
            at = pl.multiple_of((ids[0] ^ r) * span, span)
            for s in range(slots):
                standard, _ = standardize(block[s].astype(F32))
                normed[s, pl.ds(at, span), :] = (standard * gain1[...]).astype(LOW)
                grad = n2g_own[r, s] + n2g_other[r, s].astype(F32)
                unit, inverse = standardize(residual[r, s])
                gain_grad += jnp.sum(grad * unit, axis=0, keepdims=True)
                value = cot[r, s].astype(F32) + norm_back(grad, unit, inverse, gain2[...])
                residual_grad[s, pl.ds(at, span), :] = value
                branch[s, pl.ds(at, span), :] = value.astype(LOW)
        gains_grad[1:2] = gain_grad
        total[...] = jnp.zeros_like(total)

    def slope_mix(low, taps):
        wide = low.astype(F32)
        before, after = shifts(wide)
        return before, wide, after, taps[0:1] * before + taps[1:2] * wide + taps[2:3] * after

    def finish(grad, sides, taps):
        sums = [jnp.sum(grad * side, axis=0, keepdims=True) for side in sides]
        before, after = shifts(grad)
        return sums, (taps[0:1] * after + taps[1:2] * grad + taps[2:3] * before).astype(LOW)

    tap_sums, static_total, projected = [], None, []
    for s in range(slots):
        live = live_mask(ids[2 + s], count)
        gated_grad = live * dot(branch[s], w_out[...], 1, 1)
        *gate_sides, gate_in = slope_mix(p_gate[s], t_gate[...])
        gate_grad = gated_grad * conv_ref[s].astype(F32)
        conv_grad = (gated_grad * gate_in).astype(LOW)
        gs = dot(table[...], conv_grad)
        re, im = spectrum_product(gs, kernel_spec[s].astype(F32), -1.0)
        value_grad = live * dot(table[...], weighted(re, im, 1.0 / count), 0, 0)
        re, im = spectrum_product(gs, value_spec[s].astype(F32), -1.0)
        back = dot(table[...], weighted(re, im, 1.0 / count), 0, 0)
        static_total = back if s == 0 else static_total + back
        *cond_sides, cond_in = slope_mix(p_cond[s], t_cond[...])
        cond_grad = (live * scale) * back * gelu_parts(cond_in)[1]
        value_low = p_value[s].astype(F32)
        value_before, value_after = shifts(value_low)
        sums_g, pg = finish(gate_grad, gate_sides, t_gate[...])
        sums_v, pv = finish(value_grad, (value_before, value_low, value_after), t_value[...])
        sums_c, pc = finish(cond_grad, cond_sides, t_cond[...])
        tap_sums.append((sums_g, sums_v, sums_c))
        projected.append((pg, pv, pc))
        total[s] += dot(pg, w_gate[...], 1, 1) + dot(pv, w_value[...], 1, 1) + dot(pc, w_cond[...], 1, 1)
    static_grad[...] = static_total.astype(LOW)
    for m, ref in enumerate((taps_gate, taps_value, taps_cond)):
        for i in range(3):
            ref[i : i + 1] = sum(sums[m][i] for sums in tap_sums)
    for m, ref in enumerate((in_gate, in_value, in_cond)):
        ref[...] = sum(dot(normed[s], projected[s][m], 0, 0) for s in range(slots)).astype(LOW)
    out_grad[...] = sum(dot(gated_ref[s], branch[s], 0, 0) for s in range(slots)).astype(LOW)

    @pl.when(j == pl.num_programs(0) - 1)
    def _():
        gain_grad = jnp.zeros((1, x0.shape[2]), F32)
        for r, block in enumerate(blocks):
            at = pl.multiple_of((ids[0] ^ r) * span, span)
            for s in range(slots):
                standard, inverse = standardize(block[s].astype(F32))
                grad = total[s, pl.ds(at, span), :]
                gain_grad += jnp.sum(grad * standard, axis=0, keepdims=True)
                value = residual_grad[s, pl.ds(at, span), :] + norm_back(grad, standard, inverse, gain1[...])
                input_grad[r, s] = value.astype(LOW)
        gains_grad[0:1] = gain_grad


def mixer_backward(
    ids, x_blocks, n2g_own, n2g_other, cot, residual, in_weight, taps, table, out_weight, gain1, gain2, saved
):
    slots, span, width = x_blocks[0].shape
    count = span * len(x_blocks)
    steps = width // BLOCK
    whole = lambda shape: pl.BlockSpec(shape, lambda j, ids: (0,) * len(shape), pipeline_mode=pl.Buffered(1))
    part = lambda rows, m: pl.BlockSpec((rows, BLOCK), lambda j, ids, m=m: (0, m * steps + j))
    seqs = pl.BlockSpec((slots, count, BLOCK), lambda j, ids: (0, 0, j))
    rows = pl.BlockSpec((BLOCK, width), lambda j, ids: (j, 0))
    last = lambda shape: pl.BlockSpec(shape, lambda j, ids: (0,) * len(shape))
    rel = (len(x_blocks), slots, span, width)
    return pl.pallas_call(
        mixer_back_kernel,
        grid_spec=pltpu.PrefetchScalarGridSpec(
            num_scalar_prefetch=1,
            grid=(steps,),
            in_specs=[whole((slots, span, width))] * len(x_blocks)
            + [whole(rel)] * 4
            + [part(width, m) for m in range(3)]
            + [part(3, m) for m in range(3)]
            + [whole((count, count)), rows, whole((1, width)), whole((1, width))]
            + [seqs] * 7,
            out_specs=[rows]
            + [part(width, 0)] * 3
            + [part(count, 0)]
            + [part(3, 0)] * 3
            + [last((2, width)), last(rel)],
            scratch_shapes=[
                pltpu.VMEM((slots, count, width), LOW),
                pltpu.VMEM((slots, count, width), F32),
                pltpu.VMEM((slots, count, width), LOW),
                pltpu.VMEM((slots, count, width), F32),
            ],
        ),
        out_shape=[jax.ShapeDtypeStruct((width, width), LOW)] * 4
        + [jax.ShapeDtypeStruct((count, width), LOW)]
        + [jax.ShapeDtypeStruct((3, width), F32)] * 3
        + [jax.ShapeDtypeStruct((2, width), F32), jax.ShapeDtypeStruct(rel, LOW)],
        compiler_params=pltpu.CompilerParams(vmem_limit_bytes=60 * MIB),
    )(
        ids, *x_blocks, n2g_own, n2g_other, cot, residual, in_weight, in_weight, in_weight, taps, taps, taps,
        table, out_weight, gain1, gain2, *saved,
    )


def exchange(x, partner):
    n_seq, n_batch = lax.axis_size("seq"), lax.axis_size("batch")
    pairs = []
    for s in range(n_seq):
        for b in range(n_batch):
            to_s, to_b = partner(s, b)
            pairs.append((s * n_batch + b, to_s * n_batch + to_b))
    return lax.ppermute(x, ("seq", "batch"), pairs)


def other_core(x):
    return exchange(x, lambda s, b: (s, b ^ 1))


def first_side(s, b):
    return s ^ (1 if b % 2 == 0 else 2), b


def second_side(s, b):
    return s ^ (2 if b % 2 == 0 else 1), b


def add_low(a, b):
    return (a.astype(F32) + b.astype(F32)).astype(LOW)


def halve(x, dim, bit, partner):
    half = x.shape[dim] // 2
    sent = lax.dynamic_slice_in_dim(x, (1 - bit) * half, half, dim)
    kept = lax.dynamic_slice_in_dim(x, bit * half, half, dim)
    return add_low(kept, exchange(sent, partner))


def seq_halving(x, core, seq):
    rel = jnp.array([0, 1, 2, 3]) ^ seq
    order = jnp.where(core == 0, rel[jnp.array([0, 2, 1, 3])], rel)
    x = jnp.take(x, order, axis=0, mode="clip")
    x = add_low(x[:2], exchange(x[2:], first_side))
    return add_low(x[0], exchange(x[1], second_side))


def chip_halving(x, dim, place):
    n_chip = lax.axis_size("batch") // 2
    shape = x.shape
    x = x.reshape(shape[:dim] + (n_chip, shape[dim] // n_chip) + shape[dim + 1 :])
    step = 1
    while step < n_chip:
        bit = (place // step) % 2
        cut = x.shape
        x = x.reshape(cut[:dim] + (cut[dim] // 2, 2) + cut[dim + 1 :])
        x = halve(x, dim + 1, bit, lambda s, b, step=step: (s, b ^ (2 * step)))
        x = x.reshape(cut[:dim] + (cut[dim] // 2,) + cut[dim + 1 :])
        step *= 2
    return x.reshape(x.shape[:dim] + x.shape[dim + 1 :])


def to_blocks(x, seq):
    n_seq = lax.axis_size("seq")
    own = x.shape[1] // n_seq
    turned = x.transpose(1, 0, 2)
    blocks = []
    for r in range(n_seq):
        block = lax.dynamic_slice_in_dim(turned, (seq ^ r) * own, own, 0)
        blocks.append(block if r == 0 else exchange(block, lambda s, b, r=r: (s ^ r, b)))
    return blocks


def from_blocks(blocks, seq):
    n_seq = lax.axis_size("seq")
    moved = [blocks[0]] + [exchange(blocks[r], lambda s, b, r=r: (s ^ r, b)) for r in range(1, n_seq)]
    order = jnp.arange(n_seq) ^ seq
    whole = jnp.take(jnp.stack(moved, axis=0), order, axis=0, mode="clip")
    return whole.reshape((-1,) + whole.shape[2:]).transpose(1, 0, 2)


def on_device(
    inputs,
    lengths,
    norm1_gain,
    in_weight,
    short_taps,
    static_kernel,
    out_weight,
    norm2_gain,
    glu_weight,
    down_weight,
    cotangent,
):
    width = inputs.shape[2]
    n_seq, n_batch = lax.axis_size("seq"), lax.axis_size("batch")
    seq, batch = lax.axis_index("seq"), lax.axis_index("batch")
    core, place = batch % 2, batch // 2
    n_chip = n_batch // 2
    total_pos = inputs.shape[0] * n_seq
    own_slots = inputs.shape[1] // n_seq
    tokens = own_slots * total_pos
    table = jnp.asarray(half_table(total_pos))
    gain1, gain2 = norm1_gain[None], norm2_gain[None]

    block = jnp.arange(4, dtype=jnp.int32)
    rel = block ^ seq
    swapped = (rel % 2) * 2 + rel // 2
    glu_at = jnp.where(core == 0, swapped, rel)
    chip_rel = block ^ place
    down_at = (chip_rel % 2) * 2 + chip_rel // 2 if n_chip == 4 else block
    own_lengths = lax.dynamic_slice_in_dim(lengths, seq * own_slots, own_slots)
    head = jnp.zeros(8, jnp.int32).at[0].set(seq).at[1].set(core).at[2 : 2 + own_slots].set(own_lengths)
    ids = jnp.concatenate([head, glu_at, down_at])

    x_blocks = to_blocks(inputs, seq)
    w_glu, w_down = pack_weights(ids, glu_weight, down_weight, n_seq)
    ct_blocks = to_blocks(cotangent, seq)
    *saved, residual, n2 = mixer_forward(
        ids, x_blocks, in_weight, short_taps, static_kernel, table, out_weight, gain1, gain2
    )
    cot = jnp.stack(ct_blocks, axis=0)
    flat = lambda a: a.reshape(tokens, width)
    n2_own, ct_own = flat(n2), flat(cot)
    ct_other = other_core(ct_own)
    n2_other = other_core(n2_own)

    chunks = [
        glu_chunk(ids, n2_own, n2_other, ct_own, ct_other, w_glu, w_down, k, n_seq) for k in range(CHUNKS)
    ]
    gates, ups, hiddens = [c[1] for c in chunks], [c[2] for c in chunks], [c[0] for c in chunks]
    n2g_own, n2g_sent = token_call(n2_grad_kernel, gates + ups, w_glu, width)
    n2g_other = other_core(n2g_sent)
    out_own, out_sent = token_call(out_kernel, hiddens, w_down, width)
    out = residual + (out_own + other_core(out_sent).astype(F32)).reshape(residual.shape)
    out = out.astype(LOW)
    output = from_blocks([out[r] for r in range(n_seq)], seq)

    out_grad, in_gate, in_value, in_cond, static_grad, taps_g, taps_v, taps_c, gains_grad, x_grad = mixer_backward(
        ids, x_blocks, n2g_own.reshape(residual.shape), n2g_other.reshape(residual.shape), cot, residual,
        in_weight, short_taps, table, out_weight, gain1, gain2, saved,
    )
    input_grad = from_blocks([x_grad[r] for r in range(n_seq)], seq).astype(F32)

    def join(own, other, dim):
        low = jnp.where(core == 0, own, other)
        high = jnp.where(core == 0, other, own)
        return jnp.concatenate([low, high], axis=dim)

    def summed(grad):
        rows, cols = grad.shape
        grad = grad.reshape(n_seq, 2, rows // n_seq // 2, cols)
        grad = halve(grad, 1, core, lambda s, b: (s, b ^ 1))
        grad = seq_halving(grad, core, seq)[0]
        grad = chip_halving(grad, 1, place).reshape(-1, 2, cols // n_batch)
        other = other_core(lax.dynamic_index_in_dim(grad, 1 - core, 1, keepdims=False))
        own = lax.dynamic_index_in_dim(grad, core, 1, keepdims=False)
        return join(own, other, 0).astype(F32)

    in_grad = jnp.concatenate([in_gate, in_value, in_cond], axis=1)
    total_in, total_out, total_static = summed(in_grad), summed(out_grad), summed(static_grad)

    glus, downs = [], []
    for _, _, _, glu_keep, glu_send, down_keep, down_send in chunks:
        part = add_low(glu_keep, exchange(glu_send, first_side))
        glus.append(add_low(part[0], exchange(part[1], second_side)))
        if n_chip == 4:
            part = add_low(down_keep, exchange(down_send, lambda s, b: (s, b ^ 2)))
            downs.append(add_low(part[0], exchange(part[1], lambda s, b: (s, b ^ 4))))
        else:
            downs.append(jnp.concatenate([down_keep, down_send], axis=0))
    side = n_seq // 2
    glu = jnp.stack([g.reshape(-1, side, 2, side, LANES) for g in glus], axis=4)
    glu = glu.transpose(0, 2, 1, 3, 4, 5)
    share = CHUNKS * LANES
    if n_chip == 4:
        glu = chip_halving(glu.reshape(-1, 2 * side, side, share), 1, place).reshape(-1, side, share)
        other = other_core(lax.dynamic_index_in_dim(glu, 1 - core, 1, keepdims=False))
        own = lax.dynamic_index_in_dim(glu, core, 1, keepdims=False)
        total_glu = join(own, other, 1).astype(F32)
        down = jnp.stack([d.reshape(-1, n_seq, LANES) for d in downs], axis=2)
        down = seq_halving(down.transpose(1, 0, 2, 3).reshape(n_seq, -1, share), core, seq)
        down = down.reshape(2, -1, share)
        other = other_core(lax.dynamic_index_in_dim(down, 1 - core, 0, keepdims=False))
        own = lax.dynamic_index_in_dim(down, core, 0, keepdims=False)
        total_down = join(own, other, 1).T.astype(F32)
    else:
        mine = (jnp.arange(2) == core)[:, None]
        glu = glu.reshape(-1, 2 * n_seq, 1, share)
        glu = jnp.where(mine, glu, 0).astype(F32).reshape(-1, 4 * n_seq * share)
        total_glu = lax.psum_scatter(glu, "batch", scatter_dimension=1, tiled=True)
        down = jnp.stack([d.reshape(width, n_seq, LANES) for d in downs], axis=2).reshape(width, n_seq, 1, share)
        down = jnp.where(mine, down, 0).astype(F32).reshape(width, 2 * n_seq * share)
        down = lax.psum_scatter(down, "batch", scatter_dimension=0, tiled=True)
        down = lax.psum_scatter(down, "seq", scatter_dimension=1, tiled=True)
        total_down = down.T

    small = jnp.concatenate([gains_grad, taps_g, taps_v, taps_c], axis=0)
    step = 1
    while step < n_seq:
        small = small + exchange(small, lambda s, b, step=step: (s ^ step, b))
        step *= 2
    step = 1
    while step < n_batch:
        small = small + exchange(small, lambda s, b, step=step: (s, b ^ step))
        step *= 2
    total_taps = jnp.concatenate([small[2:5], small[5:8], small[8:11]], axis=1)
    return (
        output,
        input_grad,
        small[0],
        total_in,
        total_taps,
        total_static,
        total_out,
        small[1],
        total_glu,
        total_down,
    )


def solution(mesh):
    return jax.shard_map(
        on_device,
        mesh=mesh,
        in_specs=(
            P("seq", "batch", None),
            P("batch"),
            P(),
            P(),
            P(),
            P(),
            P(),
            P(),
            P(),
            P(),
            P("seq", "batch", None),
        ),
        out_specs=(
            P("seq", "batch", None),
            P("seq", "batch", None),
            P(),
            P("seq", "batch"),
            P(),
            P("seq", "batch"),
            P("seq", "batch"),
            P(),
            P("seq", "batch"),
            P("seq", "batch"),
        ),
        check_vma=False,
    )
```

```python
import functools
import math

import jax
import jax.numpy as jnp
import numpy as np
from jax import lax
from jax.experimental import pallas as pl
from jax.experimental.pallas import tpu as pltpu
from jax.sharding import PartitionSpec as P

F32 = jnp.float32
LOW = jnp.bfloat16
CHUNKS = 3
LANES = 128
ROOT = math.sqrt(2.0 / math.pi)
CUBE = 0.044715
MIB = 2**20
COST = 1000
TILES = 4
ANY = pl.BlockSpec(memory_space=pl.ANY)

SEQ, CORE, PLACE, LENGTH, ROW_AT, CHIP_AT, COL_AT = 0, 1, 2, 3, 5, 9, 13


def half_table(count):
    steps = np.arange(count)
    angle = (np.arange(count // 2)[:, None] * steps[None, :] % count) * (2.0 * math.pi / count)
    low_rows = np.cos(angle)
    high_rows = -np.sin(angle)
    high_rows[0] = np.where(steps % 2 == 0, 1.0, -1.0)
    return np.concatenate([low_rows, high_rows], axis=0).astype(LOW)


def dot(a, b, ca=1, cb=0):
    return lax.dot_general(a, b, (((ca,), (cb,)), ((), ())), preferred_element_type=F32)


def gelu_parts(z):
    square = z * z
    tanh = jnp.tanh(z * (ROOT + (ROOT * CUBE) * square))
    plus = 0.5 + 0.5 * tanh
    act = z * plus
    return act, plus + act * (1.0 - tanh) * (ROOT + (3.0 * ROOT * CUBE) * square)


def gelu(z):
    return z * (0.5 + 0.5 * jnp.tanh(z * (ROOT + (ROOT * CUBE) * (z * z))))


def standardize(values):
    centred = values - jnp.mean(values, axis=-1, keepdims=True)
    inverse = lax.rsqrt(jnp.mean(centred * centred, axis=-1, keepdims=True) + 1e-05)
    return centred * inverse, inverse


def norm_back(grad_in, standard, inverse, gain_vec):
    scaled = grad_in * gain_vec
    inner = (
        scaled
        - jnp.mean(scaled, axis=-1, keepdims=True)
        - standard * jnp.mean(scaled * standard, axis=-1, keepdims=True)
    )
    return inverse * inner


def shifts(a):
    count = a.shape[0]
    row = lax.broadcasted_iota(jnp.int32, a.shape, 0)
    before = jnp.where(row == 0, 0.0, pltpu.roll(a, 1, 0))
    after = jnp.where(row == count - 1, 0.0, pltpu.roll(a, count - 1, 0))
    return before, after


def mix(low, taps):
    wide = low.astype(F32)
    before, after = shifts(wide)
    return taps[0:1] * before + taps[1:2] * wide + taps[2:3] * after


def mix_back(grad, low, taps):
    wide = low.astype(F32)
    before, after = shifts(grad)
    sums = [jnp.sum(side * wide, axis=0, keepdims=True) for side in (after, grad, before)]
    return sums, (taps[0:1] * after + taps[1:2] * grad + taps[2:3] * before).astype(LOW)


def spectrum_product(a, b, sign):
    half = a.shape[0] // 2
    ar, ai, br, bi = a[:half], a[half:], b[:half], b[half:]
    first = lax.broadcasted_iota(jnp.int32, ar.shape, 0) == 0
    both = ai * bi
    re = ar * br - jnp.where(first, 0.0, sign * both)
    im = jnp.where(first, both, ai * br + sign * (ar * bi))
    return re, im


def weighted(re, im, scale):
    first = lax.broadcasted_iota(jnp.int32, (re.shape[0], 1), 0) == 0
    weight = jnp.where(first, scale, 2.0 * scale)
    return jnp.concatenate([(re * weight).astype(LOW), (im * weight).astype(LOW)], axis=0)


def live_mask(length, count):
    return (lax.broadcasted_iota(jnp.int32, (count, 1), 0) < length).astype(F32)


def whole(shape):
    return pl.BlockSpec(shape, lambda *at: (0,) * len(shape))


def kept(shape):
    return pl.BlockSpec(shape, lambda *at: (0,) * len(shape), pipeline_mode=pl.Buffered(1))


def sds(shape, dtype=LOW):
    return jax.ShapeDtypeStruct(shape, dtype)


def call(body, grid, ids, in_specs, out_specs, out_shape, args, scratch=(), aliases=None, mib=12):
    return pl.pallas_call(
        body,
        grid_spec=pltpu.PrefetchScalarGridSpec(
            num_scalar_prefetch=1, grid=grid, in_specs=in_specs, out_specs=out_specs, scratch_shapes=list(scratch)
        ),
        out_shape=out_shape,
        compiler_params=pltpu.CompilerParams(vmem_limit_bytes=mib * MIB),
        input_output_aliases=aliases or {},
        cost_estimate=pl.CostEstimate(flops=COST, bytes_accessed=COST, transcendentals=0),
    )(ids, *args)


def turn_kernel(by_slot, ids, x_ref, *refs):
    outs, held = refs[:-1], refs[-1]
    held[...] = jnp.swapaxes(x_ref[...].astype(F32), 0, 1).astype(LOW)
    n_seq = 4
    own = held.shape[0] // n_seq
    for r in range(n_seq):
        at = (ids[SEQ] ^ r) * own
        for s in range(own):
            if by_slot:
                outs[s * n_seq + r][...] = held[at + s]
            else:
                outs[r][s] = held[at + s]


def turn(ids, x, by_slot):
    span, slots, width = x.shape
    own = slots // 4
    shape = (span, width) if by_slot else (own, span, width)
    n_out = slots if by_slot else 4
    return call(
        functools.partial(turn_kernel, by_slot), (1,), ids, [whole(x.shape)], [whole(shape)] * n_out,
        [sds(shape)] * n_out, (x,), [pltpu.VMEM((slots, span, width), LOW)], mib=20,
    )


def unturn_kernel(by_side, ids, *refs):
    blocks, out, held = refs[:-2], refs[-2], refs[-1]
    own = blocks[0].shape[1]
    rels = (0, 1 + ids[CORE], 2 - ids[CORE], 3) if by_side else range(4)
    for rel, block in zip(rels, blocks):
        for s in range(own):
            held[(ids[SEQ] ^ rel) * own + s] = block[0, s].astype(F32)
    out[...] = jnp.swapaxes(held[...], 0, 1).astype(out.dtype)


def unturn(ids, blocks, dtype, by_side):
    _, own, span, width = blocks[0][0].shape
    slots = own * len(blocks)
    cut = width // 3
    return call(
        functools.partial(unturn_kernel, by_side),
        (3,),
        ids,
        [pl.BlockSpec((1, own, span, cut), lambda j, ids, at=at: (at, 0, 0, j)) for _, at in blocks],
        pl.BlockSpec((span, slots, cut), lambda j, ids: (0, 0, j)),
        sds((span, slots, width), dtype),
        [a for a, _ in blocks],
        [pltpu.VMEM((slots, span, cut), F32)],
        mib=16,
    )


def mixer_kernel(
    slot, ids, x0, x1, x2, x3, in_weight, taps, static, table, w_out, gain1, gain2, *refs
):
    p_ref, spec_ref, conv_ref, gated_ref, normed_ref, x_ref, residual_ref, n2_ref, total = refs[-9:]
    blocks = (x0, x1, x2, x3)
    span, width = x0.shape
    count = span * len(blocks)
    scale = count**-0.5
    for r, block in enumerate(blocks):
        at = pl.multiple_of((ids[SEQ] ^ r) * span, span)
        wide = block[...].astype(F32)
        standard, _ = standardize(wide)
        normed_ref[0, pl.ds(at, span), :] = (standard * gain1[...]).astype(LOW)
        x_ref[0, pl.ds(at, span), :] = block[...]
        total[pl.ds(at, span), :] = wide
    live = live_mask(ids[LENGTH + slot], count)
    p_ref[0] = dot(normed_ref[0], in_weight[...]).astype(LOW)
    static_spec = dot(table[...], static[...].astype(LOW))
    value = (live * mix(p_ref[0, :, width : 2 * width], taps[:, width : 2 * width])).astype(LOW)
    vs = dot(table[...], value)
    cond = (live * gelu(mix(p_ref[0, :, 2 * width :], taps[:, 2 * width :]))).astype(LOW)
    ks = static_spec + scale * dot(table[...], cond)
    spec_ref[0, :, :width], spec_ref[0, :, width:] = vs.astype(LOW), ks.astype(LOW)
    re, im = spectrum_product(vs, ks, 1.0)
    conv = dot(table[...], weighted(re, im, 1.0 / count), 0, 0).astype(LOW)
    conv_ref[0] = conv
    gated = (live * mix(p_ref[0, :, :width], taps[:, :width]) * conv.astype(F32)).astype(LOW)
    gated_ref[0] = gated
    total[...] += dot(gated, w_out[...])
    for r in range(len(blocks)):
        at = pl.multiple_of((ids[SEQ] ^ r) * span, span)
        rows = total[pl.ds(at, span), :]
        residual_ref[0, r] = rows
        standard, _ = standardize(rows)
        n2_ref[r] = (standard * gain2[...]).astype(LOW)


def mixer_forward(ids, slot, slots, x_blocks, weights, before):
    span, width = x_blocks[0].shape
    count = span * len(x_blocks)
    in_weight, taps, static, table, w_out, gain1, gain2 = weights
    seqs = lambda m: pl.BlockSpec((1, count, m * width), lambda i, ids: (slot, 0, 0))
    cols = (3, 2, 1, 1, 1, 1)
    rel = (len(x_blocks), span, width)
    args = (*x_blocks, in_weight, taps, static, table, w_out, gain1, gain2)
    in_specs = [kept(a.shape) for a in args]
    aliases = {}
    if before is not None:
        aliases = {1 + len(args) + i: i for i in range(len(before))}
        args, in_specs = args + tuple(before), in_specs + [ANY] * len(before)
    return call(
        functools.partial(mixer_kernel, slot),
        (1,),
        ids,
        in_specs,
        [seqs(m) for m in cols] + [pl.BlockSpec((1, *rel), lambda i, ids: (slot, 0, 0, 0)), whole(rel)],
        [sds((slots, count, m * width)) for m in cols] + [sds((slots, *rel), F32), sds(rel)],
        args,
        [pltpu.VMEM((count, width), F32)],
        aliases,
        mib=48,
    )


def into(parts, held, sems):
    copies, at = [], 0
    for i, part in enumerate(parts):
        rows = part.shape[0]
        copies.append(pltpu.make_async_copy(part, held.at[pl.ds(at, rows)], sems.at[i]))
        at += rows
    return copies


def glu_forward_kernel(n_parts, n_seq, ids, *refs):
    parts, rest = refs[:n_parts], refs[n_parts:]
    first = len(rest) > 11
    if first:
        glu_blocks, down_blocks, rest = rest[: 2 * n_seq], rest[2 * n_seq : 3 * n_seq], rest[3 * n_seq :]
        hidden_ref, act_ref, slope_ref, out, w_glu, w_down, n2, total, sems = rest
    else:
        w_glu, w_down, hidden_ref, act_ref, slope_ref, out, n2, total, sems = rest
    k = pl.program_id(0)

    @pl.when(k == 0)
    def _():
        copies = into(parts, n2, sems)
        for copy in copies:
            copy.start()
        total[...] = jnp.zeros_like(total)
        for copy in copies:
            copy.wait()

    if first:
        for i, ref in enumerate(glu_blocks):
            w_glu[0, :, i * LANES : (i + 1) * LANES] = ref[...]
        for i, ref in enumerate(down_blocks):
            w_down[0, i * LANES : (i + 1) * LANES] = ref[...]
    units = n_seq * LANES
    rows = n2.shape[0] // TILES
    for h in range(TILES):
        here = slice(h * rows, (h + 1) * rows)
        gate = dot(n2[here], w_glu[0, :, :units])
        up = dot(n2[here], w_glu[0, :, units:])
        act, slope = gelu_parts(gate)
        hidden = (act * up).astype(LOW)
        hidden_ref[0, here], act_ref[0, here], slope_ref[0, here] = hidden, act.astype(LOW), (slope * up).astype(LOW)
        total[here] += dot(hidden, w_down[0])

    @pl.when(k == pl.num_programs(0) - 1)
    def _():
        out[...] = total[...].astype(out.dtype)


def glu_forward(ids, n2_parts, weights, n_seq, out_dtype):
    tokens = sum(p.shape[0] for p in n2_parts)
    first = weights[0].ndim == 2
    width, units = n2_parts[0].shape[1], n_seq * LANES
    cols = pl.BlockSpec((1, tokens, units), lambda k, ids: (k, 0, 0))
    at = lambda m: lambda k, ids: (2 * m + ids[CORE]) * CHUNKS + k
    packed_specs = [
        pl.BlockSpec((1, width, 2 * units), lambda k, ids: (k, 0, 0)),
        pl.BlockSpec((1, units, width), lambda k, ids: (k, 0, 0)),
    ]
    if first:
        w_args = (*[weights[0]] * (2 * n_seq), *[weights[1]] * n_seq)
        w_specs = [pl.BlockSpec((width, LANES), lambda k, ids, f=at(m): (0, f(k, ids))) for m in range(2 * n_seq)]
        w_specs += [pl.BlockSpec((LANES, width), lambda k, ids, f=at(m): (f(k, ids), 0)) for m in range(n_seq)]
        out_specs, out_shape = packed_specs, [sds((CHUNKS, width, 2 * units)), sds((CHUNKS, units, width))]
    else:
        w_args, w_specs, out_specs, out_shape = weights, packed_specs, [], []
    return call(
        functools.partial(glu_forward_kernel, len(n2_parts), n_seq),
        (CHUNKS,),
        ids,
        [ANY] * len(n2_parts) + w_specs,
        [cols] * 3 + [whole((tokens, width))] + out_specs,
        [sds((CHUNKS, tokens, units))] * 3 + [sds((tokens, width), out_dtype)] + out_shape,
        (*n2_parts, *w_args),
        [pltpu.VMEM((tokens, width), LOW), pltpu.VMEM((tokens, width), F32), pltpu.SemaphoreType.DMA((len(n2_parts),))],
        mib=44,
    )


def glu_back_kernel(k, by_rows, n_parts, ids, *refs):
    n2_parts, ct_parts = refs[:n_parts], refs[n_parts : n_parts + 2]
    saved = refs[n_parts + 2 : n_parts + 8]
    (
        w_hbm, gu_hbm, glu_keep, glu_send, down_keep, down_send,
        n2, ct, act, slope, hidden, w, gu, g_total, d_total, g_low, d_low, sems, out_sems, n2_sems, ct_sems,
    ) = refs[n_parts + 8 :]
    rows = ct.shape[0] // 2
    units = w.shape[0]
    halves = [pl.ds(h * rows, rows) for h in range(2)]
    n2_copies, ct_copies = into(n2_parts, n2, n2_sems), into(ct_parts, ct, ct_sems)
    per = n_parts // 2
    w_copy = pltpu.make_async_copy(w_hbm.at[k], w, sems.at[6])
    streams = [
        [
            pltpu.make_async_copy(saved[3 * h + i].at[k], dst.at[halves[h]], sems.at[3 * h + i])
            for i, dst in enumerate((hidden, act, slope))
        ]
        for h in range(2)
    ]
    w_copy.start()
    for h in range(2):
        ct_copies[h].start()
        for copy in streams[h]:
            copy.start()
        for copy in n2_copies[h * per : (h + 1) * per]:
            copy.start()
    w_copy.wait()
    outs = [pltpu.make_async_copy(gu.at[halves[h]], gu_hbm.at[halves[h]], out_sems.at[h]) for h in range(2)]
    for h in range(2):
        here = halves[h]
        ct_copies[h].wait()
        hidden_grad = dot(ct[here], w[...], 1, 1)
        for copy in streams[h]:
            copy.wait()
        gu[here, :units] = (hidden_grad * slope[here].astype(F32)).astype(LOW)
        gu[here, units:] = (hidden_grad * act[here].astype(F32)).astype(LOW)
        outs[h].start()
        for copy in n2_copies[h * per : (h + 1) * per]:
            copy.wait()
        g_part = dot(n2[here], gu[here], 0, 0)
        d_part = dot(ct[here], hidden[here], 0, 0)
        if h == 0:
            g_total[...], d_total[...] = g_part, d_part
        else:
            g_sum, d_sum = g_total[...] + g_part, d_total[...] + d_part
    side = units // 2
    size = g_sum.shape[0] // 4
    for q in range(4):
        here = pl.ds(pl.multiple_of(ids[ROW_AT + q] * size, size), size)
        for high in range(2):
            for g in range(2):
                at = (high ^ (ids[PLACE] % 2)) * 2 + (g ^ (ids[PLACE] // 2 % 2))
                from_col = g * units + high * side
                part = g_sum[q * size : (q + 1) * size, from_col : from_col + side]
                g_low[here, pl.ds(pl.multiple_of(at * side, side), side)] = part.astype(LOW)
    for q in range(4):
        here = pl.ds(pl.multiple_of(ids[CHIP_AT + q] * size, size), size)
        for s in range(4):
            part = d_sum[q * size : (q + 1) * size, s * LANES : (s + 1) * LANES]
            d_low[here, pl.ds(pl.multiple_of(ids[COL_AT + s] * LANES, LANES), LANES)] = part.astype(LOW)
    half = d_low.shape[0] // 2
    d_cuts = (
        (d_low.at[pl.ds(0, half)], d_low.at[pl.ds(half, half)])
        if by_rows
        else (d_low.at[:, pl.ds(0, units // 2)], d_low.at[:, pl.ds(units // 2, units // 2)])
    )
    outs += [
        pltpu.make_async_copy(src, dst, out_sems.at[2 + i])
        for i, (src, dst) in enumerate(
            (
                (g_low.at[pl.ds(half, half)], glu_send),
                (d_cuts[1], down_send),
                (g_low.at[pl.ds(0, half)], glu_keep),
                (d_cuts[0], down_keep),
            )
        )
    ]
    for copy in outs[2:]:
        copy.start()
    for copy in outs:
        copy.wait()


def glu_backward(ids, k, by_rows, n2_parts, ct_parts, saved, w_down):
    tokens, units = 2 * saved[0].shape[1], saved[0].shape[2]
    width = w_down.shape[2]
    n_parts = len(n2_parts)
    down_half = (width // 2, units) if by_rows else (width, units // 2)
    return call(
        functools.partial(glu_back_kernel, k, by_rows, n_parts),
        (1,),
        ids,
        [ANY] * (n_parts + 9),
        [ANY] * 5,
        [sds((tokens, 2 * units))] + [sds((width // 2, 2 * units))] * 2 + [sds(down_half)] * 2,
        (*n2_parts, *ct_parts, *saved, w_down),
        [
            pltpu.VMEM((tokens, width), LOW),
            pltpu.VMEM((tokens, width), LOW),
            pltpu.VMEM((tokens, units), LOW),
            pltpu.VMEM((tokens, units), LOW),
            pltpu.VMEM((tokens, units), LOW),
            pltpu.VMEM((units, width), LOW),
            pltpu.VMEM((tokens, 2 * units), LOW),
            pltpu.VMEM((width, 2 * units), F32),
            pltpu.VMEM((width, units), F32),
            pltpu.VMEM((width, 2 * units), LOW),
            pltpu.VMEM((width, units), LOW),
            pltpu.SemaphoreType.DMA((7,)),
            pltpu.SemaphoreType.DMA((6,)),
            pltpu.SemaphoreType.DMA((n_parts,)),
            pltpu.SemaphoreType.DMA((2,)),
        ],
        mib=44,
    )


def n2_grad_kernel(ids, *refs):
    grads, w_glu, own, other = refs[:CHUNKS], refs[-3], refs[-2], refs[-1]
    result = dot(grads[0][...], w_glu[0], 1, 1)
    for k in range(1, CHUNKS):
        result += dot(grads[k][...], w_glu[k], 1, 1)

    @pl.when(pl.program_id(0) < pl.num_programs(0) // 2)
    def _():
        other[...] = result.astype(LOW)

    @pl.when(pl.program_id(0) >= pl.num_programs(0) // 2)
    def _():
        own[...] = result


def n2_gradient(ids, grads, w_glu, rows=256):
    tokens, cols = grads[0].shape
    width = w_glu.shape[1]
    per = tokens // 2 // rows
    return call(
        n2_grad_kernel,
        (2 * per,),
        ids,
        [pl.BlockSpec((rows, cols), lambda i, ids: ((i + per) % (2 * per), 0))] * CHUNKS + [kept(w_glu.shape)],
        [
            pl.BlockSpec((rows, width), lambda i, ids: (jnp.maximum(i - per, 0), 0)),
            pl.BlockSpec((rows, width), lambda i, ids: (jnp.minimum(i, per - 1), 0)),
        ],
        [sds((tokens // 2, width), F32), sds((tokens // 2, width))],
        (*grads, w_glu),
        mib=24,
    )


def combine_kernel(ids, own, other, residual, stay, later, send):
    span = stay.shape[1]
    second, first = 2 - ids[CORE], 1 + ids[CORE]
    for r, out, at in ((0, stay, 0), (second, later, 0), (first, send, 0), (3, send, 1)):
        rows = pl.ds(pl.multiple_of(r * span, span), span)
        value = (residual[0, r] + (own[rows, :] + other[rows, :].astype(F32))).astype(LOW)
        if out is send:
            send[at, 0] = value
        else:
            out[0] = value


def combine(ids, own, other, residual):
    slots, n_blocks, span, width = residual.shape
    rows = pl.BlockSpec((n_blocks * span, width), lambda s, ids: (s, 0))
    block = pl.BlockSpec((1, span, width), lambda s, ids: (s, 0, 0))
    return call(
        combine_kernel,
        (slots,),
        ids,
        [rows, rows, pl.BlockSpec((1, n_blocks, span, width), lambda s, ids: (s, 0, 0, 0))],
        [block, block, pl.BlockSpec((2, 1, span, width), lambda s, ids: (0, s, 0, 0))],
        [sds((slots, span, width))] * 2 + [sds((2, slots, span, width))],
        (own, other, residual),
        mib=16,
    )


def place_halves(ids, grads, keep, send):
    at = 0
    for grad in grads:
        size = grad.shape[0] // 8
        for q in range(4):
            to = ids[ROW_AT + q]
            for c in range(2):
                rows = grad[(2 * q + c) * size : (2 * q + c + 1) * size]

                @pl.when(ids[CORE] == c)
                def _(rows=rows, to=to, at=at, size=size):
                    keep[to, at : at + size] = rows

                @pl.when(ids[CORE] != c)
                def _(rows=rows, to=(to % 2) * 2 + to // 2, at=at, size=size):
                    send[to, at : at + size] = rows

        at += size


def accumulate(step, ref, value):
    @pl.when(step == 0)
    def _():
        ref[...] = value

    @pl.when(step > 0)
    def _():
        ref[...] += value


def back_out_kernel(
    ids, n2g_own, n2g_other, residual, cot, gated, conv, p_gate, normed, w_out, taps, gain2,
    residual_grad, conv_grad, pg_gate, small, keep, send, branch, out_total, in_total,
):
    s = pl.program_id(0)
    n_blocks, span = residual.shape[1:3]
    count = n_blocks * span
    gain_grad = jnp.zeros((1, branch.shape[1]), F32)
    for r in range(n_blocks):
        at = pl.multiple_of((ids[SEQ] ^ r) * span, span)
        rows = slice(r * span, (r + 1) * span)
        grad = n2g_own[rows] + n2g_other[rows].astype(F32)
        unit, inverse = standardize(residual[0, r])
        gain_grad += jnp.sum(grad * unit, axis=0, keepdims=True)
        value = cot[rows].astype(F32) + norm_back(grad, unit, inverse, gain2[...])
        residual_grad[0, r] = value
        branch[pl.ds(at, span), :] = value.astype(LOW)
    live = live_mask(ids[LENGTH + s], count)
    gated_grad = live * dot(branch[...], w_out[...], 1, 1)
    conv_grad[0] = (gated_grad * mix(p_gate[0], taps[...])).astype(LOW)
    sums, pg = mix_back(gated_grad * conv[0].astype(F32), p_gate[0], taps[...])
    pg_gate[0] = pg
    accumulate(s, small, jnp.concatenate(sums + [gain_grad], axis=0))
    accumulate(s, out_total, dot(gated[0], branch[...], 0, 0))
    accumulate(s, in_total, dot(normed[0], pg, 0, 0))

    @pl.when(s == pl.num_programs(0) - 1)
    def _():
        place_halves(ids, (out_total[...].astype(LOW), in_total[...].astype(LOW)), keep, send)


def back_out(ids, n2g_own, n2g_other, residual, cot, gated, conv, p_all, normed, w_out, taps, gain2):
    slots, n_blocks, span, width = residual.shape
    count = n_blocks * span
    rows = pl.BlockSpec((count, width), lambda s, ids: (s, 0))
    seqs = pl.BlockSpec((1, count, width), lambda s, ids: (s, 0, 0))
    rel = pl.BlockSpec((1, n_blocks, span, width), lambda s, ids: (s, 0, 0, 0))
    part = (4, 2 * width // 8, width)
    return call(
        back_out_kernel,
        (slots,),
        ids,
        [rows, rows, rel, rows] + [seqs] * 4 + [kept(w_out.shape), kept((3, width)), kept((1, width))],
        [rel, seqs, seqs, whole((4, width)), whole(part), whole(part)],
        [sds(residual.shape, F32), sds((slots, count, width)), sds((slots, count, width)), sds((4, width), F32)]
        + [sds(part)] * 2,
        (n2g_own, n2g_other, residual, cot, gated, conv, p_all, normed, w_out, taps, gain2),
        [pltpu.VMEM((count, width), LOW), pltpu.VMEM((width, width), F32), pltpu.VMEM((width, width), F32)],
        mib=48,
    )


def back_conv_kernel(
    ids, conv_grad, spec, p_value, p_cond, normed, table, t_value, t_cond,
    pg_ref, small, keep, send, static_total, in_total,
):
    s = pl.program_id(0)
    count, width = conv_grad.shape[1:]
    scale = count**-0.5
    live = live_mask(ids[LENGTH + s], count)
    gs = dot(table[...], conv_grad[0])
    re, im = spectrum_product(gs, spec[0, :, width:].astype(F32), -1.0)
    value_grad = live * dot(table[...], weighted(re, im, 1.0 / count), 0, 0)
    re, im = spectrum_product(gs, spec[0, :, :width].astype(F32), -1.0)
    back = dot(table[...], weighted(re, im, 1.0 / count), 0, 0)
    accumulate(s, static_total, back)
    sums_v, pg = mix_back(value_grad, p_value[0], t_value[...])
    pg_ref[0, :, :width] = pg
    cond_grad = (live * scale) * back * gelu_parts(mix(p_cond[0], t_cond[...]))[1]
    sums_c, pg = mix_back(cond_grad, p_cond[0], t_cond[...])
    pg_ref[0, :, width:] = pg
    accumulate(s, small, jnp.concatenate(sums_v + sums_c, axis=0))
    accumulate(s, in_total, dot(normed[0], pg_ref[0], 0, 0))

    @pl.when(s == pl.num_programs(0) - 1)
    def _():
        low = in_total[...].astype(LOW)
        place_halves(ids, (low[:, :width], low[:, width:], static_total[...].astype(LOW)), keep, send)


def back_conv(ids, conv_grad, spec, p_all, normed, table, taps):
    slots, count, width = conv_grad.shape
    seqs = lambda m, at=0: pl.BlockSpec((1, count, m * width), lambda s, ids, at=at: (s, 0, at))
    tap = lambda m: pl.BlockSpec((3, width), lambda s, ids, m=m: (0, m))
    part = (4, (2 * width + count) // 8, width)
    return call(
        back_conv_kernel,
        (slots,),
        ids,
        [seqs(1), seqs(2), seqs(1, 1), seqs(1, 2), seqs(1), kept(table.shape), tap(1), tap(2)],
        [seqs(2), whole((6, width)), whole(part), whole(part)],
        [sds((slots, count, 2 * width)), sds((6, width), F32), sds(part), sds(part)],
        (conv_grad, spec, p_all, p_all, normed, table, taps, taps),
        [pltpu.VMEM((count, width), F32), pltpu.VMEM((width, 2 * width), F32)],
        mib=48,
    )


def back_in_kernel(ids, pg_gate, pg_rest, x, residual_grad, in_weight, gain1, gain_ref, *refs):
    outs, total = refs[:-1], refs[-1]
    s = pl.program_id(0)
    width = x.shape[2]
    span = residual_grad.shape[2]
    total[...] = dot(pg_gate[0], in_weight[:, :width], 1, 1) + dot(pg_rest[0], in_weight[:, width:], 1, 1)
    gain_grad = jnp.zeros((1, width), F32)
    for r, out in enumerate(outs):
        at = pl.ds(pl.multiple_of((ids[SEQ] ^ r) * span, span), span)
        standard, inverse = standardize(x[0, at, :].astype(F32))
        grad = total[at, :]
        gain_grad += jnp.sum(grad * standard, axis=0, keepdims=True)
        out[0] = (residual_grad[0, r] + norm_back(grad, standard, inverse, gain1[...])).astype(LOW)
    accumulate(s, gain_ref, gain_grad)


def back_in(ids, pg_gate, pg_rest, x, residual_grad, in_weight, gain1):
    slots, count, width = x.shape
    n_blocks, span = residual_grad.shape[1:3]
    seqs = lambda m: pl.BlockSpec((1, count, m * width), lambda s, ids: (s, 0, 0))
    rel = pl.BlockSpec((1, n_blocks, span, width), lambda s, ids: (s, 0, 0, 0))
    return call(
        back_in_kernel,
        (slots,),
        ids,
        [seqs(1), seqs(2), seqs(1), rel, kept(in_weight.shape), kept((1, width))],
        [whole((1, width))] + [pl.BlockSpec((1, span, width), lambda s, ids: (s, 0, 0))] * n_blocks,
        [sds((1, width), F32)] + [sds((slots, span, width))] * n_blocks,
        (pg_gate, pg_rest, x, residual_grad, in_weight, gain1),
        [pltpu.VMEM((count, width), F32)],
        mib=32,
    )


def exchange(x, partner):
    n_seq, n_batch = lax.axis_size("seq"), lax.axis_size("batch")
    pairs = []
    for s in range(n_seq):
        for b in range(n_batch):
            to_s, to_b = partner(s, b)
            pairs.append((s * n_batch + b, to_s * n_batch + to_b))
    return lax.ppermute(x, ("seq", "batch"), pairs)


def across(s, b):
    return s, b ^ 1


def first_side(s, b):
    return s ^ (1 if b % 2 == 0 else 2), b


def second_side(s, b):
    return s ^ (2 if b % 2 == 0 else 1), b


def next_chip(s, b):
    return s, b ^ 2


def far_chip(s, b):
    return s, b ^ 4


def blocks_of(r):
    return lambda s, b: (s ^ r, b)


def tie(*groups):
    return lax.optimization_barrier(groups)


class Piece:
    def __init__(self, keep, send, steps):
        self.keep, self.steps = keep, list(steps)
        self.arriving, self.place = exchange(send, self.steps[0][0]), 0


def shape_after(shape, cut):
    rows, cols = shape
    if cut == "rows":
        return rows // 2, cols
    if cut == "lanes":
        return rows, cols // 2
    return rows, cols


def slabs(shape):
    return shape[0] * shape[1] // LANES


def engine_kernel(plan, n_in, n_out, ids, *refs):
    ins, outs, rest = refs[:n_in], refs[n_in : n_in + n_out], refs[n_in + n_out :]
    scratch, sem_in, sem_out = rest[:-2], rest[-2], rest[-1]
    loads, stores = [], []
    for i, (keep, src, row, *_) in enumerate(plan):
        held, arrived = scratch[4 * i : 4 * i + 2]
        pair = (
            pltpu.make_async_copy(ins[keep], held, sem_in.at[2 * i]),
            pltpu.make_async_copy(ins[src].at[pl.ds(row, arrived.shape[0])], arrived, sem_in.at[2 * i + 1]),
        )
        for copy in pair:
            copy.start()
        loads.append(pair)
    for i, (_, _, _, (rows, cols), cut, stay, dst, at) in enumerate(plan):
        held, arrived, left, gone = scratch[4 * i : 4 * i + 4]
        for copy in loads[i]:
            copy.wait()
        plain = arrived.shape == held.shape
        for c in range(cols // LANES):
            lanes = slice(c * LANES, (c + 1) * LANES)
            there = arrived[:, lanes] if plain else arrived[c * rows : (c + 1) * rows]
            total = (held[:, lanes].astype(F32) + there.astype(F32)).astype(LOW)
            if cut == "rows":
                half = rows // 2
                left[:, lanes] = total[:half]
                gone[c * half : (c + 1) * half] = total[half:]
            elif cut == "lanes" and c >= cols // LANES // 2:
                at_c = c - cols // LANES // 2
                gone[at_c * rows : (at_c + 1) * rows] = total
            else:
                left[:, lanes] = total
                if cut == "all":
                    gone[c * rows : (c + 1) * rows] = total
        if cut != "done":
            stores.append(
                pltpu.make_async_copy(gone, outs[dst].at[pl.ds(at, gone.shape[0])], sem_out.at[2 * i + 1])
            )
            stores[-1].start()
        stores.append(pltpu.make_async_copy(left, outs[stay], sem_out.at[2 * i]))
        stores[-1].start()
    for copy in stores:
        copy.wait()


def boundary(ids, pieces, guard):
    active = [p for p in pieces if p.steps]
    if not active:
        return guard
    arrivals = {id(p.arriving): p.arriving for p in active}
    keys = list(arrivals)
    landed, guard = tie([arrivals[k] for k in keys], guard)
    landed = dict(zip(keys, landed))
    partners = []
    for p in active:
        if len(p.steps) > 1 and p.steps[1][0] not in partners:
            partners.append(p.steps[1][0])
    ins, plan, stays, scratch = [landed[k] for k in keys], [], [], []
    rows_of = dict.fromkeys(partners, 0)
    for p in active:
        shape, cut = p.keep.shape, p.steps[0][1]
        after = shape_after(shape, cut)
        arrived = landed[id(p.arriving)]
        plain = arrived.shape == shape
        dst = at = None
        if cut != "done":
            partner = p.steps[1][0]
            dst, at = partners.index(partner), rows_of[partner]
            rows_of[partner] += slabs(after)
        plan.append((len(ins), keys.index(id(p.arriving)), p.place, shape, cut, len(partners) + len(stays), dst, at))
        ins.append(p.keep)
        stays.append(after)
        scratch += [
            pltpu.VMEM(shape, LOW),
            pltpu.VMEM(shape if plain else (slabs(shape), LANES), LOW),
            pltpu.VMEM(after, LOW),
            pltpu.VMEM((slabs(after) if cut != "done" else 16, LANES), LOW),
        ]
    out_shape = [sds((rows_of[q], LANES)) for q in partners] + [sds(x) for x in stays]
    outs = call(
        functools.partial(engine_kernel, plan, len(ins), len(out_shape)),
        (1,),
        ids,
        [ANY] * len(ins),
        [ANY] * len(out_shape),
        out_shape,
        ins,
        scratch + [pltpu.SemaphoreType.DMA((2 * len(plan),))] * 2,
        mib=16,
    )
    outs, guard = tie(outs, guard)
    sent = [exchange(outs[i], q) for i, q in enumerate(partners)]
    for p, (*_, stay, dst, at) in zip(active, plan):
        p.steps.pop(0)
        p.keep = outs[stay]
        p.arriving, p.place = (sent[dst], at) if p.steps else (None, None)
    return guard


def wide_sum(keep, arrived, at):
    r, cols = keep.shape
    parts = [arrived[at + c * r : at + (c + 1) * r] for c in range(cols // LANES)]
    return keep[...].astype(F32) + jnp.concatenate(parts, axis=1).astype(F32)


def by_chip_kernel(places, ids, a_keep, b_keep, small_keep, arrived, keep, send, small_out):
    a, b, small = [wide_sum(ref, arrived, at) for ref, at in zip((a_keep, b_keep, small_keep), places)]
    small = small.astype(LOW)
    width = a.shape[1]
    half = a.shape[0] // 2
    n_chip = 4
    rows = jnp.concatenate([a[half:], b[:half], b[half : 2 * half]], axis=1)
    size, part = 3 * width // n_chip, width // n_chip
    static = b[2 * half :]
    packed = static.shape[0] // n_chip
    count = keep.shape[1]
    for q in range(n_chip):
        top = jnp.concatenate([rows[:, q * size : (q + 1) * size], a[:half, q * part : (q + 1) * part]], axis=1)
        cols = static[:, q * part : (q + 1) * part]
        low = jnp.concatenate([cols[m * packed : (m + 1) * packed] for m in range(n_chip)], axis=1)
        message = jnp.concatenate([top, low], axis=0).astype(LOW)
        to = ids[CHIP_AT + q]

        @pl.when(to < 2)
        def _(message=message, to=to):
            keep[to] = message

        @pl.when(to >= 2)
        def _(message=message, to=to):
            send[pl.ds(pl.multiple_of((to - 2) * count, 16), count), :] = message

    send[2 * count :] = small
    small_out[...] = small


def by_chip(ids, a, b, small):
    width = a.keep.shape[1]
    half = a.keep.shape[0] // 2
    rows = half + (b.keep.shape[0] - 2 * half) // 4
    args = (a.keep, b.keep, small.keep, b.arriving)
    outs = [(2, rows, width), (2 * rows + small.keep.shape[0], width), small.keep.shape]
    return call(
        functools.partial(by_chip_kernel, (a.place, b.place, small.place)), (1,), ids, [whole(x.shape) for x in args], [whole(x) for x in outs], [sds(x) for x in outs],
        args, mib=24,
    )


def next_sum_kernel(ids, keep, small_ref, arrived, stay, send, small_out):
    rows = keep.shape[1]
    stay[...] = (keep[0].astype(F32) + arrived[:rows].astype(F32)).astype(LOW)
    send[:rows] = (keep[1].astype(F32) + arrived[rows : 2 * rows].astype(F32)).astype(LOW)
    small = (small_ref[...].astype(F32) + arrived[2 * rows :].astype(F32)).astype(LOW)
    send[rows:] = small
    small_out[...] = small


def next_sum(ids, keep, small, arrived):
    _, rows, width = keep.shape
    outs = [(rows, width), (rows + small.shape[0], width), small.shape]
    args = (keep, small, arrived)
    return call(
        next_sum_kernel, (1,), ids, [whole(x.shape) for x in args], [whole(x) for x in outs], [sds(x) for x in outs],
        args, mib=8,
    )


def cut_cores_kernel(batches, ids, total_ref, small_ref, arrived, *refs):
    glus, downs, own, send = refs[:CHUNKS], refs[CHUNKS : 2 * CHUNKS], refs[-2], refs[-1]
    rows, width = total_ref.shape
    total = total_ref[...].astype(F32) + arrived[:rows].astype(F32)
    small = small_ref[...].astype(F32) + arrived[rows:].astype(F32)
    top = width // 8
    size, part = 3 * width // batches, width // batches
    first = ids[CORE] == 0

    def put(at, low, high):
        here = slice(at, at + low.shape[0])
        own[here, : low.shape[1]] = jnp.where(first, low, high).astype(LOW)
        send[here, : low.shape[1]] = jnp.where(first, high, low).astype(LOW)
        return at + low.shape[0]

    static = jnp.concatenate([total[top:, m * 2 * part : (m + 1) * 2 * part] for m in range(4)], axis=0)
    pair = [
        jnp.concatenate(
            [total[:top, c * size : (c + 1) * size], total[:top, 2 * size + c * part : 2 * size + (c + 1) * part]], axis=1
        )
        for c in range(2)
    ]
    at = put(0, *pair)
    glu = jnp.concatenate([g[...].astype(F32) for g in glus], axis=1)
    side = [
        jnp.concatenate([glu[:, (2 * k + c) * LANES : (2 * k + c + 1) * LANES] for k in range(CHUNKS)], axis=1)
        for c in range(2)
    ]
    at = put(at, *side)
    down = jnp.concatenate([d[...].astype(F32) for d in downs], axis=1)
    at = put(at, down[: down.shape[0] // 2], down[down.shape[0] // 2 :])
    tall = jnp.concatenate([small[:, : width // 2], small[:, width // 2 :]], axis=0)
    at = put(at, tall, tall)
    put(at, static[:, :part], static[:, part:])


def cut_cores(ids, total, small, arrived, glus, downs, batches):
    rows, width = total.shape
    top = width // 8
    tall = 2 * small.shape[0]
    shape = (top + glus[0].shape[0] + downs[0].shape[0] // 2 + tall + 4 * (rows - top), CHUNKS * LANES)
    args = (total, small, arrived, *glus, *downs)
    return call(
        functools.partial(cut_cores_kernel, batches), (1,), ids, [whole(x.shape) for x in args], [whole(shape)] * 2,
        [sds(shape)] * 2, args, mib=16,
    )


def finish_kernel(ids, own, other, in_ref, out_ref, static_ref, small_ref, glu_ref, down_ref):
    part, share = out_ref.shape[1], own.shape[1]
    top, half, tall = in_ref.shape[0] // 2, glu_ref.shape[0], 2 * small_ref.shape[0]
    for ref, core in ((own, ids[CORE]), (other, 1 - ids[CORE])):
        rows = pl.ds(pl.multiple_of(core * top, 8), top)
        both = ref[:top].astype(F32)
        in_ref[rows, :] = both[:, : share - part]
        out_ref[rows, :] = both[:, share - part :]
        cols = pl.ds(pl.multiple_of(core * share, LANES), share)
        at = top
        glu_ref[:, cols] = ref[at : at + half].astype(F32)
        at += half
        down_ref[cols, :] = ref[at : at + part].astype(F32).T
        at += part + tall
        count = static_ref.shape[0] // 2
        static_ref[pl.ds(pl.multiple_of(core * count, 8), count), :] = ref[at:, :part].astype(F32)
    at = top + half + part
    tall_sum = own[at : at + tall].astype(F32) + other[at : at + tall].astype(F32)
    small_ref[...] = jnp.concatenate([tall_sum[: tall // 2], tall_sum[tall // 2 :]], axis=1)


def finish(ids, own, other, width, count, batches, n_small):
    part = width // batches
    rows = width // 4
    shapes = [
        (rows, 3 * part), (rows, part), (count // 4, part), (n_small, width), (rows, 2 * own.shape[1]),
        (2 * own.shape[1], part),
    ]
    return call(
        finish_kernel, (1,), ids, [whole(own.shape)] * 2, [whole(x) for x in shapes], [sds(x, F32) for x in shapes],
        (own, other), mib=16,
    )


def add_low(a, b):
    return (a.astype(F32) + b.astype(F32)).astype(LOW)


def seq_sums(keep, send):
    part = add_low(keep, exchange(send, first_side))
    return add_low(part[0], exchange(part[1], second_side))


def spread_sum(x, core, rows, dim):
    x = x.astype(F32)
    zero = jnp.zeros_like(x)
    low, high = jnp.where(core == 0, x, zero), jnp.where(core == 0, zero, x)
    both = jnp.concatenate([low, high], axis=dim)
    return lax.psum_scatter(both, "batch", scatter_dimension=1 - rows, tiled=True)


def on_device(
    inputs,
    lengths,
    norm1_gain,
    in_weight,
    short_taps,
    static_kernel,
    out_weight,
    norm2_gain,
    glu_weight,
    down_weight,
    cotangent,
):
    span, n_slots, width = inputs.shape
    n_seq, n_batch = lax.axis_size("seq"), lax.axis_size("batch")
    seq, batch = lax.axis_index("seq"), lax.axis_index("batch")
    core, place = batch % 2, batch // 2
    paired = n_batch == 8
    total_pos = span * n_seq
    slots = n_slots // n_seq
    tokens = slots * total_pos
    table = jnp.asarray(half_table(total_pos))
    gain1, gain2 = norm1_gain[None], norm2_gain[None]

    block = jnp.arange(4, dtype=jnp.int32)
    swap = lambda rel: (rel % 2) * 2 + rel // 2
    rel = block ^ seq
    row_at = jnp.where(core == 0, swap(rel), rel)
    chip_at = swap(block ^ place) if paired else block
    col_at = row_at if paired else block
    own_lengths = lax.dynamic_slice_in_dim(lengths, seq * slots, slots)
    head = jnp.stack([seq, core, place if paired else jnp.zeros_like(place)]).astype(jnp.int32)
    ids = jnp.concatenate([head, own_lengths, row_at, chip_at, col_at])

    x_turned = turn(ids, inputs, True)
    x_sent = [x_turned[s * n_seq : (s + 1) * n_seq] for s in range(slots)]
    x_blocks = [
        [sent[0]] + [exchange(sent[r], blocks_of(r)) for r in range(1, n_seq)] for sent in x_sent
    ]
    ct_turned = turn(ids, cotangent, False)
    weights = (in_weight, short_taps, static_kernel, table, out_weight, gain1, gain2)
    first, ct_turned = tie(x_blocks[0], ct_turned)
    x_blocks = [first] + x_blocks[1:]

    saved, n2_parts, n2_others = None, [], []
    for s in range(slots):
        if s == 1:
            x_blocks, ct_turned, saved = tie(x_blocks, ct_turned, saved)
            ct_blocks = [ct_turned[0]] + [exchange(ct_turned[r], blocks_of(r)) for r in range(1, n_seq)]
        *saved, n2 = mixer_forward(ids, s, slots, x_blocks[s], weights, saved)
        n2_parts.append(n2.reshape(total_pos, width))
        n2_others.append(exchange(n2_parts[-1], across))
    ct_blocks, n2_parts = tie(ct_blocks, n2_parts)
    ct_own = jnp.stack(ct_blocks, axis=1).reshape(tokens, width)
    ct_other = exchange(ct_own, across)
    p_all, spec, conv, gated, normed, x_whole, residual = saved
    *ff_own, out_own, w_glu, w_down = glu_forward(ids, n2_parts, (glu_weight, down_weight), n_seq, F32)
    n2_others, ct_other, w_glu = tie(n2_others, ct_other, w_glu)
    *ff_other, out_sent = glu_forward(ids, n2_others, (w_glu, w_down), n_seq, LOW)
    n2_parts = n2_parts + n2_others
    ff_saved = [*ff_own, *ff_other]
    ct_parts = [ct_own, ct_other]
    out_other = exchange(out_sent, across)

    pieces, chunks, grads = [], [], []
    for k in range(CHUNKS):
        by_rows = k == CHUNKS - 1
        gu, *parts = glu_backward(ids, k, by_rows, n2_parts, ct_parts, ff_saved, w_down)
        gu, w_down, w_glu = boundary(ids, pieces, (gu, w_down, w_glu))
        grads.append(gu)
        chunks.append(parts)
        if not paired:
            continue
        chip_steps, seq_steps = (next_chip, far_chip), (first_side, second_side)
        pieces.append(Piece(*parts[:2], zip(seq_steps + chip_steps, ("rows", "lanes", "lanes", "done"))))
        if by_rows:
            pieces.append(Piece(*parts[2:], zip(chip_steps + seq_steps, ("rows", "lanes", "lanes", "done"))))
        else:
            pieces.append(Piece(*parts[2:], zip(seq_steps + chip_steps, ("lanes", "rows", "rows", "done"))))
    ff_pieces = list(pieces)
    n2g_own, n2g_sent = n2_gradient(ids, grads, w_glu)
    n2g_other = exchange(n2g_sent, across)
    stay, later, sent = combine(ids, out_own, out_other, residual)
    flat = lambda a: a.reshape(-1, width)
    n2g_own, n2g_other, later, sent = boundary(ids, pieces, (n2g_own, n2g_other, later, sent))
    got_first, got_second = exchange(flat(sent), first_side), exchange(flat(later), second_side)
    residual_grad, conv_grad, pg_gate, small_out, a_keep, a_send = back_out(
        ids, n2g_own, n2g_other, residual, ct_own, gated, conv, p_all, normed, out_weight, short_taps, gain2
    )
    conv_grad, pg_gate, got_first, got_second = boundary(ids, pieces, (conv_grad, pg_gate, got_first, got_second))
    got_far = exchange(got_first[slots * span :], second_side)
    sum_steps = [(across, "rows"), (first_side, "rows"), (second_side, "done")]
    a = Piece(flat(a_keep), flat(a_send), sum_steps)
    if paired:
        pieces.append(a)
    pg_rest, small_conv, b_keep, b_send = back_conv(ids, conv_grad, spec, p_all, normed, table, short_taps)
    b = Piece(flat(b_keep), flat(b_send), sum_steps)
    if paired:
        pieces.append(b)
    block = lambda x: x.reshape(-1, slots, span, width)
    got_far, pg_rest = tie(got_far, pg_rest)
    output = unturn(
        ids, [(block(stay), 0), (block(got_first), 0), (block(got_second), 0), (block(got_far), 0)], LOW, True
    )
    pg_rest, pg_gate, output = boundary(ids, pieces, (pg_rest, pg_gate, output))
    gain_in, *x_sent = back_in(ids, pg_gate, pg_rest, x_whole, residual_grad, in_weight, gain1)
    x_got = [x_sent[0]] + [exchange(x_sent[r], blocks_of(r)) for r in range(1, n_seq)]
    small = jnp.concatenate([gain_in, small_out, small_conv], axis=0)
    n_small = small.shape[0]
    if paired:
        small = jnp.pad(small, ((0, -n_small % 16), (0, 0))).astype(LOW)
        small = Piece(small, small, [(first_side, "all"), (second_side, "all")])
        pieces.append(small)
        boundary(ids, pieces, ())
        keep, sent, total_small = by_chip(ids, a, b, small)
        keep, sent, total_small = next_sum(ids, keep, total_small, exchange(sent, next_chip))
        own, sent = cut_cores(
            ids, keep, total_small, exchange(sent, far_chip),
            [p.keep for p in ff_pieces[0::2]], [p.keep for p in ff_pieces[1::2]], n_batch,
        )
        total_in, total_out, total_static, small, total_glu, total_down = finish(
            ids, own, exchange(sent, across), width, total_pos, n_batch, small.keep.shape[0]
        )
    else:
        pieces = [a, b]
        while a.steps:
            boundary(ids, pieces, ())
        top = width // 8
        in_rows = jnp.concatenate([a.keep[top:], b.keep[:top], b.keep[top : 2 * top]], axis=1)
        total_in = spread_sum(in_rows, core, 0, 0)
        total_out = spread_sum(a.keep[:top], core, 0, 0)
        total_static = spread_sum(b.keep[2 * top :], core, 0, 0)
        side = n_seq // 2
        halves = lambda x: x.reshape(2, x.shape[0] // 2, x.shape[1])
        glu = jnp.stack(
            [seq_sums(halves(c[0]), halves(c[1])).reshape(-1, side, 2, side, LANES) for c in chunks], axis=4
        )
        glu = glu.transpose(0, 2, 1, 3, 4, 5).reshape(-1, 2 * n_seq, 1, CHUNKS * LANES)
        mine = (jnp.arange(2) == core)[:, None]
        glu = jnp.where(mine, glu, 0).astype(F32).reshape(glu.shape[0], -1)
        total_glu = lax.psum_scatter(glu, "batch", scatter_dimension=1, tiled=True)
        joined = [jnp.concatenate([c[2], c[3]], axis=int(c[2].shape[0] == width)) for c in chunks]
        down = jnp.stack([d.reshape(width, n_seq, LANES) for d in joined], axis=2)
        down = down.reshape(width, n_seq, 1, CHUNKS * LANES)
        down = jnp.where(mine, down, 0).astype(F32).reshape(width, -1)
        down = lax.psum_scatter(down, "batch", scatter_dimension=0, tiled=True)
        total_down = lax.psum_scatter(down, "seq", scatter_dimension=1, tiled=True).T

        small = lax.psum(small, ("seq", "batch"))
    total_taps = jnp.concatenate([small[1:4], small[5:8], small[8:11]], axis=1)
    input_grad = unturn(ids, [(block(g), 0) for g in x_got], F32, False)
    return (
        output,
        input_grad,
        small[0],
        total_in,
        total_taps,
        total_static,
        total_out,
        small[4],
        total_glu,
        total_down,
    )


def solution(mesh):
    return jax.shard_map(
        on_device,
        mesh=mesh,
        in_specs=(
            P("seq", "batch", None),
            P("batch"),
            P(),
            P(),
            P(),
            P(),
            P(),
            P(),
            P(),
            P(),
            P("seq", "batch", None),
        ),
        out_specs=(
            P("seq", "batch", None),
            P("seq", "batch", None),
            P(),
            P("seq", "batch"),
            P(),
            P("seq", "batch"),
            P("seq", "batch"),
            P(),
            P("seq", "batch"),
            P("seq", "batch"),
        ),
        check_vma=False,
    )
```

```python
import functools
import math

import jax
import jax.numpy as jnp
import numpy as np
from jax import lax
from jax.experimental import pallas as pl
from jax.experimental.pallas import tpu as pltpu
from jax.sharding import PartitionSpec as P

F32 = jnp.float32
LOW = jnp.bfloat16
CHUNKS = 3
LANES = 128
ROOT = math.sqrt(2.0 / math.pi)
CUBE = 0.044715
MIB = 2**20
COST = 1000
LONG = 3 * 10**10
TILES = 4
ANY = pl.BlockSpec(memory_space=pl.ANY)

SEQ, CORE, PLACE, LENGTH, ROW_AT, CHIP_AT, COL_AT = 0, 1, 2, 3, 5, 9, 13


def half_table(count):
    steps = np.arange(count)
    angle = (np.arange(count // 2)[:, None] * steps[None, :] % count) * (2.0 * math.pi / count)
    low_rows = np.cos(angle)
    high_rows = -np.sin(angle)
    high_rows[0] = np.where(steps % 2 == 0, 1.0, -1.0)
    return np.concatenate([low_rows, high_rows], axis=0).astype(LOW)


def dot(a, b, ca=1, cb=0):
    return lax.dot_general(a, b, (((ca,), (cb,)), ((), ())), preferred_element_type=F32)


def gelu_parts(z):
    square = z * z
    tanh = jnp.tanh(z * (ROOT + (ROOT * CUBE) * square))
    plus = 0.5 + 0.5 * tanh
    act = z * plus
    return act, plus + act * (1.0 - tanh) * (ROOT + (3.0 * ROOT * CUBE) * square)


def gelu(z):
    return z * (0.5 + 0.5 * jnp.tanh(z * (ROOT + (ROOT * CUBE) * (z * z))))


def standardize(values):
    centred = values - jnp.mean(values, axis=-1, keepdims=True)
    inverse = lax.rsqrt(jnp.mean(centred * centred, axis=-1, keepdims=True) + 1e-05)
    return centred * inverse, inverse


def norm_back(grad_in, standard, inverse, gain_vec):
    scaled = grad_in * gain_vec
    inner = (
        scaled
        - jnp.mean(scaled, axis=-1, keepdims=True)
        - standard * jnp.mean(scaled * standard, axis=-1, keepdims=True)
    )
    return inverse * inner


def shifts(a):
    count = a.shape[0]
    row = lax.broadcasted_iota(jnp.int32, a.shape, 0)
    before = jnp.where(row == 0, 0.0, pltpu.roll(a, 1, 0))
    after = jnp.where(row == count - 1, 0.0, pltpu.roll(a, count - 1, 0))
    return before, after


def mix(low, taps):
    wide = low.astype(F32)
    before, after = shifts(wide)
    return taps[0:1] * before + taps[1:2] * wide + taps[2:3] * after


def mix_back(grad, low, taps):
    wide = low.astype(F32)
    before, after = shifts(grad)
    sums = [jnp.sum(side * wide, axis=0, keepdims=True) for side in (after, grad, before)]
    return sums, (taps[0:1] * after + taps[1:2] * grad + taps[2:3] * before).astype(LOW)


def spectrum_product(a, b, sign):
    half = a.shape[0] // 2
    ar, ai, br, bi = a[:half], a[half:], b[:half], b[half:]
    first = lax.broadcasted_iota(jnp.int32, ar.shape, 0) == 0
    both = ai * bi
    re = ar * br - jnp.where(first, 0.0, sign * both)
    im = jnp.where(first, both, ai * br + sign * (ar * bi))
    return re, im


def weighted(re, im, scale):
    first = lax.broadcasted_iota(jnp.int32, (re.shape[0], 1), 0) == 0
    weight = jnp.where(first, scale, 2.0 * scale)
    return jnp.concatenate([(re * weight).astype(LOW), (im * weight).astype(LOW)], axis=0)


def live_mask(length, count):
    return (lax.broadcasted_iota(jnp.int32, (count, 1), 0) < length).astype(F32)


def whole(shape):
    return pl.BlockSpec(shape, lambda *at: (0,) * len(shape))


def kept(shape):
    return pl.BlockSpec(shape, lambda *at: (0,) * len(shape), pipeline_mode=pl.Buffered(1))


def sds(shape, dtype=LOW):
    return jax.ShapeDtypeStruct(shape, dtype)


def call(body, grid, ids, in_specs, out_specs, out_shape, args, scratch=(), aliases=None, mib=12, cost=COST):
    return pl.pallas_call(
        body,
        grid_spec=pltpu.PrefetchScalarGridSpec(
            num_scalar_prefetch=1, grid=grid, in_specs=in_specs, out_specs=out_specs, scratch_shapes=list(scratch)
        ),
        out_shape=out_shape,
        compiler_params=pltpu.CompilerParams(vmem_limit_bytes=mib * MIB),
        input_output_aliases=aliases or {},
        cost_estimate=pl.CostEstimate(flops=cost, bytes_accessed=COST, transcendentals=0),
    )(ids, *args)


def turn_kernel(by_slot, ids, x_ref, *refs):
    outs, held = refs[:-1], refs[-1]
    held[...] = jnp.swapaxes(x_ref[...].astype(F32), 0, 1).astype(LOW)
    n_seq = 4
    own = held.shape[0] // n_seq
    for r in range(n_seq):
        at = (ids[SEQ] ^ r) * own
        for s in range(own):
            if by_slot:
                outs[s * n_seq + r][...] = held[at + s]
            else:
                outs[r][s] = held[at + s]


def turn(ids, x, by_slot):
    span, slots, width = x.shape
    own = slots // 4
    shape = (span, width) if by_slot else (own, span, width)
    n_out = slots if by_slot else 4
    return call(
        functools.partial(turn_kernel, by_slot), (1,), ids, [whole(x.shape)], [whole(shape)] * n_out,
        [sds(shape)] * n_out, (x,), [pltpu.VMEM((slots, span, width), LOW)], mib=20,
    )


def unturn_kernel(places, ids, *refs):
    blocks, out, held = refs[:-2], refs[-2], refs[-1]
    slots, span, width = held.shape
    own = slots // 4
    rels = range(4) if places is None else (0, 1 + ids[CORE], 2 - ids[CORE], 3)
    for i, (rel, block) in enumerate(zip(rels, blocks)):
        for s in range(own):
            to = (ids[SEQ] ^ rel) * own + s
            if places is None or i == 0:
                held[to] = block[s].astype(F32)
            else:
                for c in range(width // LANES):
                    row = places[i - 1] + (c * own + s) * span
                    held[to, :, c * LANES : (c + 1) * LANES] = block[row : row + span].astype(F32)
    out[...] = jnp.swapaxes(held[...], 0, 1).astype(out.dtype)


def unturn(ids, blocks, dtype, places=None):
    own, span, width = blocks[0].shape
    slots = own * 4
    return call(
        functools.partial(unturn_kernel, places),
        (1,),
        ids,
        [whole(b.shape) for b in blocks],
        whole((span, slots, width)),
        sds((span, slots, width), dtype),
        blocks,
        [pltpu.VMEM((slots, span, width), F32)],
        mib=32,
    )


def mixer_kernel(
    slot, ids, x0, x1, x2, x3, in_weight, taps, static, table, w_out, gain1, gain2, *refs
):
    p_ref, spec_ref, conv_ref, gated_ref, normed_ref, x_ref, residual_ref, n2_ref, total = refs[-9:]
    blocks = (x0, x1, x2, x3)
    span, width = x0.shape
    count = span * len(blocks)
    scale = count**-0.5
    for r, block in enumerate(blocks):
        at = pl.multiple_of((ids[SEQ] ^ r) * span, span)
        wide = block[...].astype(F32)
        standard, _ = standardize(wide)
        normed_ref[0, pl.ds(at, span), :] = (standard * gain1[...]).astype(LOW)
        x_ref[0, pl.ds(at, span), :] = block[...]
        total[pl.ds(at, span), :] = wide
    live = live_mask(ids[LENGTH + slot], count)
    p_ref[0] = dot(normed_ref[0], in_weight[...]).astype(LOW)
    static_spec = dot(table[...], static[...].astype(LOW))
    value = (live * mix(p_ref[0, :, width : 2 * width], taps[:, width : 2 * width])).astype(LOW)
    vs = dot(table[...], value)
    cond = (live * gelu(mix(p_ref[0, :, 2 * width :], taps[:, 2 * width :]))).astype(LOW)
    ks = static_spec + scale * dot(table[...], cond)
    spec_ref[0, :, :width], spec_ref[0, :, width:] = vs.astype(LOW), ks.astype(LOW)
    re, im = spectrum_product(vs, ks, 1.0)
    conv = dot(table[...], weighted(re, im, 1.0 / count), 0, 0).astype(LOW)
    conv_ref[0] = conv
    gated = (live * mix(p_ref[0, :, :width], taps[:, :width]) * conv.astype(F32)).astype(LOW)
    gated_ref[0] = gated
    total[...] += dot(gated, w_out[...])
    for r in range(len(blocks)):
        at = pl.multiple_of((ids[SEQ] ^ r) * span, span)
        rows = total[pl.ds(at, span), :]
        residual_ref[0, r] = rows
        standard, _ = standardize(rows)
        n2_ref[r] = (standard * gain2[...]).astype(LOW)


def mixer_forward(ids, slot, slots, x_blocks, weights, before):
    span, width = x_blocks[0].shape
    count = span * len(x_blocks)
    in_weight, taps, static, table, w_out, gain1, gain2 = weights
    seqs = lambda m: pl.BlockSpec((1, count, m * width), lambda i, ids: (slot, 0, 0))
    cols = (3, 2, 1, 1, 1, 1)
    rel = (len(x_blocks), span, width)
    args = (*x_blocks, in_weight, taps, static, table, w_out, gain1, gain2)
    in_specs = [kept(a.shape) for a in args]
    aliases = {}
    if before is not None:
        aliases = {1 + len(args) + i: i for i in range(len(before))}
        args, in_specs = args + tuple(before), in_specs + [ANY] * len(before)
    return call(
        functools.partial(mixer_kernel, slot),
        (1,),
        ids,
        in_specs,
        [seqs(m) for m in cols] + [pl.BlockSpec((1, *rel), lambda i, ids: (slot, 0, 0, 0)), whole(rel)],
        [sds((slots, count, m * width)) for m in cols] + [sds((slots, *rel), F32), sds(rel)],
        args,
        [pltpu.VMEM((count, width), F32)],
        aliases,
        mib=48,
        cost=LONG,
    )


def glu_kernel(k, last, n_seq, slots, ids, *refs):
    n_blocks = 4
    n2_parts, ct_parts = refs[: 2 * slots], refs[2 * slots : 2 * slots + 2 * n_blocks]
    glu_hbm, down_hbm, rest = refs[2 * (slots + n_blocks)], refs[2 * (slots + n_blocks) + 1], refs[2 * (slots + n_blocks) + 2 :]
    if k > 0:
        sums_in, rest = rest[:2], rest[2:]
    glu_keep, glu_send, down_keep, down_send, *rest = rest
    n_sums = 4 if last else 2
    sums_out, rest = rest[:n_sums], rest[n_sums:]
    (n2, ct, w_glu, w_down, hidden, gu, g_low, d_low, sums, low,
     n2_sems, ct_sems, w_sems, sum_sems, out_sems) = rest
    rows = n2.shape[0] // 2
    span = rows // n_blocks // slots
    units = w_down.shape[0]
    halves = [pl.ds(h * rows, rows) for h in range(2)]

    def load(h):
        copies = []
        for s in range(slots):
            for r in range(n_blocks):
                copies.append(
                    pltpu.make_async_copy(
                        n2_parts[h * slots + s].at[pl.ds(r * span, span)],
                        n2.at[pl.ds(h * rows + (r * slots + s) * span, span)],
                        n2_sems.at[(h * slots + s) * n_blocks + r],
                    )
                )
        return copies, [
            pltpu.make_async_copy(
                ct_parts[h * n_blocks + r],
                ct.at[pl.ds(h * rows + r * slots * span, slots * span)],
                ct_sems.at[h * n_blocks + r],
            )
            for r in range(n_blocks)
        ]

    loads = [load(h) for h in range(2)]
    gate_copies, down_copies = [], []
    for m in range(2 * n_seq):
        col = pl.multiple_of(((2 * m + ids[CORE]) * CHUNKS + k) * LANES, LANES)
        gate_copies.append(
            pltpu.make_async_copy(
                glu_hbm.at[:, pl.ds(col, LANES)], w_glu.at[:, pl.ds(m * LANES, LANES)], w_sems.at[m]
            )
        )
    for m in range(n_seq):
        row = pl.multiple_of(((2 * m + ids[CORE]) * CHUNKS + k) * LANES, LANES)
        down_copies.append(
            pltpu.make_async_copy(
                down_hbm.at[pl.ds(row, LANES)], w_down.at[pl.ds(m * LANES, LANES)], w_sems.at[2 * n_seq + m]
            )
        )
    sum_copies = [
        [pltpu.make_async_copy(sums_in[i].at[halves[h]], sums.at[i, h], sum_sems.at[2 * i + h]) for i in range(2)]
        for h in range(2)
    ] if k > 0 else [[], []]
    for copy in loads[0][0] + gate_copies + down_copies + loads[0][1] + loads[1][0] + loads[1][1]:
        copy.start()
    for copy in sum_copies[0] + sum_copies[1]:
        copy.start()
    outs = []
    for h in range(2):
        here = halves[h]
        for copy in loads[h][0] + (gate_copies if h == 0 else []):
            copy.wait()
        gate_up = dot(n2[here], w_glu[...])
        gate, up = gate_up[:, :units], gate_up[:, units:]
        for copy in loads[h][1] + (down_copies if h == 0 else []):
            copy.wait()
        hidden_grad = dot(ct[here], w_down[...], 1, 1)
        act, slope = gelu_parts(gate)
        hidden[here] = (act * up).astype(LOW)
        gu[here, :units] = (hidden_grad * up * slope).astype(LOW)
        gu[here, units:] = (hidden_grad * act).astype(LOW)
        for copy in sum_copies[h]:
            copy.wait()
        for i, value in enumerate((dot(gu[here], w_glu[...], 1, 1), dot(hidden[here], w_down[...]))):
            if k > 0:
                value = sums[i, h] + value
            if last and h == 1:
                low[i] = value.astype(LOW)
                copy = pltpu.make_async_copy(low.at[i], sums_out[2 * i + 1], out_sems.at[4 + 2 * i + h])
            else:
                sums[i, h] = value
                to = sums_out[2 * i] if last else sums_out[i].at[here]
                copy = pltpu.make_async_copy(sums.at[i, h], to, out_sems.at[4 + 2 * i + h])
            copy.start()
            outs.append(copy)
    g_sum, d_sum = dot(n2[...], gu[...], 0, 0), dot(ct[...], hidden[...], 0, 0)
    side = units // 2
    size = g_sum.shape[0] // 4
    for q in range(4):
        here = pl.ds(pl.multiple_of(ids[ROW_AT + q] * size, size), size)
        for high in range(2):
            for g in range(2):
                at = (high ^ (ids[PLACE] % 2)) * 2 + (g ^ (ids[PLACE] // 2 % 2))
                from_col = g * units + high * side
                part = g_sum[q * size : (q + 1) * size, from_col : from_col + side]
                g_low[here, pl.ds(pl.multiple_of(at * side, side), side)] = part.astype(LOW)
    for q in range(4):
        here = pl.ds(pl.multiple_of(ids[CHIP_AT + q] * size, size), size)
        for s in range(4):
            part = d_sum[q * size : (q + 1) * size, s * LANES : (s + 1) * LANES]
            d_low[here, pl.ds(pl.multiple_of(ids[COL_AT + s] * LANES, LANES), LANES)] = part.astype(LOW)
    half = d_low.shape[0] // 2
    for i, (src, to) in enumerate(
        (
            (g_low.at[pl.ds(half, half)], glu_send),
            (d_low.at[pl.ds(half, half)], down_send),
            (g_low.at[pl.ds(0, half)], glu_keep),
            (d_low.at[pl.ds(0, half)], down_keep),
        )
    ):
        copy = pltpu.make_async_copy(src, to, out_sems.at[i])
        copy.start()
        outs.append(copy)
    for copy in outs:
        copy.wait()


def glu_chunk(ids, k, n2_parts, ct_parts, glu_weight, down_weight, sums, n_seq):
    width, units = glu_weight.shape[0], n_seq * LANES
    slots, n_blocks = len(n2_parts) // 2, 4
    tokens = sum(p.shape[0] for p in n2_parts)
    last = k == CHUNKS - 1
    rows = tokens // 2
    sum_shapes = [sds((rows, width), F32), sds((rows, width))] * 2 if last else [sds((tokens, width), F32)] * 2
    args = (*n2_parts, *ct_parts, glu_weight, down_weight, *(sums if k > 0 else ()))
    return call(
        functools.partial(glu_kernel, k, last, n_seq, slots),
        (1,),
        ids,
        [ANY] * len(args),
        [ANY] * (4 + len(sum_shapes)),
        [sds((width // 2, 2 * units))] * 2 + [sds((width // 2, units))] * 2 + sum_shapes,
        args,
        [
            pltpu.VMEM((tokens, width), LOW),
            pltpu.VMEM((tokens, width), LOW),
            pltpu.VMEM((width, 2 * units), LOW),
            pltpu.VMEM((units, width), LOW),
            pltpu.VMEM((tokens, units), LOW),
            pltpu.VMEM((tokens, 2 * units), LOW),
            pltpu.VMEM((width, 2 * units), LOW),
            pltpu.VMEM((width, units), LOW),
            pltpu.VMEM((2, 2, rows, width), F32),
            pltpu.VMEM((2, rows, width), LOW),
            pltpu.SemaphoreType.DMA((2 * slots * n_blocks,)),
            pltpu.SemaphoreType.DMA((2 * n_blocks,)),
            pltpu.SemaphoreType.DMA((3 * n_seq,)),
            pltpu.SemaphoreType.DMA((4,)),
            pltpu.SemaphoreType.DMA((8,)),
        ],
        mib=56,
        cost=LONG,
    )


def combine_kernel(ids, own, other, residual, stay, later, send):
    span = stay.shape[1]
    second, first = 2 - ids[CORE], 1 + ids[CORE]
    for r, out, at in ((0, stay, 0), (second, later, 0), (first, send, 0), (3, send, 1)):
        value = (residual[0, r] + (own[r, 0] + other[r, 0].astype(F32))).astype(LOW)
        if out is send:
            send[at, 0] = value
        else:
            out[0] = value


def combine(ids, own, other, residual):
    slots, n_blocks, span, width = residual.shape
    rows = pl.BlockSpec((n_blocks, 1, span, width), lambda s, ids: (0, s, 0, 0))
    block = pl.BlockSpec((1, span, width), lambda s, ids: (s, 0, 0))
    own, other = [x.reshape(n_blocks, slots, span, width) for x in (own, other)]
    return call(
        combine_kernel,
        (slots,),
        ids,
        [rows, rows, pl.BlockSpec((1, n_blocks, span, width), lambda s, ids: (s, 0, 0, 0))],
        [block, block, pl.BlockSpec((2, 1, span, width), lambda s, ids: (0, s, 0, 0))],
        [sds((slots, span, width))] * 2 + [sds((2, slots, span, width))],
        (own, other, residual),
        mib=16,
    )


def place_halves(ids, grads, keep, send):
    at = 0
    for grad in grads:
        size = grad.shape[0] // 8
        for q in range(4):
            to = ids[ROW_AT + q]
            for c in range(2):
                rows = grad[(2 * q + c) * size : (2 * q + c + 1) * size]

                @pl.when(ids[CORE] == c)
                def _(rows=rows, to=to, at=at, size=size):
                    keep[to, at : at + size] = rows

                @pl.when(ids[CORE] != c)
                def _(rows=rows, to=(to % 2) * 2 + to // 2, at=at, size=size):
                    send[to, at : at + size] = rows

        at += size


def accumulate(step, ref, value):
    @pl.when(step == 0)
    def _():
        ref[...] = value

    @pl.when(step > 0)
    def _():
        ref[...] += value


def back_out_kernel(
    ids, n2g_own, n2g_other, residual, ct0, ct1, ct2, ct3, gated, conv, p_gate, normed, w_out, taps, gain2,
    residual_grad, conv_grad, pg_gate, small, keep, send, branch, out_total, in_total,
):
    s = pl.program_id(0)
    n_blocks, span = residual.shape[1:3]
    count = n_blocks * span
    gain_grad = jnp.zeros((1, branch.shape[1]), F32)
    for r in range(n_blocks):
        at = pl.multiple_of((ids[SEQ] ^ r) * span, span)
        grad = n2g_own[r, 0] + n2g_other[r, 0].astype(F32)
        unit, inverse = standardize(residual[0, r])
        gain_grad += jnp.sum(grad * unit, axis=0, keepdims=True)
        value = (ct0, ct1, ct2, ct3)[r][0].astype(F32) + norm_back(grad, unit, inverse, gain2[...])
        residual_grad[0, r] = value
        branch[pl.ds(at, span), :] = value.astype(LOW)
    live = live_mask(ids[LENGTH + s], count)
    gated_grad = live * dot(branch[...], w_out[...], 1, 1)
    conv_grad[0] = (gated_grad * mix(p_gate[0], taps[...])).astype(LOW)
    sums, pg = mix_back(gated_grad * conv[0].astype(F32), p_gate[0], taps[...])
    pg_gate[0] = pg
    accumulate(s, small, jnp.concatenate(sums + [gain_grad], axis=0))
    accumulate(s, out_total, dot(gated[0], branch[...], 0, 0))
    accumulate(s, in_total, dot(normed[0], pg, 0, 0))

    @pl.when(s == pl.num_programs(0) - 1)
    def _():
        place_halves(ids, (out_total[...].astype(LOW), in_total[...].astype(LOW)), keep, send)


def back_out(ids, n2g_own, n2g_other, residual, cot, gated, conv, p_all, normed, w_out, taps, gain2):
    slots, n_blocks, span, width = residual.shape
    count = n_blocks * span
    rows = pl.BlockSpec((n_blocks, 1, span, width), lambda s, ids: (0, s, 0, 0))
    ct = pl.BlockSpec((1, span, width), lambda s, ids: (s, 0, 0))
    n2g_own, n2g_other = [x.reshape(n_blocks, slots, span, width) for x in (n2g_own, n2g_other)]
    seqs = pl.BlockSpec((1, count, width), lambda s, ids: (s, 0, 0))
    rel = pl.BlockSpec((1, n_blocks, span, width), lambda s, ids: (s, 0, 0, 0))
    part = (4, 2 * width // 8, width)
    return call(
        back_out_kernel,
        (slots,),
        ids,
        [rows, rows, rel] + [ct] * n_blocks + [seqs] * 4 + [kept(w_out.shape), kept((3, width)), kept((1, width))],
        [rel, seqs, seqs, whole((4, width)), whole(part), whole(part)],
        [sds(residual.shape, F32), sds((slots, count, width)), sds((slots, count, width)), sds((4, width), F32)]
        + [sds(part)] * 2,
        (n2g_own, n2g_other, residual, *cot, gated, conv, p_all, normed, w_out, taps, gain2),
        [pltpu.VMEM((count, width), LOW), pltpu.VMEM((width, width), F32), pltpu.VMEM((width, width), F32)],
        mib=48,
        cost=LONG,
    )


def back_conv_kernel(
    ids, conv_grad, spec, p_value, p_cond, normed, table, t_value, t_cond,
    pg_ref, small, keep, send, static_total, in_total,
):
    s = pl.program_id(0)
    count, width = conv_grad.shape[1:]
    scale = count**-0.5
    live = live_mask(ids[LENGTH + s], count)
    gs = dot(table[...], conv_grad[0])
    re, im = spectrum_product(gs, spec[0, :, width:].astype(F32), -1.0)
    value_grad = live * dot(table[...], weighted(re, im, 1.0 / count), 0, 0)
    re, im = spectrum_product(gs, spec[0, :, :width].astype(F32), -1.0)
    back = dot(table[...], weighted(re, im, 1.0 / count), 0, 0)
    accumulate(s, static_total, back)
    sums_v, pg = mix_back(value_grad, p_value[0], t_value[...])
    pg_ref[0, :, :width] = pg
    cond_grad = (live * scale) * back * gelu_parts(mix(p_cond[0], t_cond[...]))[1]
    sums_c, pg = mix_back(cond_grad, p_cond[0], t_cond[...])
    pg_ref[0, :, width:] = pg
    accumulate(s, small, jnp.concatenate(sums_v + sums_c, axis=0))
    accumulate(s, in_total, dot(normed[0], pg_ref[0], 0, 0))

    @pl.when(s == pl.num_programs(0) - 1)
    def _():
        low = in_total[...].astype(LOW)
        place_halves(ids, (low[:, :width], low[:, width:], static_total[...].astype(LOW)), keep, send)


def back_conv(ids, conv_grad, spec, p_all, normed, table, taps):
    slots, count, width = conv_grad.shape
    seqs = lambda m, at=0: pl.BlockSpec((1, count, m * width), lambda s, ids, at=at: (s, 0, at))
    tap = lambda m: pl.BlockSpec((3, width), lambda s, ids, m=m: (0, m))
    part = (4, (2 * width + count) // 8, width)
    return call(
        back_conv_kernel,
        (slots,),
        ids,
        [seqs(1), seqs(2), seqs(1, 1), seqs(1, 2), seqs(1), kept(table.shape), tap(1), tap(2)],
        [seqs(2), whole((6, width)), whole(part), whole(part)],
        [sds((slots, count, 2 * width)), sds((6, width), F32), sds(part), sds(part)],
        (conv_grad, spec, p_all, p_all, normed, table, taps, taps),
        [pltpu.VMEM((count, width), F32), pltpu.VMEM((width, 2 * width), F32)],
        mib=48,
        cost=LONG,
    )


def back_in_kernel(ids, pg_gate, pg_rest, x, residual_grad, in_weight, gain1, gain_ref, *refs):
    outs, total = refs[:-1], refs[-1]
    s = pl.program_id(0)
    width = x.shape[2]
    span = residual_grad.shape[2]
    total[...] = dot(pg_gate[0], in_weight[:, :width], 1, 1) + dot(pg_rest[0], in_weight[:, width:], 1, 1)
    gain_grad = jnp.zeros((1, width), F32)
    for r, out in enumerate(outs):
        at = pl.ds(pl.multiple_of((ids[SEQ] ^ r) * span, span), span)
        standard, inverse = standardize(x[0, at, :].astype(F32))
        grad = total[at, :]
        gain_grad += jnp.sum(grad * standard, axis=0, keepdims=True)
        out[0] = (residual_grad[0, r] + norm_back(grad, standard, inverse, gain1[...])).astype(LOW)
    accumulate(s, gain_ref, gain_grad)


def back_in(ids, pg_gate, pg_rest, x, residual_grad, in_weight, gain1):
    slots, count, width = x.shape
    n_blocks, span = residual_grad.shape[1:3]
    seqs = lambda m: pl.BlockSpec((1, count, m * width), lambda s, ids: (s, 0, 0))
    rel = pl.BlockSpec((1, n_blocks, span, width), lambda s, ids: (s, 0, 0, 0))
    return call(
        back_in_kernel,
        (slots,),
        ids,
        [seqs(1), seqs(2), seqs(1), rel, kept(in_weight.shape), kept((1, width))],
        [whole((1, width))] + [pl.BlockSpec((1, span, width), lambda s, ids: (s, 0, 0))] * n_blocks,
        [sds((1, width), F32)] + [sds((slots, span, width))] * n_blocks,
        (pg_gate, pg_rest, x, residual_grad, in_weight, gain1),
        [pltpu.VMEM((count, width), F32)],
        mib=32,
        cost=LONG,
    )


def exchange(x, partner):
    n_seq, n_batch = lax.axis_size("seq"), lax.axis_size("batch")
    pairs = []
    for s in range(n_seq):
        for b in range(n_batch):
            to_s, to_b = partner(s, b)
            pairs.append((s * n_batch + b, to_s * n_batch + to_b))
    return lax.ppermute(x, ("seq", "batch"), pairs)


def across(s, b):
    return s, b ^ 1


def first_side(s, b):
    return s ^ (1 if b % 2 == 0 else 2), b


def second_side(s, b):
    return s ^ (2 if b % 2 == 0 else 1), b


def next_chip(s, b):
    return s, b ^ 2


def far_chip(s, b):
    return s, b ^ 4


def blocks_of(r):
    return lambda s, b: (s ^ r, b)


def tie(*groups):
    return lax.optimization_barrier(groups)


class Piece:
    def __init__(self, keep, send, steps, alone=False):
        self.keep, self.send, self.steps = keep, send, list(steps)
        self.arriving, self.place, self.got = None, 0, []
        if alone:
            self.arriving = exchange(send, self.steps[0][0])


def shape_after(shape, cut):
    rows, cols = shape
    if cut == "rows":
        return rows // 2, cols
    if cut == "lanes":
        return rows, cols // 2
    return rows, cols


def slabs(shape):
    return shape[0] * shape[1] // LANES


def put_slabs(to, at, value):
    rows = value.shape[0]
    for c in range(value.shape[1] // LANES):
        to[at + c * rows : at + (c + 1) * rows] = value[:, c * LANES : (c + 1) * LANES]


def engine_kernel(plan, n_in, *refs):
    ins, outs = refs[:n_in], refs[n_in:]
    for op, *rest in plan:
        if op == "fresh":
            src, row, (rows, cols), dst, at = rest
            put_slabs(outs[dst], at, ins[src][row : row + rows])
        elif op == "move":
            src, row, rows, dst, at = rest
            outs[dst][at : at + rows] = ins[src][row : row + rows]
        else:
            keep, src, row, (rows, cols), cut, stay, dst, at = rest
            held, arrived = ins[keep], ins[src]
            plain = arrived.shape == held.shape
            for c in range(cols // LANES):
                lanes = slice(c * LANES, (c + 1) * LANES)
                there = arrived[:, lanes] if plain else arrived[row + c * rows : row + (c + 1) * rows]
                total = (held[:, lanes].astype(F32) + there.astype(F32)).astype(LOW)
                if cut == "rows":
                    half = rows // 2
                    outs[stay][:, lanes] = total[:half]
                    outs[dst][at + c * half : at + (c + 1) * half] = total[half:]
                elif cut == "lanes" and c >= cols // LANES // 2:
                    to = at + (c - cols // LANES // 2) * rows
                    outs[dst][to : to + rows] = total
                else:
                    outs[stay][:, lanes] = total
                    if cut == "all":
                        outs[dst][at + c * rows : at + (c + 1) * rows] = total


def boundary(ids, pieces, guard):
    active = [p for p in pieces if p.steps]
    if not active:
        return guard
    arrivals = {id(p.arriving): p.arriving for p in active if p.arriving is not None}
    keys = list(arrivals)
    landed, guard = tie([arrivals[k] for k in keys], guard)
    landed = dict(zip(keys, landed))
    partners = []
    for p in active:
        upcoming = p.steps if p.arriving is None else p.steps[1:]
        if upcoming and upcoming[0][0] not in partners:
            partners.append(upcoming[0][0])
    ins, index, plan, stays, results = [], {}, [], [], []
    rows_of = dict.fromkeys(partners, 0)

    def source(x):
        if id(x) not in index:
            index[id(x)] = len(ins)
            ins.append(x)
        return index[id(x)]

    def message(partner, rows):
        at = rows_of[partner]
        rows_of[partner] += rows
        return partners.index(partner), at

    for p in active:
        partner, cut = p.steps[0]
        if p.arriving is None:
            parts = 2 if cut == "relay" else 1
            shape = (p.send.shape[0] // parts, p.send.shape[1])
            dst, at = message(partner, parts * slabs(shape))
            for i in range(parts):
                plan.append(("fresh", source(p.send), i * shape[0], shape, dst, at + i * slabs(shape)))
            results.append((p, False, None, dst, at))
            continue
        arrived, n = landed[id(p.arriving)], slabs(p.keep.shape)
        if cut == "relay":
            dst, at = message(p.steps[1][0], 2 * n)
            plan.append(("fresh", source(p.keep), 0, p.keep.shape, dst, at))
            plan.append(("move", source(arrived), p.place + n, n, dst, at + n))
            p.got.append((arrived, p.place))
            results.append((p, True, None, dst, at))
        elif cut == "land":
            p.got += [(arrived, p.place), (arrived, p.place + n)]
            results.append((p, True, None, None, None))
        else:
            after = shape_after(p.keep.shape, cut)
            dst, at = message(p.steps[1][0], slabs(after)) if cut != "done" else (None, None)
            stay = len(partners) + len(stays)
            stays.append(after)
            plan.append(("add", source(p.keep), source(arrived), p.place, p.keep.shape, cut, stay, dst, at))
            results.append((p, True, stay, dst, at))
    outs = []
    if plan:
        shapes = [(rows_of[q], LANES) for q in partners] + stays
        size = sum(x.size for x in ins) + sum(a * b for a, b in shapes)
        outs = pl.pallas_call(
            functools.partial(engine_kernel, plan, len(ins)),
            out_shape=[sds(x) for x in shapes],
            in_specs=[pl.BlockSpec(memory_space=pltpu.VMEM)] * len(ins),
            out_specs=[pl.BlockSpec(memory_space=pltpu.VMEM)] * len(shapes),
            compiler_params=pltpu.CompilerParams(vmem_limit_bytes=2 * size + 4 * MIB),
            cost_estimate=pl.CostEstimate(flops=LONG, bytes_accessed=COST, transcendentals=0),
        )(*ins)
        outs, guard = tie(outs, guard)
    sent = [exchange(outs[i], q) for i, q in enumerate(partners)]
    for p, stepped, stay, dst, at in results:
        if stepped:
            p.steps.pop(0)
        if stay is not None:
            p.keep = outs[stay]
        p.arriving, p.place = (sent[dst], at) if p.steps else (None, None)
    return guard


def wide_sum(keep, arrived, at):
    r, cols = keep.shape
    parts = [arrived[at + c * r : at + (c + 1) * r] for c in range(cols // LANES)]
    return keep[...].astype(F32) + jnp.concatenate(parts, axis=1).astype(F32)


def by_chip_kernel(places, ids, a_keep, b_keep, small_keep, arrived, *outs):
    a = a_keep[...].astype(F32)
    b, small = [wide_sum(ref, arrived, at) for ref, at in zip((b_keep, small_keep), places)]
    width = a.shape[1]
    half = a.shape[0] // 2
    n_chip = len(outs)
    rows = jnp.concatenate([a[half:], b[:half], b[half : 2 * half]], axis=1)
    size, part = 3 * width // n_chip, width // n_chip
    static = b[2 * half :]
    packed = static.shape[0] // n_chip
    count = half + packed
    for q in range(n_chip):
        top = jnp.concatenate([rows[:, q * size : (q + 1) * size], a[:half, q * part : (q + 1) * part]], axis=1)
        cols = static[:, q * part : (q + 1) * part]
        tail = jnp.concatenate([cols[m * packed : (m + 1) * packed] for m in range(n_chip)], axis=1)
        message = jnp.concatenate([top, tail], axis=0).astype(LOW)
        for rel, out in enumerate(outs):

            @pl.when(ids[PLACE] == (q ^ rel))
            def _(message=message, out=out):
                out[:count] = message

    for out in outs:
        out[count:] = small.astype(LOW)


def by_chip(ids, a, b, small):
    width = a.keep.shape[1]
    half = a.keep.shape[0] // 2
    rows = half + (b.keep.shape[0] - 2 * half) // 4 + small.keep.shape[0]
    args = (a.keep, b.keep, small.keep, b.arriving)
    return call(
        functools.partial(by_chip_kernel, (b.place, small.place)), (1,), ids, [whole(x.shape) for x in args],
        [whole((rows, width))] * 4, [sds((rows, width))] * 4, args, mib=24,
    )


def cut_cores_kernel(batches, n_small, ids, *refs):
    parts, glus, downs, own, send = refs[:4], refs[4 : 4 + CHUNKS], refs[4 + CHUNKS : 4 + 2 * CHUNKS], refs[-2], refs[-1]
    total = sum(ref[...].astype(F32) for ref in parts)
    rows, width = total.shape
    total, small = total[: rows - n_small], total[rows - n_small :]
    top = width // 8
    size, part = 3 * width // batches, width // batches
    first = ids[CORE] == 0

    def put(at, low, high):
        here = slice(at, at + low.shape[0])
        own[here, : low.shape[1]] = jnp.where(first, low, high).astype(LOW)
        send[here, : low.shape[1]] = jnp.where(first, high, low).astype(LOW)
        return at + low.shape[0]

    static = jnp.concatenate([total[top:, m * 2 * part : (m + 1) * 2 * part] for m in range(4)], axis=0)
    pair = [
        jnp.concatenate(
            [total[:top, c * size : (c + 1) * size], total[:top, 2 * size + c * part : 2 * size + (c + 1) * part]], axis=1
        )
        for c in range(2)
    ]
    at = put(0, *pair)
    glu = jnp.concatenate([g[...].astype(F32) for g in glus], axis=1)
    side = [
        jnp.concatenate([glu[:, (2 * k + c) * LANES : (2 * k + c + 1) * LANES] for k in range(CHUNKS)], axis=1)
        for c in range(2)
    ]
    at = put(at, *side)
    down = jnp.concatenate([d[...].astype(F32) for d in downs], axis=1)
    at = put(at, down[: down.shape[0] // 2], down[down.shape[0] // 2 :])
    tall = jnp.concatenate([small[:, : width // 2], small[:, width // 2 :]], axis=0)
    at = put(at, tall, tall)
    put(at, static[:, :part], static[:, part:])


def cut_cores(ids, parts, glus, downs, batches, n_small):
    rows, width = parts[0].shape
    top = width // 8
    shape = (
        top + glus[0].shape[0] + downs[0].shape[0] // 2 + 2 * n_small + 4 * (rows - n_small - top), CHUNKS * LANES
    )
    args = (*parts, *glus, *downs)
    return call(
        functools.partial(cut_cores_kernel, batches, n_small), (1,), ids, [whole(x.shape) for x in args], [whole(shape)] * 2,
        [sds(shape)] * 2, args, mib=16,
    )


def finish_kernel(ids, own, other, in_ref, out_ref, static_ref, small_ref, glu_ref, down_ref):
    part, share = out_ref.shape[1], own.shape[1]
    top, half, tall = in_ref.shape[0] // 2, glu_ref.shape[0], 2 * small_ref.shape[0]
    for ref, core in ((own, ids[CORE]), (other, 1 - ids[CORE])):
        rows = pl.ds(pl.multiple_of(core * top, 8), top)
        both = ref[:top].astype(F32)
        in_ref[rows, :] = both[:, : share - part]
        out_ref[rows, :] = both[:, share - part :]
        cols = pl.ds(pl.multiple_of(core * share, LANES), share)
        at = top
        glu_ref[:, cols] = ref[at : at + half].astype(F32)
        at += half
        down_ref[cols, :] = ref[at : at + part].astype(F32).T
        at += part + tall
        count = static_ref.shape[0] // 2
        static_ref[pl.ds(pl.multiple_of(core * count, 8), count), :] = ref[at:, :part].astype(F32)
    at = top + half + part
    tall_sum = own[at : at + tall].astype(F32) + other[at : at + tall].astype(F32)
    small_ref[...] = jnp.concatenate([tall_sum[: tall // 2], tall_sum[tall // 2 :]], axis=1)


def finish(ids, own, other, width, count, batches, n_small):
    part = width // batches
    rows = width // 4
    shapes = [
        (rows, 3 * part), (rows, part), (count // 4, part), (n_small, width), (rows, 2 * own.shape[1]),
        (2 * own.shape[1], part),
    ]
    return call(
        finish_kernel, (1,), ids, [whole(own.shape)] * 2, [whole(x) for x in shapes], [sds(x, F32) for x in shapes],
        (own, other), mib=16,
    )


def add_low(a, b):
    return (a.astype(F32) + b.astype(F32)).astype(LOW)


def seq_sums(keep, send):
    part = add_low(keep, exchange(send, first_side))
    return add_low(part[0], exchange(part[1], second_side))


def spread_sum(x, core, rows, dim):
    x = x.astype(F32)
    zero = jnp.zeros_like(x)
    low, high = jnp.where(core == 0, x, zero), jnp.where(core == 0, zero, x)
    both = jnp.concatenate([low, high], axis=dim)
    return lax.psum_scatter(both, "batch", scatter_dimension=1 - rows, tiled=True)


def on_device(
    inputs,
    lengths,
    norm1_gain,
    in_weight,
    short_taps,
    static_kernel,
    out_weight,
    norm2_gain,
    glu_weight,
    down_weight,
    cotangent,
):
    span, n_slots, width = inputs.shape
    n_seq, n_batch = lax.axis_size("seq"), lax.axis_size("batch")
    seq, batch = lax.axis_index("seq"), lax.axis_index("batch")
    core, place = batch % 2, batch // 2
    paired = n_batch == 8
    total_pos = span * n_seq
    slots = n_slots // n_seq
    tokens = slots * total_pos
    table = jnp.asarray(half_table(total_pos))
    gain1, gain2 = norm1_gain[None], norm2_gain[None]

    block = jnp.arange(4, dtype=jnp.int32)
    swap = lambda rel: (rel % 2) * 2 + rel // 2
    rel = block ^ seq
    row_at = jnp.where(core == 0, swap(rel), rel)
    chip_at = swap(block ^ place) if paired else block
    col_at = row_at if paired else block
    own_lengths = lax.dynamic_slice_in_dim(lengths, seq * slots, slots)
    head = jnp.stack([seq, core, place if paired else jnp.zeros_like(place)]).astype(jnp.int32)
    ids = jnp.concatenate([head, own_lengths, row_at, chip_at, col_at])

    x_turned = turn(ids, inputs, True)
    x_sent = [x_turned[s * n_seq : (s + 1) * n_seq] for s in range(slots)]
    x_blocks = [
        [sent[0]] + [exchange(sent[r], blocks_of(r)) for r in range(1, n_seq)] for sent in x_sent
    ]
    ct_turned = turn(ids, cotangent, False)
    weights = (in_weight, short_taps, static_kernel, table, out_weight, gain1, gain2)
    first, ct_turned = tie(x_blocks[0], ct_turned)
    x_blocks = [first] + x_blocks[1:]

    saved, n2_parts, n2_others = None, [], []
    for s in range(slots):
        if s == 1:
            x_blocks, ct_turned, saved = tie(x_blocks, ct_turned, saved)
            ct_blocks = [ct_turned[0]] + [exchange(ct_turned[r], blocks_of(r)) for r in range(1, n_seq)]
        *saved, n2 = mixer_forward(ids, s, slots, x_blocks[s], weights, saved)
        n2_parts.append(n2.reshape(total_pos, width))
        n2_others.append(exchange(n2_parts[-1], across))
    flat = lambda a: a.reshape(-1, width)
    ct_parts = [flat(c) for c in ct_blocks]
    ct_parts = ct_parts + [exchange(c, across) for c in ct_parts]
    p_all, spec, conv, gated, normed, x_whole, residual = saved
    n2_parts = n2_parts + n2_others

    pieces, chunks, sums = [], [], None
    chip_steps, seq_steps, cuts = (next_chip, far_chip), (first_side, second_side), ("rows", "lanes", "lanes", "done")
    for k in range(CHUNKS):
        *parts, _, _ = out = glu_chunk(ids, k, n2_parts, ct_parts, glu_weight, down_weight, sums, n_seq)
        parts, sums = out[:4], out[4:]
        chunks.append(parts)
        if paired:
            pieces.append(Piece(*parts[:2], zip(seq_steps + chip_steps, cuts), alone=k == 0))
            pieces.append(Piece(*parts[2:], zip(chip_steps + seq_steps, cuts), alone=k == 0))
        if 0 < k < CHUNKS - 1:
            sums = boundary(ids, pieces, sums)
    ff_pieces = list(pieces)
    n2g_own, n2g_sent, out_own, out_sent = sums
    n2g_other = exchange(n2g_sent, across)
    n2g_own = boundary(ids, pieces, n2g_own)
    n2g_own, out_sent = tie(n2g_own, out_sent)
    out_other = exchange(out_sent, across)
    residual_grad, conv_grad, pg_gate, small_out, a_keep, a_send = back_out(
        ids, n2g_own, n2g_other, residual, ct_blocks, gated, conv, p_all, normed, out_weight, short_taps, gain2
    )
    out_other, conv_grad = tie(out_other, conv_grad)
    stay, later, sent = combine(ids, out_own, out_other, residual)
    moved = Piece(flat(later), flat(sent), [(first_side, "relay"), (second_side, "land")])
    pieces.append(moved)
    conv_grad, pg_gate = boundary(ids, pieces, (conv_grad, pg_gate))
    sum_steps = [(across, "rows"), (first_side, "rows"), (second_side, "done")]
    a = Piece(flat(a_keep), flat(a_send), sum_steps, alone=True)
    if paired:
        pieces.append(a)
    pg_rest, small_conv, b_keep, b_send = back_conv(ids, conv_grad, spec, p_all, normed, table, short_taps)
    pg_rest, pg_gate = boundary(ids, pieces, (pg_rest, pg_gate))
    b = Piece(flat(b_keep), flat(b_send), sum_steps, alone=True)
    if paired:
        pieces.append(b)
    gain_in, *x_sent = back_in(ids, pg_gate, pg_rest, x_whole, residual_grad, in_weight, gain1)
    x_sent = boundary(ids, pieces, x_sent)
    x_got = [x_sent[0]] + [exchange(x_sent[r], blocks_of(r)) for r in range(1, n_seq)]
    output = unturn(ids, [stay] + [ref for ref, _ in moved.got], LOW, tuple(at for _, at in moved.got))
    small = jnp.concatenate([gain_in, small_out, small_conv], axis=0)
    n_small = small.shape[0] + -small.shape[0] % 16
    if paired:
        small = jnp.pad(small, ((0, n_small - small.shape[0]), (0, 0))).astype(LOW)
        small = Piece(small, small, [(first_side, "all"), (second_side, "all")], alone=True)
        pieces.append(small)
        boundary(ids, pieces, ())
        own, *sent = by_chip(ids, a, b, small)
        got = [exchange(x, lambda s, b, rel=rel: (s, b ^ (2 * rel))) for rel, x in enumerate(sent, 1)]
        own, sent = cut_cores(
            ids, (own, *got), [p.keep for p in ff_pieces[0::2]], [p.keep for p in ff_pieces[1::2]], n_batch, n_small
        )
        total_in, total_out, total_static, small, total_glu, total_down = finish(
            ids, own, exchange(sent, across), width, total_pos, n_batch, n_small
        )
    else:
        pieces = [a, b]
        while a.steps:
            boundary(ids, pieces, ())
        top = width // 8
        in_rows = jnp.concatenate([a.keep[top:], b.keep[:top], b.keep[top : 2 * top]], axis=1)
        total_in = spread_sum(in_rows, core, 0, 0)
        total_out = spread_sum(a.keep[:top], core, 0, 0)
        total_static = spread_sum(b.keep[2 * top :], core, 0, 0)
        side = n_seq // 2
        halves = lambda x: x.reshape(2, x.shape[0] // 2, x.shape[1])
        glu = jnp.stack(
            [seq_sums(halves(c[0]), halves(c[1])).reshape(-1, side, 2, side, LANES) for c in chunks], axis=4
        )
        glu = glu.transpose(0, 2, 1, 3, 4, 5).reshape(-1, 2 * n_seq, 1, CHUNKS * LANES)
        mine = (jnp.arange(2) == core)[:, None]
        glu = jnp.where(mine, glu, 0).astype(F32).reshape(glu.shape[0], -1)
        total_glu = lax.psum_scatter(glu, "batch", scatter_dimension=1, tiled=True)
        joined = [jnp.concatenate([c[2], c[3]], axis=int(c[2].shape[0] == width)) for c in chunks]
        down = jnp.stack([d.reshape(width, n_seq, LANES) for d in joined], axis=2)
        down = down.reshape(width, n_seq, 1, CHUNKS * LANES)
        down = jnp.where(mine, down, 0).astype(F32).reshape(width, -1)
        down = lax.psum_scatter(down, "batch", scatter_dimension=0, tiled=True)
        total_down = lax.psum_scatter(down, "seq", scatter_dimension=1, tiled=True).T

        small = lax.psum(small, ("seq", "batch"))
    total_taps = jnp.concatenate([small[1:4], small[5:8], small[8:11]], axis=1)
    input_grad = unturn(ids, x_got, F32)
    return (
        output,
        input_grad,
        small[0],
        total_in,
        total_taps,
        total_static,
        total_out,
        small[4],
        total_glu,
        total_down,
    )


def solution(mesh):
    return jax.shard_map(
        on_device,
        mesh=mesh,
        in_specs=(
            P("seq", "batch", None),
            P("batch"),
            P(),
            P(),
            P(),
            P(),
            P(),
            P(),
            P(),
            P(),
            P("seq", "batch", None),
        ),
        out_specs=(
            P("seq", "batch", None),
            P("seq", "batch", None),
            P(),
            P("seq", "batch"),
            P(),
            P("seq", "batch"),
            P("seq", "batch"),
            P(),
            P("seq", "batch"),
            P("seq", "batch"),
        ),
        check_vma=False,
    )
```

```python
import functools
import math

import jax
import jax.numpy as jnp
import numpy as np
from jax import lax
from jax.experimental import pallas as pl
from jax.experimental.pallas import tpu as pltpu
from jax.sharding import PartitionSpec as P

F32 = jnp.float32
LOW = jnp.bfloat16
CHUNKS = 3
LANES = 128
ROOT = math.sqrt(2.0 / math.pi)
CUBE = 0.044715
MIB = 2**20
COST = 1000
LONG = 3 * 10**10
GLU_MIB = 50
MIX_MIB = 44
BACK_MIB = 46
ANY = pl.BlockSpec(memory_space=pl.ANY)

SEQ, CORE, PLACE, LENGTH, ROW_AT, CHIP_AT, COL_AT = 0, 1, 2, 3, 5, 9, 13


def half_tables(count):
    steps = np.arange(count)
    angle = (np.arange(count // 2)[:, None] * steps[None, :] % count) * (2.0 * math.pi / count)
    low_rows = np.cos(angle)
    high_rows = -np.sin(angle)
    high_rows[0] = np.where(steps % 2 == 0, 1.0, -1.0)
    table = np.concatenate([low_rows, high_rows], axis=0)
    weight = np.where(steps % (count // 2) == 0, 1.0, 2.0) / count
    return table.astype(LOW), (table * weight[:, None]).T.astype(LOW)


def dot(a, b, ca=1, cb=0):
    return lax.dot_general(a, b, (((ca,), (cb,)), ((), ())), preferred_element_type=F32)


def gelu_parts(z):
    square = z * z
    tanh = jnp.tanh(z * (ROOT + (ROOT * CUBE) * square))
    plus = 0.5 + 0.5 * tanh
    act = z * plus
    return act, plus + act * (1.0 - tanh) * (ROOT + (3.0 * ROOT * CUBE) * square)


def gelu(z):
    return z * (0.5 + 0.5 * jnp.tanh(z * (ROOT + (ROOT * CUBE) * (z * z))))


def standardize(values):
    centred = values - jnp.mean(values, axis=-1, keepdims=True)
    inverse = lax.rsqrt(jnp.mean(centred * centred, axis=-1, keepdims=True) + 1e-05)
    return centred * inverse, inverse


def norm_back(grad_in, standard, inverse, gain_vec):
    scaled = grad_in * gain_vec
    inner = (
        scaled
        - jnp.mean(scaled, axis=-1, keepdims=True)
        - standard * jnp.mean(scaled * standard, axis=-1, keepdims=True)
    )
    return inverse * inner


def shifts(a):
    count = a.shape[0]
    row = lax.broadcasted_iota(jnp.int32, a.shape, 0)
    before = jnp.where(row == 0, 0.0, pltpu.roll(a, 1, 0))
    after = jnp.where(row == count - 1, 0.0, pltpu.roll(a, count - 1, 0))
    return before, after


def mix(low, taps):
    wide = low.astype(F32)
    before, after = shifts(wide)
    return taps[0:1] * before + taps[1:2] * wide + taps[2:3] * after


def mix_back(grad, low, taps):
    wide = low.astype(F32)
    before, after = shifts(grad)
    sums = [jnp.sum(side * wide, axis=0, keepdims=True) for side in (after, grad, before)]
    return sums, (taps[0:1] * after + taps[1:2] * grad + taps[2:3] * before).astype(LOW)


def spectrum_product(a, b, sign):
    half = a.shape[0] // 2
    ar, ai, br, bi = a[:half], a[half:], b[:half], b[half:]
    first = lax.broadcasted_iota(jnp.int32, ar.shape, 0) == 0
    both = ai * bi
    re = ar * br - jnp.where(first, 0.0, sign * both)
    im = jnp.where(first, both, ai * br + sign * (ar * bi))
    return jnp.concatenate([re.astype(LOW), im.astype(LOW)], axis=0)


def live_mask(length, count):
    return (lax.broadcasted_iota(jnp.int32, (count, 1), 0) < length).astype(F32)


def whole(shape):
    return pl.BlockSpec(shape, lambda *at: (0,) * len(shape))


def kept(shape):
    return pl.BlockSpec(shape, lambda *at: (0,) * len(shape), pipeline_mode=pl.Buffered(1))


def in_hbm(arrays):
    return [pltpu.with_memory_space_constraint(a, pltpu.HBM) for a in arrays]


def sds(shape, dtype=LOW):
    return jax.ShapeDtypeStruct(shape, dtype)


def call(body, grid, ids, in_specs, out_specs, out_shape, args, scratch=(), aliases=None, mib=12, cost=COST):
    return pl.pallas_call(
        body,
        grid_spec=pltpu.PrefetchScalarGridSpec(
            num_scalar_prefetch=1, grid=grid, in_specs=in_specs, out_specs=out_specs, scratch_shapes=list(scratch)
        ),
        out_shape=out_shape,
        compiler_params=pltpu.CompilerParams(vmem_limit_bytes=mib * MIB),
        input_output_aliases=aliases or {},
        cost_estimate=pl.CostEstimate(flops=cost, bytes_accessed=COST, transcendentals=0),
    )(ids, *args)


def turn_kernel(by_slot, ids, x_ref, *refs):
    outs, held = refs[:-1], refs[-1]
    held[...] = jnp.swapaxes(x_ref[...].astype(F32), 0, 1).astype(LOW)
    n_seq = 4
    own = held.shape[0] // n_seq
    for r in range(n_seq):
        at = (ids[SEQ] ^ r) * own
        for s in range(own):
            if by_slot:
                outs[s * n_seq + r][...] = held[at + s]
            else:
                outs[r][s] = held[at + s]


def turn(ids, x, by_slot):
    span, slots, width = x.shape
    own = slots // 4
    shape = (span, width) if by_slot else (own, span, width)
    n_out = slots if by_slot else 4
    return call(
        functools.partial(turn_kernel, by_slot), (1,), ids, [whole(x.shape)], [whole(shape)] * n_out,
        [sds(shape)] * n_out, (x,), [pltpu.VMEM((slots, span, width), LOW)], mib=20,
    )


def unturn_kernel(places, ids, *refs):
    blocks, out, held = refs[:-2], refs[-2], refs[-1]
    slots, span, width = held.shape
    own = slots // 4
    rels = range(4) if places is None else (0, 1 + ids[CORE], 2 - ids[CORE], 3)
    for i, (rel, block) in enumerate(zip(rels, blocks)):
        for s in range(own):
            to = (ids[SEQ] ^ rel) * own + s
            if places is None or i == 0:
                held[to] = block[s].astype(F32)
            else:
                for c in range(width // LANES):
                    row = places[i - 1] + (c * own + s) * span
                    held[to, :, c * LANES : (c + 1) * LANES] = block[row : row + span].astype(F32)
    out[...] = jnp.swapaxes(held[...], 0, 1).astype(out.dtype)


def unturn(ids, blocks, dtype, places=None):
    own, span, width = blocks[0].shape
    slots = own * 4
    return call(
        functools.partial(unturn_kernel, places),
        (1,),
        ids,
        [whole(b.shape) for b in blocks],
        whole((span, slots, width)),
        sds((span, slots, width), dtype),
        blocks,
        [pltpu.VMEM((slots, span, width), F32)],
        mib=32,
    )


class Copies:
    def __init__(self, sems):
        self.sems, self.made = sems, []

    def start(self, src, to):
        copy = pltpu.make_async_copy(src, to, self.sems.at[len(self.made)])
        copy.start()
        self.made.append(copy)
        return copy

    def finish(self):
        for copy in self.made:
            copy.wait()


def mixer_kernel(
    slot, ids, x0, x1, x2, x3, in_weight, static, table, inverse, w_out, taps, gain1, gain2, *refs
):
    p_hbm, spec_hbm, conv_hbm, gated_hbm, normed_hbm, x_hbm, residual_hbm, n2_hbm = refs[-22:-14]
    (x, w_in, static_low, tab, inv, w_o, p, spec, conv, gated, normed, total, sems_in, sems_out) = refs[-14:]
    blocks = (x0, x1, x2, x3)
    count, width = x.shape
    span = count // len(blocks)
    scale = count**-0.5
    loads, stores = Copies(sems_in), Copies(sems_out)
    place = [pl.ds(pl.multiple_of((ids[SEQ] ^ r) * span, span), span) for r in range(len(blocks))]
    x_copies = [loads.start(block, x.at[place[r]]) for r, block in enumerate(blocks)]
    w_copy, *t_copies = [
        loads.start(src, to)
        for src, to in ((in_weight, w_in), (table, tab), (static, static_low), (inverse, inv), (w_out, w_o))
    ]
    for copy in x_copies:
        copy.wait()
    stores.start(x, x_hbm.at[slot])
    for q in range(len(blocks)):
        rows = slice(q * span, (q + 1) * span)
        wide = x[rows].astype(F32)
        standard, _ = standardize(wide)
        normed[rows] = (standard * gain1[...]).astype(LOW)
        total[rows] = wide
    stores.start(normed, normed_hbm.at[slot])
    live = live_mask(ids[LENGTH + slot], count)
    w_copy.wait()
    p[...] = dot(normed[...], w_in[...]).astype(LOW)
    stores.start(p, p_hbm.at[slot])
    for copy in t_copies:
        copy.wait()
    static_spec = dot(tab[...], static_low[...].astype(LOW))
    value = (live * mix(p[:, width : 2 * width], taps[:, width : 2 * width])).astype(LOW)
    vs = dot(tab[...], value)
    cond = (live * gelu(mix(p[:, 2 * width :], taps[:, 2 * width :]))).astype(LOW)
    ks = static_spec + scale * dot(tab[...], cond)
    spec[:, :width], spec[:, width:] = vs.astype(LOW), ks.astype(LOW)
    stores.start(spec, spec_hbm.at[slot])
    conv[...] = dot(inv[...], spectrum_product(vs, ks, 1.0)).astype(LOW)
    stores.start(conv, conv_hbm.at[slot])
    gated[...] = (live * mix(p[:, :width], taps[:, :width]) * conv[...].astype(F32)).astype(LOW)
    stores.start(gated, gated_hbm.at[slot])
    total[...] += dot(gated[...], w_o[...])
    for r in range(len(blocks)):
        stores.start(total.at[place[r]], residual_hbm.at[slot, r])
    n2 = x
    stores.made[0].wait()
    for q in range(len(blocks)):
        rows = slice(q * span, (q + 1) * span)
        standard, _ = standardize(total[rows])
        n2[rows] = (standard * gain2[...]).astype(LOW)
    for r in range(len(blocks)):
        stores.start(n2.at[place[r]], n2_hbm.at[r])
    for copy in stores.made[1:]:
        copy.wait()


def mixer_forward(ids, slot, slots, x_blocks, weights, before):
    span, width = x_blocks[0].shape
    count = span * len(x_blocks)
    cols = (3, 2, 1, 1, 1, 1)
    rel = (len(x_blocks), span, width)
    *large, taps, gain1, gain2 = weights
    args = (*x_blocks, *in_hbm(large), taps, gain1, gain2)
    in_specs = [ANY] * (len(x_blocks) + len(large)) + [kept(a.shape) for a in (taps, gain1, gain2)]
    aliases = {}
    if before is not None:
        aliases = {1 + len(args) + i: i for i in range(len(before))}
        args, in_specs = args + tuple(before), in_specs + [ANY] * len(before)
    return call(
        functools.partial(mixer_kernel, slot),
        (1,),
        ids,
        in_specs,
        [ANY] * 8,
        [pltpu.HBM((slots, count, m * width), LOW) for m in cols] + [pltpu.HBM((slots, *rel), F32), sds(rel)],
        args,
        [
            pltpu.VMEM((count, width), LOW),
            pltpu.VMEM((width, 3 * width), LOW),
            pltpu.VMEM((count, width), F32),
            pltpu.VMEM((count, count), LOW),
            pltpu.VMEM((count, count), LOW),
            pltpu.VMEM((width, width), LOW),
            pltpu.VMEM((count, 3 * width), LOW),
            pltpu.VMEM((count, 2 * width), LOW),
            pltpu.VMEM((count, width), LOW),
            pltpu.VMEM((count, width), LOW),
            pltpu.VMEM((count, width), LOW),
            pltpu.VMEM((count, width), F32),
            pltpu.SemaphoreType.DMA((9,)),
            pltpu.SemaphoreType.DMA((14,)),
        ],
        aliases,
        mib=MIX_MIB,
        cost=LONG,
    )


def glu_kernel(k, n_seq, slots, ids, *refs):
    n_blocks = 4
    n2_parts, ct_parts = refs[: 2 * slots], refs[2 * slots : 2 * slots + 2 * n_blocks]
    glu_hbm, down_hbm = refs[2 * (slots + n_blocks) :][:2]
    (
        glu_keep, glu_send, down_keep, down_send, gu_hbm, hidden_hbm, w_glu_hbm, w_down_hbm,
        n2, ct, w_glu, w_down, hidden, gu, g_low, d_low, n2_sems, ct_sems, w_sems, out_sems,
    ) = refs[-20:]
    rows = n2.shape[0] // 2
    span = rows // n_blocks // slots
    units = w_down.shape[0]
    halves = [pl.ds(h * rows, rows) for h in range(2)]

    def load(h):
        copies = []
        for s in range(slots):
            for r in range(n_blocks):
                copies.append(
                    pltpu.make_async_copy(
                        n2_parts[h * slots + s].at[pl.ds(r * span, span)],
                        n2.at[pl.ds(h * rows + (r * slots + s) * span, span)],
                        n2_sems.at[(h * slots + s) * n_blocks + r],
                    )
                )
        return copies, [
            pltpu.make_async_copy(
                ct_parts[h * n_blocks + r],
                ct.at[pl.ds(h * rows + r * slots * span, slots * span)],
                ct_sems.at[h * n_blocks + r],
            )
            for r in range(n_blocks)
        ]

    loads = [load(h) for h in range(2)]
    gate_copies, down_copies = [], []
    for m in range(2 * n_seq):
        col = pl.multiple_of(((2 * m + ids[CORE]) * CHUNKS + k) * LANES, LANES)
        gate_copies.append(
            pltpu.make_async_copy(
                glu_hbm.at[:, pl.ds(col, LANES)], w_glu.at[:, pl.ds(m * LANES, LANES)], w_sems.at[m]
            )
        )
    for m in range(n_seq):
        row = pl.multiple_of(((2 * m + ids[CORE]) * CHUNKS + k) * LANES, LANES)
        down_copies.append(
            pltpu.make_async_copy(
                down_hbm.at[pl.ds(row, LANES)], w_down.at[pl.ds(m * LANES, LANES)], w_sems.at[2 * n_seq + m]
            )
        )
    for copy in loads[0][0] + gate_copies + down_copies + loads[0][1] + loads[1][0] + loads[1][1]:
        copy.start()
    outs = []

    def store(src, to):
        copy = pltpu.make_async_copy(src, to, out_sems.at[len(outs)])
        copy.start()
        outs.append(copy)

    for copy in loads[0][0] + gate_copies:
        copy.wait()
    gate_ups = [dot(n2[halves[0]], w_glu[...])]
    for copy in down_copies + loads[0][1] + loads[1][0] + loads[1][1]:
        copy.wait()
    gate_ups.append(dot(n2[halves[1]], w_glu[...]))
    for h, gate_up in enumerate(gate_ups):
        here = halves[h]
        gate, up = gate_up[:, :units], gate_up[:, units:]
        hidden_grad = dot(ct[here], w_down[...], 1, 1)
        act, slope = gelu_parts(gate)
        hidden[here] = (act * up).astype(LOW)
        gu[here, :units] = (hidden_grad * up * slope).astype(LOW)
        gu[here, units:] = (hidden_grad * act).astype(LOW)
    mine, wide = pl.ds(k * units, units), pl.ds(2 * k * units, 2 * units)
    store(w_glu, w_glu_hbm.at[:, wide])
    store(w_down, w_down_hbm.at[mine])
    store(hidden, hidden_hbm.at[:, mine])
    store(gu, gu_hbm.at[:, wide])
    g_sum = dot(n2[...], gu[...], 0, 0)
    side = units // 2
    size = g_sum.shape[0] // 4
    for q in range(4):
        here = pl.ds(pl.multiple_of(ids[ROW_AT + q] * size, size), size)
        for high in range(2):
            for g in range(2):
                at = (high ^ (ids[PLACE] % 2)) * 2 + (g ^ (ids[PLACE] // 2 % 2))
                from_col = g * units + high * side
                part = g_sum[q * size : (q + 1) * size, from_col : from_col + side]
                g_low[here, pl.ds(pl.multiple_of(at * side, side), side)] = part.astype(LOW)
    half = d_low.shape[0] // 2
    store(g_low.at[pl.ds(half, half)], glu_send)
    store(g_low.at[pl.ds(0, half)], glu_keep)
    d_sum = dot(ct[...], hidden[...], 0, 0)
    for q in range(4):
        here = pl.ds(pl.multiple_of(ids[CHIP_AT + q] * size, size), size)
        for s in range(4):
            part = d_sum[q * size : (q + 1) * size, s * LANES : (s + 1) * LANES]
            d_low[here, pl.ds(pl.multiple_of(ids[COL_AT + s] * LANES, LANES), LANES)] = part.astype(LOW)
    store(d_low.at[pl.ds(half, half)], down_send)
    store(d_low.at[pl.ds(0, half)], down_keep)
    for copy in outs:
        copy.wait()


def glu_chunk(ids, k, n2_parts, ct_parts, glu_weight, down_weight, shared, n_seq):
    width, units = glu_weight.shape[0], n_seq * LANES
    slots, n_blocks = len(n2_parts) // 2, 4
    tokens = sum(p.shape[0] for p in n2_parts)
    args = (*n2_parts, *ct_parts, *in_hbm((glu_weight, down_weight)), *shared)
    aliases = {1 + len(args) - len(shared) + i: 4 + i for i in range(len(shared))}
    return call(
        functools.partial(glu_kernel, k, n_seq, slots),
        (1,),
        ids,
        [ANY] * len(args),
        [ANY] * 8,
        [pltpu.VMEM((width // 2, 2 * units), LOW)] * 2
        + [pltpu.VMEM((width // 2, units), LOW)] * 2
        + [
            pltpu.HBM(x, LOW)
            for x in (
                (tokens, 2 * CHUNKS * units),
                (tokens, CHUNKS * units),
                (width, 2 * CHUNKS * units),
                (CHUNKS * units, width),
            )
        ],
        args,
        [
            pltpu.VMEM((tokens, width), LOW),
            pltpu.VMEM((tokens, width), LOW),
            pltpu.VMEM((width, 2 * units), LOW),
            pltpu.VMEM((units, width), LOW),
            pltpu.VMEM((tokens, units), LOW),
            pltpu.VMEM((tokens, 2 * units), LOW),
            pltpu.VMEM((width, 2 * units), LOW),
            pltpu.VMEM((width, units), LOW),
            pltpu.SemaphoreType.DMA((2 * slots * n_blocks,)),
            pltpu.SemaphoreType.DMA((2 * n_blocks,)),
            pltpu.SemaphoreType.DMA((3 * n_seq,)),
            pltpu.SemaphoreType.DMA((8,)),
        ],
        aliases,
        mib=GLU_MIB,
        cost=LONG,
    )


def halves_product_kernel(cb, ids, rows_ref, weight, own, other):
    result = dot(rows_ref[...], weight[...], 1, cb)

    @pl.when(pl.program_id(0) < pl.num_programs(0) // 2)
    def _():
        other[...] = result.astype(LOW)

    @pl.when(pl.program_id(0) >= pl.num_programs(0) // 2)
    def _():
        own[...] = result


def halves_product(ids, values, weight, cb, rows=512):
    tokens, size = values.shape
    width = weight.shape[1 - cb]
    per = tokens // 2 // rows
    return call(
        functools.partial(halves_product_kernel, cb),
        (2 * per,),
        ids,
        [pl.BlockSpec((rows, size), lambda i, ids: ((i + per) % (2 * per), 0)), kept(weight.shape)],
        [
            pl.BlockSpec((rows, width), lambda i, ids: (jnp.maximum(i - per, 0), 0)),
            pl.BlockSpec((rows, width), lambda i, ids: (jnp.minimum(i, per - 1), 0)),
        ],
        [sds((tokens // 2, width), F32), sds((tokens // 2, width))],
        in_hbm((values, weight)),
        mib=32,
        cost=LONG,
    )


def combine_kernel(ids, own, other, residual, stay, later, send):
    span = stay.shape[1]
    second, first = 2 - ids[CORE], 1 + ids[CORE]
    for r, out, at in ((0, stay, 0), (second, later, 0), (first, send, 0), (3, send, 1)):
        value = (residual[0, r] + (own[r, 0] + other[r, 0].astype(F32))).astype(LOW)
        if out is send:
            send[at, 0] = value
        else:
            out[0] = value


def combine(ids, own, other, residual):
    slots, n_blocks, span, width = residual.shape
    rows = pl.BlockSpec((n_blocks, 1, span, width), lambda s, ids: (0, s, 0, 0))
    block = pl.BlockSpec((1, span, width), lambda s, ids: (s, 0, 0))
    own, other = [x.reshape(n_blocks, slots, span, width) for x in (own, other)]
    return call(
        combine_kernel,
        (slots,),
        ids,
        [rows, rows, pl.BlockSpec((1, n_blocks, span, width), lambda s, ids: (s, 0, 0, 0))],
        [block, block, pl.BlockSpec((2, 1, span, width), lambda s, ids: (0, s, 0, 0))],
        [sds((slots, span, width))] * 2 + [sds((2, slots, span, width))],
        (own, other, residual),
        mib=16,
    )


def place_halves(ids, grad, at, keep, send):
    size = grad.shape[0] // 8
    for q in range(4):
        to = ids[ROW_AT + q]
        for c in range(2):
            rows = grad[(2 * q + c) * size : (2 * q + c + 1) * size]

            @pl.when(ids[CORE] == c)
            def _(rows=rows, to=to):
                keep[to, at : at + size] = rows

            @pl.when(ids[CORE] != c)
            def _(rows=rows, to=(to % 2) * 2 + to // 2):
                send[to, at : at + size] = rows


def accumulate(step, ref, value):
    @pl.when(step == 0)
    def _():
        ref[...] = value

    @pl.when(step > 0)
    def _():
        ref[...] += value


def back_out_kernel(
    ids, n2g_own_hbm, n2g_other_hbm, residual_hbm, ct0, ct1, ct2, ct3, gated_hbm, conv_hbm, p_hbm, normed_hbm, w_hbm,
    taps, gain2, residual_grad_hbm, conv_grad_hbm, pg_hbm, small, keep, send,
    n2g_own, n2g_other, residual, cot, gated, conv, p, normed, w_out, branch, conv_grad, pg, sems_in, sems_out,
):
    slots, n_blocks, span, width = residual.shape
    count = n_blocks * span
    loads, stores = Copies(sems_in), Copies(sems_out)
    early, late = [], []
    for s in range(slots):
        here = pl.ds(s * count, count)
        early.append(
            [loads.start(residual_hbm.at[s], residual.at[s])]
            + [loads.start(ref.at[s], cot.at[s, r]) for r, ref in enumerate((ct0, ct1, ct2, ct3))]
            + [loads.start(n2g_own_hbm.at[:, s], n2g_own.at[s]), loads.start(n2g_other_hbm.at[:, s], n2g_other.at[s])]
        )
        late.append(
            ([loads.start(w_hbm, w_out)] if s == 0 else [])
            + [loads.start(p_hbm.at[s, :, pl.ds(0, width)], p.at[here]), loads.start(conv_hbm.at[s], conv.at[here])]
        )
    last = [
        loads.start(ref.at[s], to.at[pl.ds(s * count, count)])
        for s in range(slots)
        for ref, to in ((gated_hbm, gated), (normed_hbm, normed))
    ]
    gain_grad, tap_sums = jnp.zeros((1, width), F32), None
    for s in range(slots):
        here = slice(s * count, (s + 1) * count)
        for copy in early[s]:
            copy.wait()
        for r in range(n_blocks):
            at = pl.multiple_of(s * count + (ids[SEQ] ^ r) * span, span)
            grad = n2g_own[s, r] + n2g_other[s, r].astype(F32)
            unit, inverse = standardize(residual[s, r])
            gain_grad += jnp.sum(grad * unit, axis=0, keepdims=True)
            value = cot[s, r].astype(F32) + norm_back(grad, unit, inverse, gain2[...])
            residual[s, r] = value
            branch[pl.ds(at, span), :] = value.astype(LOW)
        stores.start(residual.at[s], residual_grad_hbm.at[s])
        live = live_mask(ids[LENGTH + s], count)
        for copy in late[s]:
            copy.wait()
        gated_grad = live * dot(branch[here], w_out[...], 1, 1)
        conv_grad[here] = (gated_grad * mix(p[here], taps[...])).astype(LOW)
        sums, pg[here] = mix_back(gated_grad * conv[here].astype(F32), p[here], taps[...])
        tap_sums = sums if s == 0 else [x + y for x, y in zip(tap_sums, sums)]
        stores.start(conv_grad.at[pl.ds(s * count, count)], conv_grad_hbm.at[s])
        stores.start(pg.at[pl.ds(s * count, count)], pg_hbm.at[s])
    small[...] = jnp.concatenate(tap_sums + [gain_grad], axis=0)
    for copy in last:
        copy.wait()
    place_halves(ids, dot(gated[...], branch[...], 0, 0).astype(LOW), 0, keep, send)
    place_halves(ids, dot(normed[...], pg[...], 0, 0).astype(LOW), width // 8, keep, send)
    stores.finish()


def back_out(ids, n2g_own, n2g_other, residual, cot, gated, conv, p_all, normed, w_out, taps, gain2):
    slots, n_blocks, span, width = residual.shape
    count = n_blocks * span
    n2g_own, n2g_other = [x.reshape(n_blocks, slots, span, width) for x in (n2g_own, n2g_other)]
    part = (4, 2 * width // 8, width)
    args = (n2g_own, n2g_other, *in_hbm([residual]), *cot, *in_hbm((gated, conv, p_all, normed, w_out)))
    n_loads = slots * (1 + n_blocks + 2 + 2 + 2) + 1
    flat = (slots * count, width)
    return call(
        back_out_kernel,
        (1,),
        ids,
        [ANY] * len(args) + [kept((3, width)), kept((1, width))],
        [ANY] * 3 + [whole((4, width))] + [pl.BlockSpec(memory_space=pltpu.VMEM)] * 2,
        [
            pltpu.HBM(residual.shape, F32),
            pltpu.HBM((slots, count, width), LOW),
            pltpu.HBM((slots, count, width), LOW),
            sds((4, width), F32),
            pltpu.VMEM(part, LOW),
            pltpu.VMEM(part, LOW),
        ],
        (*args, taps, gain2),
        [
            pltpu.VMEM(residual.shape, F32),
            pltpu.VMEM(residual.shape, LOW),
            pltpu.VMEM(residual.shape, F32),
            pltpu.VMEM(residual.shape, LOW),
            *[pltpu.VMEM(flat, LOW)] * 4,
            pltpu.VMEM((width, width), LOW),
            *[pltpu.VMEM(flat, LOW)] * 3,
            pltpu.SemaphoreType.DMA((n_loads,)),
            pltpu.SemaphoreType.DMA((3 * slots,)),
        ],
        mib=BACK_MIB,
        cost=LONG,
    )


def back_conv_kernel(
    ids, conv_grad_hbm, spec_hbm, p_hbm, normed_hbm, table_hbm, inverse_hbm, t_value, t_cond,
    pg_hbm, small, keep, send,
    conv_grad, spec, p, normed, table, inverse, pg, sems_in, sems_out,
):
    width = t_value.shape[1]
    count = table.shape[0]
    slots = conv_grad.shape[0] // count
    scale = count**-0.5
    loads, stores = Copies(sems_in), Copies(sems_out)
    here_of = lambda s: pl.ds(s * count, count)
    first = [loads.start(table_hbm, table)]
    parts = []
    for s in range(slots):
        parts.append([loads.start(conv_grad_hbm.at[s], conv_grad.at[here_of(s)])])
        parts.append([loads.start(spec_hbm.at[s], spec.at[here_of(s)])])
        if s == 0:
            parts[-1].append(loads.start(inverse_hbm, inverse))
        parts.append([loads.start(p_hbm.at[s, :, pl.ds(width, 2 * width)], p.at[here_of(s)])])
    last = [loads.start(normed_hbm.at[s], normed.at[here_of(s)]) for s in range(slots)]
    tap_sums = static_total = None
    for s in range(slots):
        here = slice(s * count, (s + 1) * count)
        live = live_mask(ids[LENGTH + s], count)
        for copy in (first if s == 0 else []) + parts[3 * s]:
            copy.wait()
        gs = dot(table[...], conv_grad[here])
        for copy in parts[3 * s + 1]:
            copy.wait()
        value_low = spectrum_product(gs, spec[here, width:].astype(F32), -1.0)
        cond_low = spectrum_product(gs, spec[here, :width].astype(F32), -1.0)
        value_grad = live * dot(inverse[...], value_low)
        back = dot(inverse[...], cond_low)
        static_total = back if s == 0 else static_total + back
        for copy in parts[3 * s + 2]:
            copy.wait()
        sums_v, pg[here, :width] = mix_back(value_grad, p[here, :width], t_value[...])
        cond_grad = (live * scale) * back * gelu_parts(mix(p[here, width:], t_cond[...]))[1]
        sums_c, pg[here, width:] = mix_back(cond_grad, p[here, width:], t_cond[...])
        sums = sums_v + sums_c
        tap_sums = sums if s == 0 else [x + y for x, y in zip(tap_sums, sums)]
        stores.start(pg.at[here_of(s)], pg_hbm.at[s])
    small[...] = jnp.concatenate(tap_sums, axis=0)
    place_halves(ids, static_total.astype(LOW), width // 4, keep, send)
    for copy in last:
        copy.wait()
    total = dot(normed[...], pg[...], 0, 0).astype(LOW)
    place_halves(ids, total[:, :width], 0, keep, send)
    place_halves(ids, total[:, width:], width // 8, keep, send)
    stores.finish()


def back_conv(ids, conv_grad, spec, p_all, normed, tables, taps):
    slots, count, width = conv_grad.shape
    tap = lambda m: pl.BlockSpec((3, width), lambda i, ids, m=m: (0, m))
    part = (4, (2 * width + count) // 8, width)
    args = in_hbm((conv_grad, spec, p_all, normed, *tables))
    rows = slots * count
    return call(
        back_conv_kernel,
        (1,),
        ids,
        [ANY] * len(args) + [tap(1), tap(2)],
        [ANY, whole((6, width))] + [pl.BlockSpec(memory_space=pltpu.VMEM)] * 2,
        [
            pltpu.HBM((slots, count, 2 * width), LOW),
            sds((6, width), F32),
            pltpu.VMEM(part, LOW),
            pltpu.VMEM(part, LOW),
        ],
        (*args, taps, taps),
        [
            pltpu.VMEM((rows, width), LOW),
            pltpu.VMEM((rows, 2 * width), LOW),
            pltpu.VMEM((rows, 2 * width), LOW),
            pltpu.VMEM((rows, width), LOW),
            pltpu.VMEM((count, count), LOW),
            pltpu.VMEM((count, count), LOW),
            pltpu.VMEM((rows, 2 * width), LOW),
            pltpu.SemaphoreType.DMA((4 * slots + 2,)),
            pltpu.SemaphoreType.DMA((slots,)),
        ],
        mib=BACK_MIB,
        cost=LONG,
    )


def back_in_kernel(ids, pg_gate, pg_rest, x, residual_grad, in_weight, gain1, gain_ref, *refs):
    outs, total = refs[:-1], refs[-1]
    s = pl.program_id(0)
    width = x.shape[2]
    span = residual_grad.shape[2]
    total[...] = dot(pg_gate[0], in_weight[:, :width], 1, 1) + dot(pg_rest[0], in_weight[:, width:], 1, 1)
    gain_grad = jnp.zeros((1, width), F32)
    for r, out in enumerate(outs):
        at = pl.ds(pl.multiple_of((ids[SEQ] ^ r) * span, span), span)
        standard, inverse = standardize(x[0, at, :].astype(F32))
        grad = total[at, :]
        gain_grad += jnp.sum(grad * standard, axis=0, keepdims=True)
        out[0] = (residual_grad[0, r] + norm_back(grad, standard, inverse, gain1[...])).astype(LOW)
    accumulate(s, gain_ref, gain_grad)


def back_in(ids, pg_gate, pg_rest, x, residual_grad, in_weight, gain1):
    slots, count, width = x.shape
    n_blocks, span = residual_grad.shape[1:3]
    seqs = lambda m: pl.BlockSpec((1, count, m * width), lambda s, ids: (s, 0, 0))
    rel = pl.BlockSpec((1, n_blocks, span, width), lambda s, ids: (s, 0, 0, 0))
    return call(
        back_in_kernel,
        (slots,),
        ids,
        [seqs(1), seqs(2), seqs(1), rel, kept(in_weight.shape), kept((1, width))],
        [whole((1, width))] + [pl.BlockSpec((1, span, width), lambda s, ids: (s, 0, 0))] * n_blocks,
        [sds((1, width), F32)] + [sds((slots, span, width))] * n_blocks,
        (pg_gate, pg_rest, x, residual_grad, in_weight, gain1),
        [pltpu.VMEM((count, width), F32)],
        mib=32,
        cost=LONG,
    )


def exchange(x, partner):
    n_seq, n_batch = lax.axis_size("seq"), lax.axis_size("batch")
    pairs = []
    for s in range(n_seq):
        for b in range(n_batch):
            to_s, to_b = partner(s, b)
            pairs.append((s * n_batch + b, to_s * n_batch + to_b))
    return lax.ppermute(x, ("seq", "batch"), pairs)


def across(s, b):
    return s, b ^ 1


def first_side(s, b):
    return s ^ (1 if b % 2 == 0 else 2), b


def second_side(s, b):
    return s ^ (2 if b % 2 == 0 else 1), b


def next_chip(s, b):
    return s, b ^ 2


def far_chip(s, b):
    return s, b ^ 4


def blocks_of(r):
    return lambda s, b: (s ^ r, b)


def tie(*groups):
    return lax.optimization_barrier(groups)


class Piece:
    def __init__(self, keep, send, steps, alone=False):
        self.keep, self.send, self.steps = keep, send, list(steps)
        self.arriving, self.place, self.got = None, 0, []
        if alone:
            self.arriving = exchange(send, self.steps[0][0])


def shape_after(shape, cut):
    rows, cols = shape
    if cut == "rows":
        return rows // 2, cols
    if cut == "lanes":
        return rows, cols // 2
    return rows, cols


def slabs(shape):
    return shape[0] * shape[1] // LANES


def put_slabs(to, at, value):
    rows = value.shape[0]
    for c in range(value.shape[1] // LANES):
        to[at + c * rows : at + (c + 1) * rows] = value[:, c * LANES : (c + 1) * LANES]


def engine_kernel(plan, n_in, *refs):
    ins, outs = refs[:n_in], refs[n_in:]
    for op, *rest in plan:
        if op == "fresh":
            src, row, (rows, cols), dst, at = rest
            put_slabs(outs[dst], at, ins[src][row : row + rows])
        elif op == "move":
            src, row, rows, dst, at = rest
            outs[dst][at : at + rows] = ins[src][row : row + rows]
        else:
            keep, src, row, (rows, cols), cut, stay, dst, at = rest
            held, arrived = ins[keep], ins[src]
            plain = arrived.shape == held.shape
            for c in range(cols // LANES):
                lanes = slice(c * LANES, (c + 1) * LANES)
                there = arrived[:, lanes] if plain else arrived[row + c * rows : row + (c + 1) * rows]
                total = (held[:, lanes].astype(F32) + there.astype(F32)).astype(LOW)
                if cut == "rows":
                    half = rows // 2
                    outs[stay][:, lanes] = total[:half]
                    outs[dst][at + c * half : at + (c + 1) * half] = total[half:]
                elif cut == "lanes" and c >= cols // LANES // 2:
                    to = at + (c - cols // LANES // 2) * rows
                    outs[dst][to : to + rows] = total
                else:
                    outs[stay][:, lanes] = total
                    if cut == "all":
                        outs[dst][at + c * rows : at + (c + 1) * rows] = total


def boundary(ids, pieces, guard):
    active = [p for p in pieces if p.steps]
    if not active:
        return guard
    arrivals = {id(p.arriving): p.arriving for p in active if p.arriving is not None}
    keys = list(arrivals)
    landed, guard = tie([arrivals[k] for k in keys], guard)
    landed = dict(zip(keys, landed))
    partners = []
    for p in active:
        upcoming = p.steps if p.arriving is None else p.steps[1:]
        if upcoming and upcoming[0][0] not in partners:
            partners.append(upcoming[0][0])
    ins, index, plan, stays, results = [], {}, [], [], []
    rows_of = dict.fromkeys(partners, 0)

    def source(x):
        if id(x) not in index:
            index[id(x)] = len(ins)
            ins.append(x)
        return index[id(x)]

    def message(partner, rows):
        at = rows_of[partner]
        rows_of[partner] += rows
        return partners.index(partner), at

    for p in active:
        partner, cut = p.steps[0]
        if p.arriving is None:
            parts = 2 if cut == "relay" else 1
            shape = (p.send.shape[0] // parts, p.send.shape[1])
            dst, at = message(partner, parts * slabs(shape))
            for i in range(parts):
                plan.append(("fresh", source(p.send), i * shape[0], shape, dst, at + i * slabs(shape)))
            results.append((p, False, None, dst, at))
            continue
        arrived, n = landed[id(p.arriving)], slabs(p.keep.shape)
        if cut == "relay":
            dst, at = message(p.steps[1][0], 2 * n)
            plan.append(("fresh", source(p.keep), 0, p.keep.shape, dst, at))
            plan.append(("move", source(arrived), p.place + n, n, dst, at + n))
            p.got.append((arrived, p.place))
            results.append((p, True, None, dst, at))
        elif cut == "land":
            p.got += [(arrived, p.place), (arrived, p.place + n)]
            results.append((p, True, None, None, None))
        else:
            after = shape_after(p.keep.shape, cut)
            dst, at = message(p.steps[1][0], slabs(after)) if cut != "done" else (None, None)
            stay = len(partners) + len(stays)
            stays.append(after)
            plan.append(("add", source(p.keep), source(arrived), p.place, p.keep.shape, cut, stay, dst, at))
            results.append((p, True, stay, dst, at))
    outs = []
    if plan:
        shapes = [(rows_of[q], LANES) for q in partners] + stays
        size = sum(x.size for x in ins) + sum(a * b for a, b in shapes)
        outs = pl.pallas_call(
            functools.partial(engine_kernel, plan, len(ins)),
            out_shape=[sds(x) for x in shapes],
            in_specs=[pl.BlockSpec(memory_space=pltpu.VMEM)] * len(ins),
            out_specs=[pl.BlockSpec(memory_space=pltpu.VMEM)] * len(shapes),
            compiler_params=pltpu.CompilerParams(vmem_limit_bytes=2 * size + 4 * MIB),
            cost_estimate=pl.CostEstimate(flops=LONG, bytes_accessed=COST, transcendentals=0),
        )(*ins)
        outs, guard = tie(outs, guard)
    sent = [exchange(outs[i], q) for i, q in enumerate(partners)]
    for p, stepped, stay, dst, at in results:
        if stepped:
            p.steps.pop(0)
        if stay is not None:
            p.keep = outs[stay]
        p.arriving, p.place = (sent[dst], at) if p.steps else (None, None)
    return guard


def wide_sum(keep, arrived, at):
    r, cols = keep.shape
    parts = [arrived[at + c * r : at + (c + 1) * r] for c in range(cols // LANES)]
    return keep[...].astype(F32) + jnp.concatenate(parts, axis=1).astype(F32)


def by_chip_kernel(places, ids, a_keep, b_keep, small_keep, arrived, *outs):
    a = a_keep[...].astype(F32)
    b, small = [wide_sum(ref, arrived, at) for ref, at in zip((b_keep, small_keep), places)]
    width = a.shape[1]
    half = a.shape[0] // 2
    n_chip = len(outs)
    rows = jnp.concatenate([a[half:], b[:half], b[half : 2 * half]], axis=1)
    size, part = 3 * width // n_chip, width // n_chip
    static = b[2 * half :]
    packed = static.shape[0] // n_chip
    count = half + packed
    for q in range(n_chip):
        top = jnp.concatenate([rows[:, q * size : (q + 1) * size], a[:half, q * part : (q + 1) * part]], axis=1)
        cols = static[:, q * part : (q + 1) * part]
        tail = jnp.concatenate([cols[m * packed : (m + 1) * packed] for m in range(n_chip)], axis=1)
        message = jnp.concatenate([top, tail], axis=0).astype(LOW)
        for rel, out in enumerate(outs):

            @pl.when(ids[PLACE] == (q ^ rel))
            def _(message=message, out=out):
                out[:count] = message

    for out in outs:
        out[count:] = small.astype(LOW)


def by_chip(ids, a, b, small):
    width = a.keep.shape[1]
    half = a.keep.shape[0] // 2
    rows = half + (b.keep.shape[0] - 2 * half) // 4 + small.keep.shape[0]
    args = (a.keep, b.keep, small.keep, b.arriving)
    return call(
        functools.partial(by_chip_kernel, (b.place, small.place)), (1,), ids, [whole(x.shape) for x in args],
        [whole((rows, width))] * 4, [sds((rows, width))] * 4, args, mib=24,
    )


def cut_cores_kernel(batches, n_small, ids, *refs):
    parts, glus, downs, own, send = refs[:4], refs[4 : 4 + CHUNKS], refs[4 + CHUNKS : 4 + 2 * CHUNKS], refs[-2], refs[-1]
    total = sum(ref[...].astype(F32) for ref in parts)
    rows, width = total.shape
    total, small = total[: rows - n_small], total[rows - n_small :]
    top = width // 8
    size, part = 3 * width // batches, width // batches
    first = ids[CORE] == 0

    def put(at, low, high):
        here = slice(at, at + low.shape[0])
        own[here, : low.shape[1]] = jnp.where(first, low, high).astype(LOW)
        send[here, : low.shape[1]] = jnp.where(first, high, low).astype(LOW)
        return at + low.shape[0]

    static = jnp.concatenate([total[top:, m * 2 * part : (m + 1) * 2 * part] for m in range(4)], axis=0)
    pair = [
        jnp.concatenate(
            [total[:top, c * size : (c + 1) * size], total[:top, 2 * size + c * part : 2 * size + (c + 1) * part]], axis=1
        )
        for c in range(2)
    ]
    at = put(0, *pair)
    glu = jnp.concatenate([g[...].astype(F32) for g in glus], axis=1)
    side = [
        jnp.concatenate([glu[:, (2 * k + c) * LANES : (2 * k + c + 1) * LANES] for k in range(CHUNKS)], axis=1)
        for c in range(2)
    ]
    at = put(at, *side)
    down = jnp.concatenate([d[...].astype(F32) for d in downs], axis=1)
    at = put(at, down[: down.shape[0] // 2], down[down.shape[0] // 2 :])
    tall = jnp.concatenate([small[:, : width // 2], small[:, width // 2 :]], axis=0)
    at = put(at, tall, tall)
    put(at, static[:, :part], static[:, part:])


def cut_cores(ids, parts, glus, downs, batches, n_small):
    rows, width = parts[0].shape
    top = width // 8
    shape = (
        top + glus[0].shape[0] + downs[0].shape[0] // 2 + 2 * n_small + 4 * (rows - n_small - top), CHUNKS * LANES
    )
    args = (*parts, *glus, *downs)
    return call(
        functools.partial(cut_cores_kernel, batches, n_small), (1,), ids, [whole(x.shape) for x in args], [whole(shape)] * 2,
        [sds(shape)] * 2, args, mib=16,
    )


def finish_kernel(n_small, ids, own, other, in_ref, out_ref, static_ref, glu_ref, down_ref, gains_ref, taps_ref):
    part, share = out_ref.shape[1], own.shape[1]
    top, half, tall = in_ref.shape[0] // 2, glu_ref.shape[0], 2 * n_small
    for ref, core in ((own, ids[CORE]), (other, 1 - ids[CORE])):
        rows = pl.ds(pl.multiple_of(core * top, 8), top)
        both = ref[:top].astype(F32)
        in_ref[rows, :] = both[:, : share - part]
        out_ref[rows, :] = both[:, share - part :]
        cols = pl.ds(pl.multiple_of(core * share, LANES), share)
        at = top
        glu_ref[:, cols] = ref[at : at + half].astype(F32)
        at += half
        down_ref[cols, :] = ref[at : at + part].astype(F32).T
        at += part + tall
        count = static_ref.shape[0] // 2
        static_ref[pl.ds(pl.multiple_of(core * count, 8), count), :] = ref[at:, :part].astype(F32)
    at = top + half + part
    tall_sum = own[at : at + tall].astype(F32) + other[at : at + tall].astype(F32)
    small = jnp.concatenate([tall_sum[: tall // 2], tall_sum[tall // 2 :]], axis=1)
    gains_ref[0:1], gains_ref[1:2] = small[0:1], small[4:5]
    width = small.shape[1]
    for m, first in enumerate((1, 5, 8)):
        taps_ref[:, m * width : (m + 1) * width] = small[first : first + 3]


def finish(ids, own, other, width, count, batches, n_small):
    part = width // batches
    rows = width // 4
    shapes = [
        (rows, 3 * part), (rows, part), (count // 4, part), (rows, 2 * own.shape[1]), (2 * own.shape[1], part),
        (2, width), (3, 3 * width),
    ]
    return call(
        functools.partial(finish_kernel, n_small), (1,), ids, [whole(own.shape)] * 2, [whole(x) for x in shapes], [sds(x, F32) for x in shapes],
        (own, other), mib=16,
    )


def add_low(a, b):
    return (a.astype(F32) + b.astype(F32)).astype(LOW)


def seq_sums(keep, send):
    part = add_low(keep, exchange(send, first_side))
    return add_low(part[0], exchange(part[1], second_side))


def spread_sum(x, core, rows, dim):
    x = x.astype(F32)
    zero = jnp.zeros_like(x)
    low, high = jnp.where(core == 0, x, zero), jnp.where(core == 0, zero, x)
    both = jnp.concatenate([low, high], axis=dim)
    return lax.psum_scatter(both, "batch", scatter_dimension=1 - rows, tiled=True)


def on_device(
    inputs,
    lengths,
    norm1_gain,
    in_weight,
    short_taps,
    static_kernel,
    out_weight,
    norm2_gain,
    glu_weight,
    down_weight,
    cotangent,
):
    span, n_slots, width = inputs.shape
    n_seq, n_batch = lax.axis_size("seq"), lax.axis_size("batch")
    seq, batch = lax.axis_index("seq"), lax.axis_index("batch")
    core, place = batch % 2, batch // 2
    paired = n_batch == 8
    total_pos = span * n_seq
    slots = n_slots // n_seq
    tokens = slots * total_pos
    tables = [jnp.asarray(t) for t in half_tables(total_pos)]
    gain1, gain2 = norm1_gain[None], norm2_gain[None]

    block = jnp.arange(4, dtype=jnp.int32)
    swap = lambda rel: (rel % 2) * 2 + rel // 2
    rel = block ^ seq
    row_at = jnp.where(core == 0, swap(rel), rel)
    chip_at = swap(block ^ place) if paired else block
    col_at = row_at if paired else block
    own_lengths = lax.dynamic_slice_in_dim(lengths, seq * slots, slots)
    head = jnp.stack([seq, core, place if paired else jnp.zeros_like(place)]).astype(jnp.int32)
    ids = jnp.concatenate([head, own_lengths, row_at, chip_at, col_at])

    x_turned = turn(ids, inputs, True)
    x_sent = [x_turned[s * n_seq : (s + 1) * n_seq] for s in range(slots)]
    x_blocks = [
        [sent[0]] + [exchange(sent[r], blocks_of(r)) for r in range(1, n_seq)] for sent in x_sent
    ]
    ct_turned = turn(ids, cotangent, False)
    weights = (in_weight, static_kernel, *tables, out_weight, short_taps, gain1, gain2)

    saved, n2_parts, n2_others = None, [], []
    flat = lambda a: a.reshape(-1, width)
    for s in range(slots):
        if s == 0:
            x_blocks[0], ct_turned = tie(x_blocks[0], ct_turned)
            ct_blocks = [ct_turned[0]] + [exchange(ct_turned[r], blocks_of(r)) for r in range(1, n_seq - 1)]
        if s == 1:
            x_blocks, ct_blocks, last, saved = tie(x_blocks, ct_blocks, ct_turned[n_seq - 1], saved)
            ct_blocks.append(exchange(last, blocks_of(n_seq - 1)))
            ct_others = [exchange(flat(c), across) for c in ct_blocks[:-1]]
        *saved, n2 = mixer_forward(ids, s, slots, x_blocks[s], weights, saved)
        n2_parts.append(n2.reshape(total_pos, width))
        n2_others.append(exchange(n2_parts[-1], across))
    ct_others.append(exchange(flat(ct_blocks[-1]), across))
    ct_parts = [flat(c) for c in ct_blocks] + ct_others
    p_all, spec, conv, gated, normed, x_whole, residual = saved
    n2_parts = n2_parts + n2_others

    pieces, chunks, shared = [], [], []
    chip_steps, seq_steps, cuts = (next_chip, far_chip), (first_side, second_side), ("rows", "lanes", "lanes", "done")
    for k in range(CHUNKS):
        out = glu_chunk(ids, k, n2_parts, ct_parts, glu_weight, down_weight, shared, n_seq)
        parts, shared = out[:4], out[4:]
        chunks.append(parts)
        if paired:
            pieces.append(Piece(*parts[:2], zip(seq_steps + chip_steps, cuts), alone=k == 0))
            pieces.append(Piece(*parts[2:], zip(chip_steps + seq_steps, cuts), alone=k == 0))
        if k > 0:
            ct_parts, shared = boundary(ids, pieces, (ct_parts, shared))
    ff_pieces = list(pieces)
    grads, hiddens, w_glus, w_downs = shared
    out_own, out_sent = halves_product(ids, hiddens, w_downs, 0)
    out_other = exchange(out_sent, across)
    grads, out_sent = tie(grads, out_sent)
    n2g_own, n2g_sent = halves_product(ids, grads, w_glus, 1)
    n2g_other = exchange(n2g_sent, across)
    out_other, n2g_sent = tie(out_other, n2g_sent)
    stay, later, sent = combine(ids, out_own, out_other, residual)
    moved = Piece(flat(later), flat(sent), [(first_side, "relay"), (second_side, "land")])
    pieces.append(moved)
    n2g_own = boundary(ids, pieces, n2g_own)
    residual_grad, conv_grad, pg_gate, small_out, a_keep, a_send = back_out(
        ids, n2g_own, n2g_other, residual, ct_blocks, gated, conv, p_all, normed, out_weight, short_taps, gain2
    )
    conv_grad, pg_gate = boundary(ids, pieces, (conv_grad, pg_gate))
    sum_steps = [(across, "rows"), (first_side, "rows"), (second_side, "done")]
    a = Piece(flat(a_keep), flat(a_send), sum_steps, alone=True)
    if paired:
        pieces.append(a)
    pg_rest, small_conv, b_keep, b_send = back_conv(ids, conv_grad, spec, p_all, normed, tables, short_taps)
    pg_rest, pg_gate = boundary(ids, pieces, (pg_rest, pg_gate))
    b = Piece(flat(b_keep), flat(b_send), sum_steps, alone=True)
    if paired:
        pieces.append(b)
    gain_in, *x_sent = back_in(ids, pg_gate, pg_rest, x_whole, residual_grad, in_weight, gain1)
    x_sent = boundary(ids, pieces, x_sent)
    output = unturn(ids, [stay] + [ref for ref, _ in moved.got], LOW, tuple(at for _, at in moved.got))
    small = jnp.concatenate([gain_in, small_out, small_conv], axis=0)
    n_small = small.shape[0] + -small.shape[0] % 16
    if paired:
        small = jnp.pad(small, ((0, n_small - small.shape[0]), (0, 0))).astype(LOW)
        small = Piece(small, small, [(first_side, "all"), (second_side, "all")], alone=True)
        pieces.append(small)
        x_sent, output = boundary(ids, pieces, (x_sent, output))
        own, *sent = by_chip(ids, a, b, small)
        own, x_sent = tie(own, x_sent)
        got = [exchange(x, lambda s, b, rel=rel: (s, b ^ (2 * rel))) for rel, x in enumerate(sent, 1)]
        x_got = [x_sent[0]] + [exchange(x_sent[r], blocks_of(r)) for r in range(1, n_seq)]
        input_grad = unturn(ids, x_got, F32)
        got, input_grad = tie(got, input_grad)
        own, sent = cut_cores(
            ids, (own, *got), [p.keep for p in ff_pieces[0::2]], [p.keep for p in ff_pieces[1::2]], n_batch, n_small
        )
        total_in, total_out, total_static, total_glu, total_down, gains, total_taps = finish(
            ids, own, exchange(sent, across), width, total_pos, n_batch, n_small
        )
    else:
        x_got = [x_sent[0]] + [exchange(x_sent[r], blocks_of(r)) for r in range(1, n_seq)]
        pieces = [a, b]
        while a.steps:
            boundary(ids, pieces, ())
        top = width // 8
        in_rows = jnp.concatenate([a.keep[top:], b.keep[:top], b.keep[top : 2 * top]], axis=1)
        total_in = spread_sum(in_rows, core, 0, 0)
        total_out = spread_sum(a.keep[:top], core, 0, 0)
        total_static = spread_sum(b.keep[2 * top :], core, 0, 0)
        side = n_seq // 2
        halves = lambda x: x.reshape(2, x.shape[0] // 2, x.shape[1])
        glu = jnp.stack(
            [seq_sums(halves(c[0]), halves(c[1])).reshape(-1, side, 2, side, LANES) for c in chunks], axis=4
        )
        glu = glu.transpose(0, 2, 1, 3, 4, 5).reshape(-1, 2 * n_seq, 1, CHUNKS * LANES)
        mine = (jnp.arange(2) == core)[:, None]
        glu = jnp.where(mine, glu, 0).astype(F32).reshape(glu.shape[0], -1)
        total_glu = lax.psum_scatter(glu, "batch", scatter_dimension=1, tiled=True)
        joined = [jnp.concatenate([c[2], c[3]], axis=int(c[2].shape[0] == width)) for c in chunks]
        down = jnp.stack([d.reshape(width, n_seq, LANES) for d in joined], axis=2)
        down = down.reshape(width, n_seq, 1, CHUNKS * LANES)
        down = jnp.where(mine, down, 0).astype(F32).reshape(width, -1)
        down = lax.psum_scatter(down, "batch", scatter_dimension=0, tiled=True)
        total_down = lax.psum_scatter(down, "seq", scatter_dimension=1, tiled=True).T

        small = lax.psum(small, ("seq", "batch"))
        gains = jnp.stack([small[0], small[4]])
        total_taps = jnp.concatenate([small[1:4], small[5:8], small[8:11]], axis=1)
        input_grad = unturn(ids, x_got, F32)
    return (
        output,
        input_grad,
        gains[0],
        total_in,
        total_taps,
        total_static,
        total_out,
        gains[1],
        total_glu,
        total_down,
    )


def solution(mesh):
    return jax.shard_map(
        on_device,
        mesh=mesh,
        in_specs=(
            P("seq", "batch", None),
            P("batch"),
            P(),
            P(),
            P(),
            P(),
            P(),
            P(),
            P(),
            P(),
            P("seq", "batch", None),
        ),
        out_specs=(
            P("seq", "batch", None),
            P("seq", "batch", None),
            P(),
            P("seq", "batch"),
            P(),
            P("seq", "batch"),
            P("seq", "batch"),
            P(),
            P("seq", "batch"),
            P("seq", "batch"),
        ),
        check_vma=False,
    )
```

```python
import functools
import math

import jax
import jax.numpy as jnp
import numpy as np
from jax import lax
from jax.experimental import pallas as pl
from jax.experimental.pallas import tpu as pltpu
from jax.sharding import PartitionSpec as P

F32 = jnp.float32
LOW = jnp.bfloat16
CHUNKS = 3
LANES = 128
ROOT = math.sqrt(2.0 / math.pi)
CUBE = 0.044715
MIB = 2**20
COST = 1000
LONG = 3 * 10**10
GLU_MIB = 50
GROUPS = ((0, 1), (2,))
MIX_MIB = 44
BACK_MIB = 46
ANY = pl.BlockSpec(memory_space=pl.ANY)

SEQ, CORE, PLACE, LENGTH, ROW_AT, CHIP_AT, COL_AT = 0, 1, 2, 3, 5, 9, 13


def half_tables(count):
    steps = np.arange(count)
    angle = (np.arange(count // 2)[:, None] * steps[None, :] % count) * (2.0 * math.pi / count)
    low_rows = np.cos(angle)
    high_rows = -np.sin(angle)
    high_rows[0] = np.where(steps % 2 == 0, 1.0, -1.0)
    table = np.concatenate([low_rows, high_rows], axis=0)
    weight = np.where(steps % (count // 2) == 0, 1.0, 2.0) / count
    return table.astype(LOW), (table * weight[:, None]).T.astype(LOW)


def dot(a, b, ca=1, cb=0):
    return lax.dot_general(a, b, (((ca,), (cb,)), ((), ())), preferred_element_type=F32)


def gelu_parts(z):
    square = z * z
    tanh = jnp.tanh(z * (ROOT + (ROOT * CUBE) * square))
    plus = 0.5 + 0.5 * tanh
    act = z * plus
    return act, plus + act * (1.0 - tanh) * (ROOT + (3.0 * ROOT * CUBE) * square)


def gelu(z):
    return z * (0.5 + 0.5 * jnp.tanh(z * (ROOT + (ROOT * CUBE) * (z * z))))


def standardize(values):
    centred = values - jnp.mean(values, axis=-1, keepdims=True)
    inverse = lax.rsqrt(jnp.mean(centred * centred, axis=-1, keepdims=True) + 1e-05)
    return centred * inverse, inverse


def norm_back(grad_in, standard, inverse, gain_vec):
    scaled = grad_in * gain_vec
    inner = (
        scaled
        - jnp.mean(scaled, axis=-1, keepdims=True)
        - standard * jnp.mean(scaled * standard, axis=-1, keepdims=True)
    )
    return inverse * inner


def shifts(a):
    count = a.shape[0]
    row = lax.broadcasted_iota(jnp.int32, a.shape, 0)
    before = jnp.where(row == 0, 0.0, pltpu.roll(a, 1, 0))
    after = jnp.where(row == count - 1, 0.0, pltpu.roll(a, count - 1, 0))
    return before, after


def mix(low, taps):
    wide = low.astype(F32)
    before, after = shifts(wide)
    return taps[0:1] * before + taps[1:2] * wide + taps[2:3] * after


def mix_back(grad, low, taps):
    wide = low.astype(F32)
    before, after = shifts(grad)
    sums = [jnp.sum(side * wide, axis=0, keepdims=True) for side in (after, grad, before)]
    return sums, (taps[0:1] * after + taps[1:2] * grad + taps[2:3] * before).astype(LOW)


def spectrum_product(a, b, sign):
    half = a.shape[0] // 2
    ar, ai, br, bi = a[:half], a[half:], b[:half], b[half:]
    first = lax.broadcasted_iota(jnp.int32, ar.shape, 0) == 0
    both = ai * bi
    re = ar * br - jnp.where(first, 0.0, sign * both)
    im = jnp.where(first, both, ai * br + sign * (ar * bi))
    return jnp.concatenate([re.astype(LOW), im.astype(LOW)], axis=0)


def live_mask(length, count):
    return (lax.broadcasted_iota(jnp.int32, (count, 1), 0) < length).astype(F32)


def whole(shape):
    return pl.BlockSpec(shape, lambda *at: (0,) * len(shape))


def kept(shape):
    return pl.BlockSpec(shape, lambda *at: (0,) * len(shape), pipeline_mode=pl.Buffered(1))


def in_hbm(arrays):
    return [pltpu.with_memory_space_constraint(a, pltpu.HBM) for a in arrays]


def sds(shape, dtype=LOW):
    return jax.ShapeDtypeStruct(shape, dtype)


def call(body, grid, ids, in_specs, out_specs, out_shape, args, scratch=(), aliases=None, mib=12, cost=COST):
    return pl.pallas_call(
        body,
        grid_spec=pltpu.PrefetchScalarGridSpec(
            num_scalar_prefetch=1, grid=grid, in_specs=in_specs, out_specs=out_specs, scratch_shapes=list(scratch)
        ),
        out_shape=out_shape,
        compiler_params=pltpu.CompilerParams(vmem_limit_bytes=mib * MIB),
        input_output_aliases=aliases or {},
        cost_estimate=pl.CostEstimate(flops=cost, bytes_accessed=COST, transcendentals=0),
    )(ids, *args)


def turn_kernel(by_slot, ids, x_ref, *refs):
    outs, held = refs[:-1], refs[-1]
    held[...] = jnp.swapaxes(x_ref[...].astype(F32), 0, 1).astype(LOW)
    n_seq = 4
    own = held.shape[0] // n_seq
    for r in range(n_seq):
        at = (ids[SEQ] ^ r) * own
        for s in range(own):
            if by_slot:
                outs[s * n_seq + r][...] = held[at + s]
            else:
                outs[r][s] = held[at + s]


def turn(ids, x, by_slot):
    span, slots, width = x.shape
    own = slots // 4
    shape = (span, width) if by_slot else (own, span, width)
    n_out = slots if by_slot else 4
    return call(
        functools.partial(turn_kernel, by_slot), (1,), ids, [whole(x.shape)], [whole(shape)] * n_out,
        [sds(shape)] * n_out, in_hbm([x]), [pltpu.VMEM((slots, span, width), LOW)], mib=20,
    )


def unturn_kernel(places, ids, *refs):
    blocks, out, held = refs[:-2], refs[-2], refs[-1]
    slots, span, width = held.shape
    own = slots // 4
    rels = range(4) if places is None else (0, 1 + ids[CORE], 2 - ids[CORE], 3)
    for i, (rel, block) in enumerate(zip(rels, blocks)):
        for s in range(own):
            to = (ids[SEQ] ^ rel) * own + s
            if places is None or i == 0:
                held[to] = block[s].astype(F32)
            else:
                for c in range(width // LANES):
                    row = places[i - 1] + (c * own + s) * span
                    held[to, :, c * LANES : (c + 1) * LANES] = block[row : row + span].astype(F32)
    out[...] = jnp.swapaxes(held[...], 0, 1).astype(out.dtype)


def unturn(ids, blocks, dtype, places=None):
    own, span, width = blocks[0].shape
    slots = own * 4
    return call(
        functools.partial(unturn_kernel, places),
        (1,),
        ids,
        [whole(b.shape) for b in blocks],
        whole((span, slots, width)),
        sds((span, slots, width), dtype),
        blocks,
        [pltpu.VMEM((slots, span, width), F32)],
        mib=32,
    )


class Copies:
    def __init__(self, sems):
        self.sems, self.made = sems, []

    def start(self, src, to):
        copy = pltpu.make_async_copy(src, to, self.sems.at[len(self.made)])
        copy.start()
        self.made.append(copy)
        return copy

    def finish(self):
        for copy in self.made:
            copy.wait()


def mixer_kernel(
    slot, ids, x0, x1, x2, x3, in_weight, static, table, inverse, w_out, taps, gain1, gain2, *refs
):
    p_hbm, spec_hbm, conv_hbm, gated_hbm, normed_hbm, x_hbm, residual_hbm, n2_hbm = refs[-22:-14]
    (x, w_in, static_low, tab, inv, w_o, p, spec, conv, gated, normed, total, sems_in, sems_out) = refs[-14:]
    blocks = (x0, x1, x2, x3)
    count, width = x.shape
    span = count // len(blocks)
    scale = count**-0.5
    loads, stores = Copies(sems_in), Copies(sems_out)
    place = [pl.ds(pl.multiple_of((ids[SEQ] ^ r) * span, span), span) for r in range(len(blocks))]
    x_copies = [loads.start(block, x.at[place[r]]) for r, block in enumerate(blocks)]
    w_copy, *t_copies = [
        loads.start(src, to)
        for src, to in ((in_weight, w_in), (table, tab), (static, static_low), (inverse, inv), (w_out, w_o))
    ]
    for copy in x_copies:
        copy.wait()
    stores.start(x, x_hbm.at[slot])
    for q in range(len(blocks)):
        rows = slice(q * span, (q + 1) * span)
        wide = x[rows].astype(F32)
        standard, _ = standardize(wide)
        normed[rows] = (standard * gain1[...]).astype(LOW)
        total[rows] = wide
    stores.start(normed, normed_hbm.at[slot])
    live = live_mask(ids[LENGTH + slot], count)
    w_copy.wait()
    p[...] = dot(normed[...], w_in[...]).astype(LOW)
    stores.start(p, p_hbm.at[slot])
    for copy in t_copies:
        copy.wait()
    static_spec = dot(tab[...], static_low[...].astype(LOW))
    value = (live * mix(p[:, width : 2 * width], taps[:, width : 2 * width])).astype(LOW)
    vs = dot(tab[...], value)
    cond = (live * gelu(mix(p[:, 2 * width :], taps[:, 2 * width :]))).astype(LOW)
    ks = static_spec + scale * dot(tab[...], cond)
    spec[:, :width], spec[:, width:] = vs.astype(LOW), ks.astype(LOW)
    stores.start(spec, spec_hbm.at[slot])
    conv[...] = dot(inv[...], spectrum_product(vs, ks, 1.0)).astype(LOW)
    stores.start(conv, conv_hbm.at[slot])
    gated[...] = (live * mix(p[:, :width], taps[:, :width]) * conv[...].astype(F32)).astype(LOW)
    stores.start(gated, gated_hbm.at[slot])
    total[...] += dot(gated[...], w_o[...])
    for r in range(len(blocks)):
        stores.start(total.at[place[r]], residual_hbm.at[slot, r])
    n2 = x
    stores.made[0].wait()
    for q in range(len(blocks)):
        rows = slice(q * span, (q + 1) * span)
        standard, _ = standardize(total[rows])
        n2[rows] = (standard * gain2[...]).astype(LOW)
    for r in range(len(blocks)):
        stores.start(n2.at[place[r]], n2_hbm.at[r])
    for copy in stores.made[1:]:
        copy.wait()


def mixer_forward(ids, slot, slots, x_blocks, weights, before):
    span, width = x_blocks[0].shape
    count = span * len(x_blocks)
    cols = (3, 2, 1, 1, 1, 1)
    rel = (len(x_blocks), span, width)
    *large, taps, gain1, gain2 = weights
    args = (*x_blocks, *in_hbm(large), taps, gain1, gain2)
    in_specs = [ANY] * (len(x_blocks) + len(large)) + [kept(a.shape) for a in (taps, gain1, gain2)]
    aliases = {}
    if before is not None:
        aliases = {1 + len(args) + i: i for i in range(len(before))}
        args, in_specs = args + tuple(before), in_specs + [ANY] * len(before)
    return call(
        functools.partial(mixer_kernel, slot),
        (1,),
        ids,
        in_specs,
        [ANY] * 8,
        [pltpu.HBM((slots, count, m * width), LOW) for m in cols] + [pltpu.HBM((slots, *rel), F32), sds(rel)],
        args,
        [
            pltpu.VMEM((count, width), LOW),
            pltpu.VMEM((width, 3 * width), LOW),
            pltpu.VMEM((count, width), F32),
            pltpu.VMEM((count, count), LOW),
            pltpu.VMEM((count, count), LOW),
            pltpu.VMEM((width, width), LOW),
            pltpu.VMEM((count, 3 * width), LOW),
            pltpu.VMEM((count, 2 * width), LOW),
            pltpu.VMEM((count, width), LOW),
            pltpu.VMEM((count, width), LOW),
            pltpu.VMEM((count, width), LOW),
            pltpu.VMEM((count, width), F32),
            pltpu.SemaphoreType.DMA((9,)),
            pltpu.SemaphoreType.DMA((14,)),
        ],
        aliases,
        mib=MIX_MIB,
        cost=LONG,
    )


def glu_kernel(ks, n_seq, slots, ids, *refs):
    n_blocks, n = 4, len(ks)
    n2_parts, ct_parts = refs[: 2 * slots], refs[2 * slots : 2 * slots + 2 * n_blocks]
    glu_hbm, down_hbm = refs[2 * (slots + n_blocks) :][:2]
    parts_out = refs[-16 - 4 * n : -16]
    (
        gu_hbm, hidden_hbm, w_glu_hbm, w_down_hbm,
        n2, ct, w_glus, w_downs, hidden, gu, g_low, d_low, n2_sems, ct_sems, w_sems, out_sems,
    ) = refs[-16:]
    rows = n2.shape[0] // 2
    span = rows // n_blocks // slots
    units = w_downs.shape[1]
    halves = [pl.ds(h * rows, rows) for h in range(2)]

    def load(h):
        copies = []
        for s in range(slots):
            for r in range(n_blocks):
                copies.append(
                    pltpu.make_async_copy(
                        n2_parts[h * slots + s].at[pl.ds(r * span, span)],
                        n2.at[pl.ds(h * rows + (r * slots + s) * span, span)],
                        n2_sems.at[(h * slots + s) * n_blocks + r],
                    )
                )
        return copies, [
            pltpu.make_async_copy(
                ct_parts[h * n_blocks + r],
                ct.at[pl.ds(h * rows + r * slots * span, slots * span)],
                ct_sems.at[h * n_blocks + r],
            )
            for r in range(n_blocks)
        ]

    loads = [load(h) for h in range(2)]
    glu_copies, down_copies = [], []
    for i, k in enumerate(ks):
        starts = [pl.multiple_of(((2 * m + ids[CORE]) * CHUNKS + k) * LANES, LANES) for m in range(2 * n_seq)]
        glu_copies.append(
            [
                pltpu.make_async_copy(
                    glu_hbm.at[:, pl.ds(col, LANES)],
                    w_glus.at[i, :, pl.ds(m * LANES, LANES)],
                    w_sems.at[3 * n_seq * i + m],
                )
                for m, col in enumerate(starts)
            ]
        )
        down_copies.append(
            [
                pltpu.make_async_copy(
                    down_hbm.at[pl.ds(row, LANES)],
                    w_downs.at[i, pl.ds(m * LANES, LANES)],
                    w_sems.at[3 * n_seq * i + 2 * n_seq + m],
                )
                for m, row in enumerate(starts[:n_seq])
            ]
        )
    for copy in loads[0][0] + glu_copies[0] + down_copies[0] + loads[0][1] + loads[1][0] + loads[1][1]:
        copy.start()
    for i in range(1, n):
        for copy in glu_copies[i] + down_copies[i]:
            copy.start()
    outs = []

    def store(src, to):
        copy = pltpu.make_async_copy(src, to, out_sems.at[len(outs)])
        copy.start()
        outs.append(copy)

    for i, k in enumerate(ks):
        glu_keep, glu_send, down_keep, down_send = parts_out[4 * i : 4 * i + 4]
        w_glu, w_down = w_glus.at[i], w_downs.at[i]
        for copy in (loads[0][0] if i == 0 else []) + glu_copies[i]:
            copy.wait()
        gate_ups = [dot(n2[halves[0]], w_glu[...])]
        for copy in down_copies[i] + (loads[0][1] + loads[1][0] + loads[1][1] if i == 0 else outs[8 * i - 8 : 8 * i]):
            copy.wait()
        gate_ups.append(dot(n2[halves[1]], w_glu[...]))
        for h, gate_up in enumerate(gate_ups):
            here = halves[h]
            gate, up = gate_up[:, :units], gate_up[:, units:]
            hidden_grad = dot(ct[here], w_down[...], 1, 1)
            act, slope = gelu_parts(gate)
            hidden[here] = (act * up).astype(LOW)
            gu[here, :units] = (hidden_grad * up * slope).astype(LOW)
            gu[here, units:] = (hidden_grad * act).astype(LOW)
        mine, wide = pl.ds(k * units, units), pl.ds(2 * k * units, 2 * units)
        store(w_glu, w_glu_hbm.at[:, wide])
        store(w_down, w_down_hbm.at[mine])
        store(hidden, hidden_hbm.at[:, mine])
        store(gu, gu_hbm.at[:, wide])
        g_sum = dot(n2[...], gu[...], 0, 0)
        side = units // 2
        size = g_sum.shape[0] // 4
        for q in range(4):
            here = pl.ds(pl.multiple_of(ids[ROW_AT + q] * size, size), size)
            for high in range(2):
                for g in range(2):
                    at = (high ^ (ids[PLACE] % 2)) * 2 + (g ^ (ids[PLACE] // 2 % 2))
                    from_col = g * units + high * side
                    part = g_sum[q * size : (q + 1) * size, from_col : from_col + side]
                    g_low[here, pl.ds(pl.multiple_of(at * side, side), side)] = part.astype(LOW)
        half = d_low.shape[0] // 2
        store(g_low.at[pl.ds(half, half)], glu_send)
        store(g_low.at[pl.ds(0, half)], glu_keep)
        d_sum = dot(ct[...], hidden[...], 0, 0)
        for q in range(4):
            here = pl.ds(pl.multiple_of(ids[CHIP_AT + q] * size, size), size)
            for s in range(4):
                part = d_sum[q * size : (q + 1) * size, s * LANES : (s + 1) * LANES]
                d_low[here, pl.ds(pl.multiple_of(ids[COL_AT + s] * LANES, LANES), LANES)] = part.astype(LOW)
        store(d_low.at[pl.ds(half, half)], down_send)
        store(d_low.at[pl.ds(0, half)], down_keep)
    for copy in outs[8 * n - 8 :]:
        copy.wait()


def glu_chunks(ids, ks, n2_parts, ct_parts, glu_weight, down_weight, shared, n_seq):
    width, units = glu_weight.shape[0], n_seq * LANES
    slots, n_blocks, n = len(n2_parts) // 2, 4, len(ks)
    tokens = sum(p.shape[0] for p in n2_parts)
    here = [pltpu.with_memory_space_constraint(x, pltpu.VMEM) for x in n2_parts[slots:]] if not shared else n2_parts[slots:]
    args = (*n2_parts[:slots], *here, *ct_parts, *in_hbm((glu_weight, down_weight)), *shared)
    aliases = {1 + len(args) - len(shared) + i: 4 * n + i for i in range(len(shared))}
    return call(
        functools.partial(glu_kernel, ks, n_seq, slots),
        (1,),
        ids,
        [ANY] * len(args),
        [ANY] * (4 * n + 4),
        ([pltpu.VMEM((width // 2, 2 * units), LOW)] * 2 + [pltpu.VMEM((width // 2, units), LOW)] * 2) * n
        + [
            pltpu.HBM(x, LOW)
            for x in (
                (tokens, 2 * CHUNKS * units),
                (tokens, CHUNKS * units),
                (width, 2 * CHUNKS * units),
                (CHUNKS * units, width),
            )
        ],
        args,
        [
            pltpu.VMEM((tokens, width), LOW),
            pltpu.VMEM((tokens, width), LOW),
            pltpu.VMEM((n, width, 2 * units), LOW),
            pltpu.VMEM((n, units, width), LOW),
            pltpu.VMEM((tokens, units), LOW),
            pltpu.VMEM((tokens, 2 * units), LOW),
            pltpu.VMEM((width, 2 * units), LOW),
            pltpu.VMEM((width, units), LOW),
            pltpu.SemaphoreType.DMA((2 * slots * n_blocks,)),
            pltpu.SemaphoreType.DMA((2 * n_blocks,)),
            pltpu.SemaphoreType.DMA((3 * n_seq * n,)),
            pltpu.SemaphoreType.DMA((8 * n,)),
        ],
        aliases,
        mib=GLU_MIB,
        cost=LONG,
    )


def halves_product_kernel(cb, ids, rows_ref, weight, own, other):
    result = dot(rows_ref[...], weight[...], 1, cb)

    @pl.when(pl.program_id(0) < pl.num_programs(0) // 2)
    def _():
        other[...] = result.astype(LOW)

    @pl.when(pl.program_id(0) >= pl.num_programs(0) // 2)
    def _():
        own[...] = result


def halves_product(ids, values, weight, cb, rows=512):
    tokens, size = values.shape
    width = weight.shape[1 - cb]
    per = tokens // 2 // rows
    return call(
        functools.partial(halves_product_kernel, cb),
        (2 * per,),
        ids,
        [pl.BlockSpec((rows, size), lambda i, ids: ((i + per) % (2 * per), 0)), kept(weight.shape)],
        [
            pl.BlockSpec((rows, width), lambda i, ids: (jnp.maximum(i - per, 0), 0)),
            pl.BlockSpec((rows, width), lambda i, ids: (jnp.minimum(i, per - 1), 0)),
        ],
        [sds((tokens // 2, width), F32), sds((tokens // 2, width))],
        in_hbm((values, weight)),
        mib=32,
        cost=LONG,
    )


def combine_kernel(ids, own, other, residual, stay, later, send):
    span = stay.shape[1]
    second, first = 2 - ids[CORE], 1 + ids[CORE]
    for r, out, at in ((0, stay, 0), (second, later, 0), (first, send, 0), (3, send, 1)):
        value = (residual[0, r] + (own[r, 0] + other[r, 0].astype(F32))).astype(LOW)
        if out is send:
            send[at, 0] = value
        else:
            out[0] = value


def combine(ids, own, other, residual):
    slots, n_blocks, span, width = residual.shape
    rows = pl.BlockSpec((n_blocks, 1, span, width), lambda s, ids: (0, s, 0, 0))
    block = pl.BlockSpec((1, span, width), lambda s, ids: (s, 0, 0))
    own, other = [x.reshape(n_blocks, slots, span, width) for x in (own, other)]
    return call(
        combine_kernel,
        (slots,),
        ids,
        [rows, rows, pl.BlockSpec((1, n_blocks, span, width), lambda s, ids: (s, 0, 0, 0))],
        [block, block, pl.BlockSpec((2, 1, span, width), lambda s, ids: (0, s, 0, 0))],
        [sds((slots, span, width))] * 2 + [sds((2, slots, span, width))],
        (own, other, residual),
        mib=16,
    )


def place_halves(ids, grad, at, keep, send):
    size = grad.shape[0] // 8
    for q in range(4):
        to = ids[ROW_AT + q]
        for c in range(2):
            rows = grad[(2 * q + c) * size : (2 * q + c + 1) * size]

            @pl.when(ids[CORE] == c)
            def _(rows=rows, to=to):
                keep[to, at : at + size] = rows

            @pl.when(ids[CORE] != c)
            def _(rows=rows, to=(to % 2) * 2 + to // 2):
                send[to, at : at + size] = rows


def accumulate(step, ref, value):
    @pl.when(step == 0)
    def _():
        ref[...] = value

    @pl.when(step > 0)
    def _():
        ref[...] += value


def back_out_kernel(
    ids, n2g_own_hbm, n2g_other_hbm, residual_hbm, ct0, ct1, ct2, ct3, gated_hbm, conv_hbm, p_hbm, normed_hbm, w_hbm,
    taps, gain2, residual_grad_hbm, conv_grad_hbm, pg_hbm, small, keep, send,
    n2g_own, n2g_other, residual, cot, gated, conv, p, normed, w_out, branch, conv_grad, pg, sems_in, sems_out,
):
    slots, n_blocks, span, width = residual.shape
    count = n_blocks * span
    loads, stores = Copies(sems_in), Copies(sems_out)
    early, late = [], []
    for s in range(slots):
        here = pl.ds(s * count, count)
        early.append(
            [loads.start(residual_hbm.at[s], residual.at[s])]
            + [loads.start(ref.at[s], cot.at[s, r]) for r, ref in enumerate((ct0, ct1, ct2, ct3))]
            + [loads.start(n2g_own_hbm.at[:, s], n2g_own.at[s]), loads.start(n2g_other_hbm.at[:, s], n2g_other.at[s])]
        )
        late.append(
            ([loads.start(w_hbm, w_out)] if s == 0 else [])
            + [loads.start(p_hbm.at[s, :, pl.ds(0, width)], p.at[here]), loads.start(conv_hbm.at[s], conv.at[here])]
        )
    last = [
        loads.start(ref.at[s], to.at[pl.ds(s * count, count)])
        for s in range(slots)
        for ref, to in ((gated_hbm, gated), (normed_hbm, normed))
    ]
    gain_grad, tap_sums = jnp.zeros((1, width), F32), None
    for s in range(slots):
        here = slice(s * count, (s + 1) * count)
        for copy in early[s]:
            copy.wait()
        for r in range(n_blocks):
            at = pl.multiple_of(s * count + (ids[SEQ] ^ r) * span, span)
            grad = n2g_own[s, r] + n2g_other[s, r].astype(F32)
            unit, inverse = standardize(residual[s, r])
            gain_grad += jnp.sum(grad * unit, axis=0, keepdims=True)
            value = cot[s, r].astype(F32) + norm_back(grad, unit, inverse, gain2[...])
            residual[s, r] = value
            branch[pl.ds(at, span), :] = value.astype(LOW)
        stores.start(residual.at[s], residual_grad_hbm.at[s])
        live = live_mask(ids[LENGTH + s], count)
        for copy in late[s]:
            copy.wait()
        gated_grad = live * dot(branch[here], w_out[...], 1, 1)
        conv_grad[here] = (gated_grad * mix(p[here], taps[...])).astype(LOW)
        sums, pg[here] = mix_back(gated_grad * conv[here].astype(F32), p[here], taps[...])
        tap_sums = sums if s == 0 else [x + y for x, y in zip(tap_sums, sums)]
        stores.start(conv_grad.at[pl.ds(s * count, count)], conv_grad_hbm.at[s])
        stores.start(pg.at[pl.ds(s * count, count)], pg_hbm.at[s])
    small[...] = jnp.concatenate(tap_sums + [gain_grad], axis=0)
    for copy in last:
        copy.wait()
    place_halves(ids, dot(gated[...], branch[...], 0, 0).astype(LOW), 0, keep, send)
    place_halves(ids, dot(normed[...], pg[...], 0, 0).astype(LOW), width // 8, keep, send)
    stores.finish()


def back_out(ids, n2g_own, n2g_other, residual, cot, gated, conv, p_all, normed, w_out, taps, gain2):
    slots, n_blocks, span, width = residual.shape
    count = n_blocks * span
    n2g_own, n2g_other = [x.reshape(n_blocks, slots, span, width) for x in (n2g_own, n2g_other)]
    part = (4, 2 * width // 8, width)
    args = (n2g_own, n2g_other, *in_hbm([residual]), *cot, *in_hbm((gated, conv, p_all, normed, w_out)))
    n_loads = slots * (1 + n_blocks + 2 + 2 + 2) + 1
    flat = (slots * count, width)
    return call(
        back_out_kernel,
        (1,),
        ids,
        [ANY] * len(args) + [kept((3, width)), kept((1, width))],
        [ANY] * 3 + [whole((4, width))] + [pl.BlockSpec(memory_space=pltpu.VMEM)] * 2,
        [
            pltpu.HBM(residual.shape, F32),
            pltpu.HBM((slots, count, width), LOW),
            pltpu.HBM((slots, count, width), LOW),
            sds((4, width), F32),
            pltpu.VMEM(part, LOW),
            pltpu.VMEM(part, LOW),
        ],
        (*args, taps, gain2),
        [
            pltpu.VMEM(residual.shape, F32),
            pltpu.VMEM(residual.shape, LOW),
            pltpu.VMEM(residual.shape, F32),
            pltpu.VMEM(residual.shape, LOW),
            *[pltpu.VMEM(flat, LOW)] * 4,
            pltpu.VMEM((width, width), LOW),
            *[pltpu.VMEM(flat, LOW)] * 3,
            pltpu.SemaphoreType.DMA((n_loads,)),
            pltpu.SemaphoreType.DMA((3 * slots,)),
        ],
        mib=BACK_MIB,
        cost=LONG,
    )


def back_conv_kernel(
    ids, conv_grad_hbm, spec_hbm, p_hbm, normed_hbm, table_hbm, inverse_hbm, t_value, t_cond,
    pg_hbm, small, keep, send,
    conv_grad, spec, p, normed, table, inverse, pg, sems_in, sems_out,
):
    width = t_value.shape[1]
    count = table.shape[0]
    slots = conv_grad.shape[0] // count
    scale = count**-0.5
    loads, stores = Copies(sems_in), Copies(sems_out)
    here_of = lambda s: pl.ds(s * count, count)
    first = [loads.start(table_hbm, table)]
    parts = []
    for s in range(slots):
        parts.append([loads.start(conv_grad_hbm.at[s], conv_grad.at[here_of(s)])])
        parts.append([loads.start(spec_hbm.at[s], spec.at[here_of(s)])])
        if s == 0:
            parts[-1].append(loads.start(inverse_hbm, inverse))
        parts.append([loads.start(p_hbm.at[s, :, pl.ds(width, 2 * width)], p.at[here_of(s)])])
    last = [loads.start(normed_hbm.at[s], normed.at[here_of(s)]) for s in range(slots)]
    tap_sums = static_total = None
    for s in range(slots):
        here = slice(s * count, (s + 1) * count)
        live = live_mask(ids[LENGTH + s], count)
        for copy in (first if s == 0 else []) + parts[3 * s]:
            copy.wait()
        gs = dot(table[...], conv_grad[here])
        for copy in parts[3 * s + 1]:
            copy.wait()
        value_low = spectrum_product(gs, spec[here, width:].astype(F32), -1.0)
        cond_low = spectrum_product(gs, spec[here, :width].astype(F32), -1.0)
        value_grad = live * dot(inverse[...], value_low)
        back = dot(inverse[...], cond_low)
        static_total = back if s == 0 else static_total + back
        for copy in parts[3 * s + 2]:
            copy.wait()
        sums_v, pg[here, :width] = mix_back(value_grad, p[here, :width], t_value[...])
        cond_grad = (live * scale) * back * gelu_parts(mix(p[here, width:], t_cond[...]))[1]
        sums_c, pg[here, width:] = mix_back(cond_grad, p[here, width:], t_cond[...])
        sums = sums_v + sums_c
        tap_sums = sums if s == 0 else [x + y for x, y in zip(tap_sums, sums)]
        stores.start(pg.at[here_of(s)], pg_hbm.at[s])
    small[...] = jnp.concatenate(tap_sums, axis=0)
    place_halves(ids, static_total.astype(LOW), width // 4, keep, send)
    for copy in last:
        copy.wait()
    total = dot(normed[...], pg[...], 0, 0).astype(LOW)
    place_halves(ids, total[:, :width], 0, keep, send)
    place_halves(ids, total[:, width:], width // 8, keep, send)
    stores.finish()


def back_conv(ids, conv_grad, spec, p_all, normed, tables, taps):
    slots, count, width = conv_grad.shape
    tap = lambda m: pl.BlockSpec((3, width), lambda i, ids, m=m: (0, m))
    part = (4, (2 * width + count) // 8, width)
    args = in_hbm((conv_grad, spec, p_all, normed, *tables))
    rows = slots * count
    return call(
        back_conv_kernel,
        (1,),
        ids,
        [ANY] * len(args) + [tap(1), tap(2)],
        [ANY, whole((6, width))] + [pl.BlockSpec(memory_space=pltpu.VMEM)] * 2,
        [
            pltpu.HBM((slots, count, 2 * width), LOW),
            sds((6, width), F32),
            pltpu.VMEM(part, LOW),
            pltpu.VMEM(part, LOW),
        ],
        (*args, taps, taps),
        [
            pltpu.VMEM((rows, width), LOW),
            pltpu.VMEM((rows, 2 * width), LOW),
            pltpu.VMEM((rows, 2 * width), LOW),
            pltpu.VMEM((rows, width), LOW),
            pltpu.VMEM((count, count), LOW),
            pltpu.VMEM((count, count), LOW),
            pltpu.VMEM((rows, 2 * width), LOW),
            pltpu.SemaphoreType.DMA((4 * slots + 2,)),
            pltpu.SemaphoreType.DMA((slots,)),
        ],
        mib=BACK_MIB,
        cost=LONG,
    )


def back_in_kernel(ids, pg_gate, pg_rest, x, residual_grad, in_weight, gain1, gain_ref, *refs):
    outs, total = refs[:-1], refs[-1]
    s = pl.program_id(0)
    width = x.shape[2]
    span = residual_grad.shape[2]
    total[...] = dot(pg_gate[0], in_weight[:, :width], 1, 1) + dot(pg_rest[0], in_weight[:, width:], 1, 1)
    gain_grad = jnp.zeros((1, width), F32)
    for r, out in enumerate(outs):
        at = pl.ds(pl.multiple_of((ids[SEQ] ^ r) * span, span), span)
        standard, inverse = standardize(x[0, at, :].astype(F32))
        grad = total[at, :]
        gain_grad += jnp.sum(grad * standard, axis=0, keepdims=True)
        out[0] = (residual_grad[0, r] + norm_back(grad, standard, inverse, gain1[...])).astype(LOW)
    accumulate(s, gain_ref, gain_grad)


def back_in(ids, pg_gate, pg_rest, x, residual_grad, in_weight, gain1):
    slots, count, width = x.shape
    n_blocks, span = residual_grad.shape[1:3]
    seqs = lambda m: pl.BlockSpec((1, count, m * width), lambda s, ids: (s, 0, 0))
    rel = pl.BlockSpec((1, n_blocks, span, width), lambda s, ids: (s, 0, 0, 0))
    return call(
        back_in_kernel,
        (slots,),
        ids,
        [seqs(1), seqs(2), seqs(1), rel, kept(in_weight.shape), kept((1, width))],
        [whole((1, width))] + [pl.BlockSpec((1, span, width), lambda s, ids: (s, 0, 0))] * n_blocks,
        [sds((1, width), F32)] + [sds((slots, span, width))] * n_blocks,
        (pg_gate, pg_rest, x, residual_grad, in_weight, gain1),
        [pltpu.VMEM((count, width), F32)],
        mib=32,
        cost=LONG,
    )


def exchange(x, partner):
    n_seq, n_batch = lax.axis_size("seq"), lax.axis_size("batch")
    pairs = []
    for s in range(n_seq):
        for b in range(n_batch):
            to_s, to_b = partner(s, b)
            pairs.append((s * n_batch + b, to_s * n_batch + to_b))
    return lax.ppermute(x, ("seq", "batch"), pairs)


def across(s, b):
    return s, b ^ 1


def first_side(s, b):
    return s ^ (1 if b % 2 == 0 else 2), b


def second_side(s, b):
    return s ^ (2 if b % 2 == 0 else 1), b


def next_chip(s, b):
    return s, b ^ 2


def far_chip(s, b):
    return s, b ^ 4


def blocks_of(r):
    return lambda s, b: (s ^ r, b)


def tie(*groups):
    return lax.optimization_barrier(groups)


class Piece:
    def __init__(self, keep, send, steps, alone=False):
        self.keep, self.send, self.steps = keep, send, list(steps)
        self.arriving, self.place, self.got = None, 0, []
        if alone:
            self.arriving = exchange(send, self.steps[0][0])


def shape_after(shape, cut):
    rows, cols = shape
    if cut == "rows":
        return rows // 2, cols
    if cut == "lanes":
        return rows, cols // 2
    return rows, cols


def slabs(shape):
    return shape[0] * shape[1] // LANES


def put_slabs(to, at, value):
    rows = value.shape[0]
    for c in range(value.shape[1] // LANES):
        to[at + c * rows : at + (c + 1) * rows] = value[:, c * LANES : (c + 1) * LANES]


def engine_kernel(plan, n_in, *refs):
    ins, outs = refs[:n_in], refs[n_in:]
    for op, *rest in plan:
        if op == "fresh":
            src, row, (rows, cols), dst, at = rest
            put_slabs(outs[dst], at, ins[src][row : row + rows])
        elif op == "move":
            src, row, rows, dst, at = rest
            outs[dst][at : at + rows] = ins[src][row : row + rows]
        else:
            keep, src, row, (rows, cols), cut, stay, dst, at = rest
            held, arrived = ins[keep], ins[src]
            plain = arrived.shape == held.shape
            for c in range(cols // LANES):
                lanes = slice(c * LANES, (c + 1) * LANES)
                there = arrived[:, lanes] if plain else arrived[row + c * rows : row + (c + 1) * rows]
                total = (held[:, lanes].astype(F32) + there.astype(F32)).astype(LOW)
                if cut == "rows":
                    half = rows // 2
                    outs[stay][:, lanes] = total[:half]
                    outs[dst][at + c * half : at + (c + 1) * half] = total[half:]
                elif cut == "lanes" and c >= cols // LANES // 2:
                    to = at + (c - cols // LANES // 2) * rows
                    outs[dst][to : to + rows] = total
                else:
                    outs[stay][:, lanes] = total
                    if cut == "all":
                        outs[dst][at + c * rows : at + (c + 1) * rows] = total


def boundary(ids, pieces, guard):
    active = [p for p in pieces if p.steps]
    if not active:
        return guard
    arrivals = {id(p.arriving): p.arriving for p in active if p.arriving is not None}
    keys = list(arrivals)
    landed, guard = tie([arrivals[k] for k in keys], guard)
    landed = dict(zip(keys, landed))
    partners = []
    for p in active:
        upcoming = p.steps if p.arriving is None else p.steps[1:]
        if upcoming and upcoming[0][0] not in partners:
            partners.append(upcoming[0][0])
    ins, index, plan, stays, results = [], {}, [], [], []
    rows_of = dict.fromkeys(partners, 0)

    def source(x):
        if id(x) not in index:
            index[id(x)] = len(ins)
            ins.append(x)
        return index[id(x)]

    def message(partner, rows):
        at = rows_of[partner]
        rows_of[partner] += rows
        return partners.index(partner), at

    for p in active:
        partner, cut = p.steps[0]
        if p.arriving is None:
            parts = 2 if cut == "relay" else 1
            shape = (p.send.shape[0] // parts, p.send.shape[1])
            dst, at = message(partner, parts * slabs(shape))
            for i in range(parts):
                plan.append(("fresh", source(p.send), i * shape[0], shape, dst, at + i * slabs(shape)))
            results.append((p, False, None, dst, at))
            continue
        arrived, n = landed[id(p.arriving)], slabs(p.keep.shape)
        if cut == "relay":
            dst, at = message(p.steps[1][0], 2 * n)
            plan.append(("fresh", source(p.keep), 0, p.keep.shape, dst, at))
            plan.append(("move", source(arrived), p.place + n, n, dst, at + n))
            p.got.append((arrived, p.place))
            results.append((p, True, None, dst, at))
        elif cut == "land":
            p.got += [(arrived, p.place), (arrived, p.place + n)]
            results.append((p, True, None, None, None))
        else:
            after = shape_after(p.keep.shape, cut)
            dst, at = message(p.steps[1][0], slabs(after)) if cut != "done" else (None, None)
            stay = len(partners) + len(stays)
            stays.append(after)
            plan.append(("add", source(p.keep), source(arrived), p.place, p.keep.shape, cut, stay, dst, at))
            results.append((p, True, stay, dst, at))
    outs = []
    if plan:
        shapes = [(rows_of[q], LANES) for q in partners] + stays
        size = sum(x.size for x in ins) + sum(a * b for a, b in shapes)
        outs = pl.pallas_call(
            functools.partial(engine_kernel, plan, len(ins)),
            out_shape=[sds(x) for x in shapes],
            in_specs=[pl.BlockSpec(memory_space=pltpu.VMEM)] * len(ins),
            out_specs=[pl.BlockSpec(memory_space=pltpu.VMEM)] * len(shapes),
            compiler_params=pltpu.CompilerParams(vmem_limit_bytes=2 * size + 4 * MIB),
            cost_estimate=pl.CostEstimate(flops=LONG, bytes_accessed=COST, transcendentals=0),
        )(*ins)
        outs, guard = tie(outs, guard)
    sent = [exchange(outs[i], q) for i, q in enumerate(partners)]
    for p, stepped, stay, dst, at in results:
        if stepped:
            p.steps.pop(0)
        if stay is not None:
            p.keep = outs[stay]
        p.arriving, p.place = (sent[dst], at) if p.steps else (None, None)
    return guard


def wide_sum(keep, arrived, at):
    r, cols = keep.shape
    parts = [arrived[at + c * r : at + (c + 1) * r] for c in range(cols // LANES)]
    return keep[...].astype(F32) + jnp.concatenate(parts, axis=1).astype(F32)


def by_chip_kernel(places, ids, a_keep, b_keep, small_keep, arrived, *outs):
    a = a_keep[...].astype(F32)
    b, small = [wide_sum(ref, arrived, at) for ref, at in zip((b_keep, small_keep), places)]
    width = a.shape[1]
    half = a.shape[0] // 2
    n_chip = len(outs)
    rows = jnp.concatenate([a[half:], b[:half], b[half : 2 * half]], axis=1)
    size, part = 3 * width // n_chip, width // n_chip
    static = b[2 * half :]
    packed = static.shape[0] // n_chip
    count = half + packed
    for q in range(n_chip):
        top = jnp.concatenate([rows[:, q * size : (q + 1) * size], a[:half, q * part : (q + 1) * part]], axis=1)
        cols = static[:, q * part : (q + 1) * part]
        tail = jnp.concatenate([cols[m * packed : (m + 1) * packed] for m in range(n_chip)], axis=1)
        message = jnp.concatenate([top, tail], axis=0).astype(LOW)
        for rel, out in enumerate(outs):

            @pl.when(ids[PLACE] == (q ^ rel))
            def _(message=message, out=out):
                out[:count] = message

    for out in outs:
        out[count:] = small.astype(LOW)


def by_chip(ids, a, b, small):
    width = a.keep.shape[1]
    half = a.keep.shape[0] // 2
    rows = half + (b.keep.shape[0] - 2 * half) // 4 + small.keep.shape[0]
    args = (a.keep, b.keep, small.keep, b.arriving)
    return call(
        functools.partial(by_chip_kernel, (b.place, small.place)), (1,), ids, [whole(x.shape) for x in args],
        [whole((rows, width))] * 4, [sds((rows, width))] * 4, args, mib=24,
    )


def cut_cores_kernel(batches, n_small, ids, *refs):
    parts, glus, downs, own, send = refs[:4], refs[4 : 4 + CHUNKS], refs[4 + CHUNKS : 4 + 2 * CHUNKS], refs[-2], refs[-1]
    total = sum(ref[...].astype(F32) for ref in parts)
    rows, width = total.shape
    total, small = total[: rows - n_small], total[rows - n_small :]
    top = width // 8
    size, part = 3 * width // batches, width // batches
    first = ids[CORE] == 0

    def put(at, low, high):
        here = slice(at, at + low.shape[0])
        own[here, : low.shape[1]] = jnp.where(first, low, high).astype(LOW)
        send[here, : low.shape[1]] = jnp.where(first, high, low).astype(LOW)
        return at + low.shape[0]

    static = jnp.concatenate([total[top:, m * 2 * part : (m + 1) * 2 * part] for m in range(4)], axis=0)
    pair = [
        jnp.concatenate(
            [total[:top, c * size : (c + 1) * size], total[:top, 2 * size + c * part : 2 * size + (c + 1) * part]], axis=1
        )
        for c in range(2)
    ]
    at = put(0, *pair)
    glu = jnp.concatenate([g[...].astype(F32) for g in glus], axis=1)
    side = [
        jnp.concatenate([glu[:, (2 * k + c) * LANES : (2 * k + c + 1) * LANES] for k in range(CHUNKS)], axis=1)
        for c in range(2)
    ]
    at = put(at, *side)
    down = jnp.concatenate([d[...].astype(F32) for d in downs], axis=1)
    at = put(at, down[: down.shape[0] // 2], down[down.shape[0] // 2 :])
    tall = jnp.concatenate([small[:, : width // 2], small[:, width // 2 :]], axis=0)
    at = put(at, tall, tall)
    put(at, static[:, :part], static[:, part:])


def cut_cores(ids, parts, glus, downs, batches, n_small):
    rows, width = parts[0].shape
    top = width // 8
    shape = (
        top + glus[0].shape[0] + downs[0].shape[0] // 2 + 2 * n_small + 4 * (rows - n_small - top), CHUNKS * LANES
    )
    args = (*parts, *glus, *downs)
    return call(
        functools.partial(cut_cores_kernel, batches, n_small), (1,), ids, [whole(x.shape) for x in args], [whole(shape)] * 2,
        [sds(shape)] * 2, args, mib=16,
    )


def finish_kernel(n_small, ids, own, other, in_ref, out_ref, static_ref, glu_ref, down_ref, taps_ref, gain1_ref, gain2_ref):
    part, share = out_ref.shape[1], own.shape[1]
    top, half, tall = in_ref.shape[0] // 2, glu_ref.shape[0], 2 * n_small
    for ref, core in ((own, ids[CORE]), (other, 1 - ids[CORE])):
        rows = pl.ds(pl.multiple_of(core * top, 8), top)
        both = ref[:top].astype(F32)
        in_ref[rows, :] = both[:, : share - part]
        out_ref[rows, :] = both[:, share - part :]
        cols = pl.ds(pl.multiple_of(core * share, LANES), share)
        at = top
        glu_ref[:, cols] = ref[at : at + half].astype(F32)
        at += half
        down_ref[:, cols] = ref[at : at + part].astype(F32)
    at = top + half + part
    static = [ref[at + tall :, :part].astype(F32) for ref in (own, other)]
    first = ids[CORE] == 0
    static_ref[...] = jnp.concatenate(
        [jnp.where(first, static[0], static[1]), jnp.where(first, static[1], static[0])], axis=0
    ).T
    tall_sum = own[at : at + tall].astype(F32) + other[at : at + tall].astype(F32)
    small = jnp.concatenate([tall_sum[: tall // 2], tall_sum[tall // 2 :]], axis=1)
    gain1_ref[...], gain2_ref[...] = small[0], small[4]
    width = small.shape[1]
    for m, first in enumerate((1, 5, 8)):
        taps_ref[:, m * width : (m + 1) * width] = small[first : first + 3]


def finish(ids, own, other, width, count, batches, n_small):
    part = width // batches
    rows = width // 4
    shapes = [
        (rows, 3 * part), (rows, part), (part, count // 4), (rows, 2 * own.shape[1]), (part, 2 * own.shape[1]),
        (3, 3 * width), (width,), (width,),
    ]
    return call(
        functools.partial(finish_kernel, n_small), (1,), ids, [whole(own.shape)] * 2, [whole(x) for x in shapes], [sds(x, F32) for x in shapes],
        (own, other), mib=16,
    )


def add_low(a, b):
    return (a.astype(F32) + b.astype(F32)).astype(LOW)


def seq_sums(keep, send):
    part = add_low(keep, exchange(send, first_side))
    return add_low(part[0], exchange(part[1], second_side))


def spread_sum(x, core, rows, dim):
    x = x.astype(F32)
    zero = jnp.zeros_like(x)
    low, high = jnp.where(core == 0, x, zero), jnp.where(core == 0, zero, x)
    both = jnp.concatenate([low, high], axis=dim)
    return lax.psum_scatter(both, "batch", scatter_dimension=1 - rows, tiled=True)


def on_device(
    inputs,
    lengths,
    norm1_gain,
    in_weight,
    short_taps,
    static_kernel,
    out_weight,
    norm2_gain,
    glu_weight,
    down_weight,
    cotangent,
):
    span, n_slots, width = inputs.shape
    n_seq, n_batch = lax.axis_size("seq"), lax.axis_size("batch")
    seq, batch = lax.axis_index("seq"), lax.axis_index("batch")
    core, place = batch % 2, batch // 2
    paired = n_batch == 8
    total_pos = span * n_seq
    slots = n_slots // n_seq
    tokens = slots * total_pos
    tables = [jnp.asarray(t) for t in half_tables(total_pos)]
    gain1, gain2 = norm1_gain[None], norm2_gain[None]

    block = jnp.arange(4, dtype=jnp.int32)
    swap = lambda rel: (rel % 2) * 2 + rel // 2
    rel = block ^ seq
    row_at = jnp.where(core == 0, swap(rel), rel)
    chip_at = swap(block ^ place) if paired else block
    col_at = row_at if paired else block
    mine = jnp.arange(n_slots)[None, :] == (seq * slots + jnp.arange(slots))[:, None]
    own_lengths = jnp.sum(jnp.where(mine, lengths[None, :], 0), axis=1)
    head = jnp.stack([seq, core, place if paired else jnp.zeros_like(place)]).astype(jnp.int32)
    ids = jnp.concatenate([head, own_lengths, row_at, chip_at, col_at])

    x_turned = turn(ids, inputs, True)
    x_sent = [x_turned[s * n_seq : (s + 1) * n_seq] for s in range(slots)]
    x_blocks = [
        [sent[0]] + [exchange(sent[r], blocks_of(r)) for r in range(1, n_seq)] for sent in x_sent
    ]
    ct_turned = turn(ids, cotangent, False)
    weights = (in_weight, static_kernel, *tables, out_weight, short_taps, gain1, gain2)

    saved, n2_parts, n2_others = None, [], []
    flat = lambda a: a.reshape(-1, width)
    for s in range(slots):
        if s == 0:
            x_blocks[0], ct_turned = tie(x_blocks[0], ct_turned)
            ct_blocks = [ct_turned[0]] + [exchange(ct_turned[r], blocks_of(r)) for r in range(1, n_seq - 1)]
        if s == 1:
            x_blocks, ct_blocks, last, saved = tie(x_blocks, ct_blocks, ct_turned[n_seq - 1], saved)
            ct_blocks.append(exchange(last, blocks_of(n_seq - 1)))
            ct_others = [exchange(flat(c), across) for c in ct_blocks[:-1]]
        *saved, n2 = mixer_forward(ids, s, slots, x_blocks[s], weights, saved)
        n2_parts.append(n2.reshape(total_pos, width))
        n2_others.append(exchange(n2_parts[-1], across))
    ct_others.append(exchange(flat(ct_blocks[-1]), across))
    ct_parts = [flat(c) for c in ct_blocks] + ct_others
    p_all, spec, conv, gated, normed, x_whole, residual = saved
    n2_parts = n2_parts + n2_others

    pieces, chunks, shared = [], [], []
    chip_steps, seq_steps, cuts = (next_chip, far_chip), (first_side, second_side), ("rows", "lanes", "lanes", "done")
    for ks in GROUPS:
        out = glu_chunks(ids, ks, n2_parts, ct_parts, glu_weight, down_weight, shared, n_seq)
        shared = out[-4:]
        for i in range(len(ks)):
            parts = out[4 * i : 4 * i + 4]
            chunks.append(parts)
            if paired:
                pieces.append(Piece(*parts[:2], zip(seq_steps + chip_steps, cuts)))
                pieces.append(Piece(*parts[2:], zip(chip_steps + seq_steps, cuts)))
        ct_parts, shared = boundary(ids, pieces, (ct_parts, shared))
    ff_pieces = list(pieces)
    grads, hiddens, w_glus, w_downs = shared
    out_own, out_sent = halves_product(ids, hiddens, w_downs, 0)
    out_other = exchange(out_sent, across)
    grads, out_sent = tie(grads, out_sent)
    n2g_own, n2g_sent = halves_product(ids, grads, w_glus, 1)
    n2g_other = exchange(n2g_sent, across)
    out_other, n2g_sent = tie(out_other, n2g_sent)
    stay, later, sent = combine(ids, out_own, out_other, residual)
    moved = Piece(flat(later), flat(sent), [(first_side, "relay"), (second_side, "land")])
    pieces.append(moved)
    n2g_own = boundary(ids, pieces, n2g_own)
    residual_grad, conv_grad, pg_gate, small_out, a_keep, a_send = back_out(
        ids, n2g_own, n2g_other, residual, ct_blocks, gated, conv, p_all, normed, out_weight, short_taps, gain2
    )
    conv_grad, pg_gate = boundary(ids, pieces, (conv_grad, pg_gate))
    sum_steps = [(across, "rows"), (first_side, "rows"), (second_side, "done")]
    a = Piece(flat(a_keep), flat(a_send), sum_steps, alone=True)
    if paired:
        pieces.append(a)
    pg_rest, small_conv, b_keep, b_send = back_conv(ids, conv_grad, spec, p_all, normed, tables, short_taps)
    pg_rest, pg_gate = boundary(ids, pieces, (pg_rest, pg_gate))
    b = Piece(flat(b_keep), flat(b_send), sum_steps, alone=True)
    if paired:
        pieces.append(b)
    gain_in, *x_sent = back_in(ids, pg_gate, pg_rest, x_whole, residual_grad, in_weight, gain1)
    x_sent = boundary(ids, pieces, x_sent)
    output = unturn(ids, [stay] + [ref for ref, _ in moved.got], LOW, tuple(at for _, at in moved.got))
    small = jnp.concatenate([gain_in, small_out, small_conv], axis=0)
    n_small = small.shape[0] + -small.shape[0] % 16
    if paired:
        small = jnp.pad(small, ((0, n_small - small.shape[0]), (0, 0))).astype(LOW)
        small = Piece(small, small, [(first_side, "all"), (second_side, "all")], alone=True)
        pieces.append(small)
        x_sent, output = boundary(ids, pieces, (x_sent, output))
        own, *sent = by_chip(ids, a, b, small)
        own, x_sent = tie(own, x_sent)
        got = [exchange(x, lambda s, b, rel=rel: (s, b ^ (2 * rel))) for rel, x in enumerate(sent, 1)]
        x_got = [x_sent[0]] + [exchange(x_sent[r], blocks_of(r)) for r in range(1, n_seq)]
        own, sent = cut_cores(
            ids, (own, *got), [p.keep for p in ff_pieces[0::2]], [p.keep for p in ff_pieces[1::2]], n_batch, n_small
        )
        sent, x_got = tie(sent, x_got)
        theirs = exchange(sent, across)
        input_grad = unturn(ids, x_got, F32)
        theirs, input_grad = tie(theirs, input_grad)
        total_in, total_out, total_static, total_glu, total_down, total_taps, *gains = finish(
            ids, own, theirs, width, total_pos, n_batch, n_small
        )
        total_static, total_down = total_static.T, total_down.T
    else:
        x_got = [x_sent[0]] + [exchange(x_sent[r], blocks_of(r)) for r in range(1, n_seq)]
        pieces = [a, b]
        while a.steps:
            boundary(ids, pieces, ())
        top = width // 8
        in_rows = jnp.concatenate([a.keep[top:], b.keep[:top], b.keep[top : 2 * top]], axis=1)
        total_in = spread_sum(in_rows, core, 0, 0)
        total_out = spread_sum(a.keep[:top], core, 0, 0)
        total_static = spread_sum(b.keep[2 * top :], core, 0, 0)
        side = n_seq // 2
        halves = lambda x: x.reshape(2, x.shape[0] // 2, x.shape[1])
        glu = jnp.stack(
            [seq_sums(halves(c[0]), halves(c[1])).reshape(-1, side, 2, side, LANES) for c in chunks], axis=4
        )
        glu = glu.transpose(0, 2, 1, 3, 4, 5).reshape(-1, 2 * n_seq, 1, CHUNKS * LANES)
        mine = (jnp.arange(2) == core)[:, None]
        glu = jnp.where(mine, glu, 0).astype(F32).reshape(glu.shape[0], -1)
        total_glu = lax.psum_scatter(glu, "batch", scatter_dimension=1, tiled=True)
        joined = [jnp.concatenate([c[2], c[3]], axis=int(c[2].shape[0] == width)) for c in chunks]
        down = jnp.stack([d.reshape(width, n_seq, LANES) for d in joined], axis=2)
        down = down.reshape(width, n_seq, 1, CHUNKS * LANES)
        down = jnp.where(mine, down, 0).astype(F32).reshape(width, -1)
        down = lax.psum_scatter(down, "batch", scatter_dimension=0, tiled=True)
        total_down = lax.psum_scatter(down, "seq", scatter_dimension=1, tiled=True).T

        small = lax.psum(small, ("seq", "batch"))
        gains = jnp.stack([small[0], small[4]])
        total_taps = jnp.concatenate([small[1:4], small[5:8], small[8:11]], axis=1)
        input_grad = unturn(ids, x_got, F32)
    return (
        output,
        input_grad,
        gains[0],
        total_in,
        total_taps,
        total_static,
        total_out,
        gains[1],
        total_glu,
        total_down,
    )


def solution(mesh):
    return jax.shard_map(
        on_device,
        mesh=mesh,
        in_specs=(
            P("seq", "batch", None),
            P("batch"),
            P(),
            P(),
            P(),
            P(),
            P(),
            P(),
            P(),
            P(),
            P("seq", "batch", None),
        ),
        out_specs=(
            P("seq", "batch", None),
            P("seq", "batch", None),
            P(),
            P("seq", "batch"),
            P(),
            P("seq", "batch"),
            P("seq", "batch"),
            P(),
            P("seq", "batch"),
            P("seq", "batch"),
        ),
        check_vma=False,
    )
```

```python
import functools
import math

import jax
import jax.numpy as jnp
import numpy as np
from jax import lax
from jax.experimental import pallas as pl
from jax.experimental.pallas import tpu as pltpu
from jax.sharding import PartitionSpec as P

F32 = jnp.float32
LOW = jnp.bfloat16
CHUNKS = 3
LANES = 128
ROOT = math.sqrt(2.0 / math.pi)
CUBE = 0.044715
MIB = 2**20
COST = 1000
LONG = 3 * 10**10
GLU_MIB = 50
GROUPS = ((0, 1), (2,))
MIX_MIB = 44
BACK_MIB = 46
ANY = pl.BlockSpec(memory_space=pl.ANY)

SEQ, CORE, PLACE, LENGTH, ROW_AT, CHIP_AT, COL_AT = 0, 1, 2, 3, 5, 9, 13


def half_tables(count):
    steps = np.arange(count)
    angle = (np.arange(count // 2)[:, None] * steps[None, :] % count) * (2.0 * math.pi / count)
    low_rows = np.cos(angle)
    high_rows = -np.sin(angle)
    high_rows[0] = np.where(steps % 2 == 0, 1.0, -1.0)
    table = np.concatenate([low_rows, high_rows], axis=0)
    weight = np.where(steps % (count // 2) == 0, 1.0, 2.0) / count
    return table.astype(LOW), (table * weight[:, None]).T.astype(LOW)


def dot(a, b, ca=1, cb=0):
    return lax.dot_general(a, b, (((ca,), (cb,)), ((), ())), preferred_element_type=F32)


def gelu_parts(z):
    square = z * z
    tanh = jnp.tanh(z * (ROOT + (ROOT * CUBE) * square))
    plus = 0.5 + 0.5 * tanh
    act = z * plus
    return act, plus + act * (1.0 - tanh) * (ROOT + (3.0 * ROOT * CUBE) * square)


def gelu(z):
    return z * (0.5 + 0.5 * jnp.tanh(z * (ROOT + (ROOT * CUBE) * (z * z))))


def standardize(values):
    centred = values - jnp.mean(values, axis=-1, keepdims=True)
    inverse = lax.rsqrt(jnp.mean(centred * centred, axis=-1, keepdims=True) + 1e-05)
    return centred * inverse, inverse


def norm_back(grad_in, standard, inverse, gain_vec):
    scaled = grad_in * gain_vec
    inner = (
        scaled
        - jnp.mean(scaled, axis=-1, keepdims=True)
        - standard * jnp.mean(scaled * standard, axis=-1, keepdims=True)
    )
    return inverse * inner


def shifts(a):
    count = a.shape[0]
    row = lax.broadcasted_iota(jnp.int32, a.shape, 0)
    before = jnp.where(row == 0, 0.0, pltpu.roll(a, 1, 0))
    after = jnp.where(row == count - 1, 0.0, pltpu.roll(a, count - 1, 0))
    return before, after


def mix(low, taps):
    wide = low.astype(F32)
    before, after = shifts(wide)
    return taps[0:1] * before + taps[1:2] * wide + taps[2:3] * after


def mix_back(grad, low, taps):
    wide = low.astype(F32)
    before, after = shifts(grad)
    sums = [jnp.sum(side * wide, axis=0, keepdims=True) for side in (after, grad, before)]
    return sums, (taps[0:1] * after + taps[1:2] * grad + taps[2:3] * before).astype(LOW)


def spectrum_product(a, b, sign):
    half = a.shape[0] // 2
    ar, ai, br, bi = a[:half], a[half:], b[:half], b[half:]
    first = lax.broadcasted_iota(jnp.int32, ar.shape, 0) == 0
    both = ai * bi
    re = ar * br - jnp.where(first, 0.0, sign * both)
    im = jnp.where(first, both, ai * br + sign * (ar * bi))
    return jnp.concatenate([re.astype(LOW), im.astype(LOW)], axis=0)


def live_mask(length, count):
    return (lax.broadcasted_iota(jnp.int32, (count, 1), 0) < length).astype(F32)


def whole(shape):
    return pl.BlockSpec(shape, lambda *at: (0,) * len(shape))


def kept(shape):
    return pl.BlockSpec(shape, lambda *at: (0,) * len(shape), pipeline_mode=pl.Buffered(1))


def in_hbm(arrays):
    return [pltpu.with_memory_space_constraint(a, pltpu.HBM) for a in arrays]


def sds(shape, dtype=LOW):
    return jax.ShapeDtypeStruct(shape, dtype)


def call(body, grid, ids, in_specs, out_specs, out_shape, args, scratch=(), aliases=None, mib=12, cost=COST):
    return pl.pallas_call(
        body,
        grid_spec=pltpu.PrefetchScalarGridSpec(
            num_scalar_prefetch=1, grid=grid, in_specs=in_specs, out_specs=out_specs, scratch_shapes=list(scratch)
        ),
        out_shape=out_shape,
        compiler_params=pltpu.CompilerParams(vmem_limit_bytes=mib * MIB),
        input_output_aliases=aliases or {},
        cost_estimate=pl.CostEstimate(flops=cost, bytes_accessed=COST, transcendentals=0),
    )(ids, *args)


def turn_kernel(by_slot, ids, x_ref, *refs):
    outs, held = refs[:-1], refs[-1]
    held[...] = jnp.swapaxes(x_ref[...].astype(F32), 0, 1).astype(LOW)
    n_seq = 4
    own = held.shape[0] // n_seq
    for r in range(n_seq):
        at = (ids[SEQ] ^ r) * own
        for s in range(own):
            if by_slot:
                outs[s * n_seq + r][...] = held[at + s]
            else:
                outs[r][s] = held[at + s]


def turn(ids, x, by_slot):
    span, slots, width = x.shape
    own = slots // 4
    shape = (span, width) if by_slot else (own, span, width)
    n_out = slots if by_slot else 4
    return call(
        functools.partial(turn_kernel, by_slot), (1,), ids, [whole(x.shape)], [whole(shape)] * n_out,
        [sds(shape)] * n_out, in_hbm([x]), [pltpu.VMEM((slots, span, width), LOW)], mib=20,
    )


def unturn_kernel(places, ids, *refs):
    blocks, out, held = refs[:-2], refs[-2], refs[-1]
    slots, span, width = held.shape
    own = slots // 4
    rels = range(4) if places is None else (0, 1 + ids[CORE], 2 - ids[CORE], 3)
    for i, (rel, block) in enumerate(zip(rels, blocks)):
        for s in range(own):
            to = (ids[SEQ] ^ rel) * own + s
            if places is None or i == 0:
                held[to] = block[s].astype(F32)
            else:
                for c in range(width // LANES):
                    row = places[i - 1] + (c * own + s) * span
                    held[to, :, c * LANES : (c + 1) * LANES] = block[row : row + span].astype(F32)
    out[...] = jnp.swapaxes(held[...], 0, 1).astype(out.dtype)


def unturn(ids, blocks, dtype, places=None):
    own, span, width = blocks[0].shape
    slots = own * 4
    return call(
        functools.partial(unturn_kernel, places),
        (1,),
        ids,
        [whole(b.shape) for b in blocks],
        whole((span, slots, width)),
        sds((span, slots, width), dtype),
        blocks,
        [pltpu.VMEM((slots, span, width), F32)],
        mib=32,
    )


class Copies:
    def __init__(self, sems):
        self.sems, self.made = sems, []

    def start(self, src, to):
        copy = pltpu.make_async_copy(src, to, self.sems.at[len(self.made)])
        copy.start()
        self.made.append(copy)
        return copy

    def finish(self):
        for copy in self.made:
            copy.wait()


def mixer_kernel(
    slot, ids, x0, x1, x2, x3, in_weight, static, table, inverse, w_out, taps, gain1, gain2, *refs
):
    p_hbm, spec_hbm, conv_hbm, gated_hbm, normed_hbm, x_hbm, residual_hbm, n2_hbm = refs[-22:-14]
    (x, w_in, static_low, tab, inv, w_o, p, spec, conv, gated, normed, total, sems_in, sems_out) = refs[-14:]
    blocks = (x0, x1, x2, x3)
    count, width = x.shape
    span = count // len(blocks)
    scale = count**-0.5
    loads, stores = Copies(sems_in), Copies(sems_out)
    place = [pl.ds(pl.multiple_of((ids[SEQ] ^ r) * span, span), span) for r in range(len(blocks))]
    x_copies = [loads.start(block, x.at[place[r]]) for r, block in enumerate(blocks)]
    w_copy, *t_copies = [
        loads.start(src, to)
        for src, to in ((in_weight, w_in), (table, tab), (static, static_low), (inverse, inv), (w_out, w_o))
    ]
    for copy in x_copies:
        copy.wait()
    stores.start(x, x_hbm.at[slot])
    for q in range(len(blocks)):
        rows = slice(q * span, (q + 1) * span)
        wide = x[rows].astype(F32)
        standard, _ = standardize(wide)
        normed[rows] = (standard * gain1[...]).astype(LOW)
        total[rows] = wide
    stores.start(normed, normed_hbm.at[slot])
    live = live_mask(ids[LENGTH + slot], count)
    w_copy.wait()
    p[...] = dot(normed[...], w_in[...]).astype(LOW)
    stores.start(p, p_hbm.at[slot])
    for copy in t_copies:
        copy.wait()
    static_spec = dot(tab[...], static_low[...].astype(LOW))
    value = (live * mix(p[:, width : 2 * width], taps[:, width : 2 * width])).astype(LOW)
    vs = dot(tab[...], value)
    cond = (live * gelu(mix(p[:, 2 * width :], taps[:, 2 * width :]))).astype(LOW)
    ks = static_spec + scale * dot(tab[...], cond)
    spec[:, :width], spec[:, width:] = vs.astype(LOW), ks.astype(LOW)
    stores.start(spec, spec_hbm.at[slot])
    conv[...] = dot(inv[...], spectrum_product(vs, ks, 1.0)).astype(LOW)
    stores.start(conv, conv_hbm.at[slot])
    gated[...] = (live * mix(p[:, :width], taps[:, :width]) * conv[...].astype(F32)).astype(LOW)
    stores.start(gated, gated_hbm.at[slot])
    total[...] += dot(gated[...], w_o[...])
    for r in range(len(blocks)):
        stores.start(total.at[place[r]], residual_hbm.at[slot, r])
    n2 = x
    stores.made[0].wait()
    for q in range(len(blocks)):
        rows = slice(q * span, (q + 1) * span)
        standard, _ = standardize(total[rows])
        n2[rows] = (standard * gain2[...]).astype(LOW)
    for r in range(len(blocks)):
        stores.start(n2.at[place[r]], n2_hbm.at[r])
    for copy in stores.made[1:]:
        copy.wait()


def mixer_forward(ids, slot, slots, x_blocks, weights, before):
    span, width = x_blocks[0].shape
    count = span * len(x_blocks)
    cols = (3, 2, 1, 1, 1, 1)
    rel = (len(x_blocks), span, width)
    *large, taps, gain1, gain2 = weights
    args = (*x_blocks, *in_hbm(large), taps, gain1, gain2)
    in_specs = [ANY] * (len(x_blocks) + len(large)) + [kept(a.shape) for a in (taps, gain1, gain2)]
    aliases = {}
    if before is not None:
        aliases = {1 + len(args) + i: i for i in range(len(before))}
        args, in_specs = args + tuple(before), in_specs + [ANY] * len(before)
    return call(
        functools.partial(mixer_kernel, slot),
        (1,),
        ids,
        in_specs,
        [ANY] * 8,
        [pltpu.HBM((slots, count, m * width), LOW) for m in cols] + [pltpu.HBM((slots, *rel), F32), sds(rel)],
        args,
        [
            pltpu.VMEM((count, width), LOW),
            pltpu.VMEM((width, 3 * width), LOW),
            pltpu.VMEM((count, width), F32),
            pltpu.VMEM((count, count), LOW),
            pltpu.VMEM((count, count), LOW),
            pltpu.VMEM((width, width), LOW),
            pltpu.VMEM((count, 3 * width), LOW),
            pltpu.VMEM((count, 2 * width), LOW),
            pltpu.VMEM((count, width), LOW),
            pltpu.VMEM((count, width), LOW),
            pltpu.VMEM((count, width), LOW),
            pltpu.VMEM((count, width), F32),
            pltpu.SemaphoreType.DMA((9,)),
            pltpu.SemaphoreType.DMA((14,)),
        ],
        aliases,
        mib=MIX_MIB,
        cost=LONG,
    )


def glu_kernel(ks, n_seq, slots, ids, *refs):
    n_blocks, n = 4, len(ks)
    n2_parts, ct_parts = refs[: 2 * slots], refs[2 * slots : 2 * slots + 2 * n_blocks]
    glu_hbm, down_hbm = refs[2 * (slots + n_blocks) :][:2]
    parts_out = refs[-16 - 4 * n : -16]
    (
        gu_hbm, hidden_hbm, w_glu_hbm, w_down_hbm,
        n2, ct, w_glus, w_downs, hidden, gu, g_low, d_low, n2_sems, ct_sems, w_sems, out_sems,
    ) = refs[-16:]
    rows = n2.shape[0] // 2
    span = rows // n_blocks // slots
    units = w_downs.shape[1]
    halves = [pl.ds(h * rows, rows) for h in range(2)]

    def load(h):
        copies = []
        for s in range(slots):
            for r in range(n_blocks):
                copies.append(
                    pltpu.make_async_copy(
                        n2_parts[h * slots + s].at[pl.ds(r * span, span)],
                        n2.at[pl.ds(h * rows + (r * slots + s) * span, span)],
                        n2_sems.at[(h * slots + s) * n_blocks + r],
                    )
                )
        return copies, [
            pltpu.make_async_copy(
                ct_parts[h * n_blocks + r],
                ct.at[pl.ds(h * rows + r * slots * span, slots * span)],
                ct_sems.at[h * n_blocks + r],
            )
            for r in range(n_blocks)
        ]

    loads = [load(h) for h in range(2)]
    glu_copies, down_copies = [], []
    for i, k in enumerate(ks):
        starts = [pl.multiple_of(((2 * m + ids[CORE]) * CHUNKS + k) * LANES, LANES) for m in range(2 * n_seq)]
        glu_copies.append(
            [
                pltpu.make_async_copy(
                    glu_hbm.at[:, pl.ds(col, LANES)],
                    w_glus.at[i, :, pl.ds(m * LANES, LANES)],
                    w_sems.at[3 * n_seq * i + m],
                )
                for m, col in enumerate(starts)
            ]
        )
        down_copies.append(
            [
                pltpu.make_async_copy(
                    down_hbm.at[pl.ds(row, LANES)],
                    w_downs.at[i, pl.ds(m * LANES, LANES)],
                    w_sems.at[3 * n_seq * i + 2 * n_seq + m],
                )
                for m, row in enumerate(starts[:n_seq])
            ]
        )
    for copy in loads[0][0] + glu_copies[0] + down_copies[0] + loads[0][1] + loads[1][0] + loads[1][1]:
        copy.start()
    for i in range(1, n):
        for copy in glu_copies[i] + down_copies[i]:
            copy.start()
    outs = []

    def store(src, to):
        copy = pltpu.make_async_copy(src, to, out_sems.at[len(outs)])
        copy.start()
        outs.append(copy)

    for i, k in enumerate(ks):
        glu_keep, glu_send, down_keep, down_send = parts_out[4 * i : 4 * i + 4]
        w_glu, w_down = w_glus.at[i], w_downs.at[i]
        for copy in (loads[0][0] if i == 0 else []) + glu_copies[i]:
            copy.wait()
        gate_ups = [dot(n2[halves[0]], w_glu[...])]
        for copy in down_copies[i] + (loads[0][1] + loads[1][0] + loads[1][1] if i == 0 else outs[8 * i - 8 : 8 * i]):
            copy.wait()
        gate_ups.append(dot(n2[halves[1]], w_glu[...]))
        for h, gate_up in enumerate(gate_ups):
            here = halves[h]
            gate, up = gate_up[:, :units], gate_up[:, units:]
            hidden_grad = dot(ct[here], w_down[...], 1, 1)
            act, slope = gelu_parts(gate)
            hidden[here] = (act * up).astype(LOW)
            gu[here, :units] = (hidden_grad * up * slope).astype(LOW)
            gu[here, units:] = (hidden_grad * act).astype(LOW)
        mine, wide = pl.ds(k * units, units), pl.ds(2 * k * units, 2 * units)
        store(w_glu, w_glu_hbm.at[:, wide])
        store(w_down, w_down_hbm.at[mine])
        store(hidden, hidden_hbm.at[:, mine])
        store(gu, gu_hbm.at[:, wide])
        g_sum = dot(n2[...], gu[...], 0, 0)
        side = units // 2
        size = g_sum.shape[0] // 4
        for q in range(4):
            here = pl.ds(pl.multiple_of(ids[ROW_AT + q] * size, size), size)
            for high in range(2):
                for g in range(2):
                    at = (high ^ (ids[PLACE] % 2)) * 2 + (g ^ (ids[PLACE] // 2 % 2))
                    from_col = g * units + high * side
                    part = g_sum[q * size : (q + 1) * size, from_col : from_col + side]
                    g_low[here, pl.ds(pl.multiple_of(at * side, side), side)] = part.astype(LOW)
        half = d_low.shape[0] // 2
        store(g_low.at[pl.ds(half, half)], glu_send)
        store(g_low.at[pl.ds(0, half)], glu_keep)
        d_sum = dot(ct[...], hidden[...], 0, 0)
        for q in range(4):
            here = pl.ds(pl.multiple_of(ids[CHIP_AT + q] * size, size), size)
            for s in range(4):
                part = d_sum[q * size : (q + 1) * size, s * LANES : (s + 1) * LANES]
                d_low[here, pl.ds(pl.multiple_of(ids[COL_AT + s] * LANES, LANES), LANES)] = part.astype(LOW)
        store(d_low.at[pl.ds(half, half)], down_send)
        store(d_low.at[pl.ds(0, half)], down_keep)
    for copy in outs[8 * n - 8 :]:
        copy.wait()


def glu_chunks(ids, ks, n2_parts, ct_parts, glu_weight, down_weight, shared, n_seq):
    width, units = glu_weight.shape[0], n_seq * LANES
    slots, n_blocks, n = len(n2_parts) // 2, 4, len(ks)
    tokens = sum(p.shape[0] for p in n2_parts)
    here = [pltpu.with_memory_space_constraint(x, pltpu.VMEM) for x in n2_parts[slots:]] if not shared else n2_parts[slots:]
    args = (*n2_parts[:slots], *here, *ct_parts, *in_hbm((glu_weight, down_weight)), *shared)
    aliases = {1 + len(args) - len(shared) + i: 4 * n + i for i in range(len(shared))}
    return call(
        functools.partial(glu_kernel, ks, n_seq, slots),
        (1,),
        ids,
        [ANY] * len(args),
        [ANY] * (4 * n + 4),
        ([pltpu.VMEM((width // 2, 2 * units), LOW)] * 2 + [pltpu.VMEM((width // 2, units), LOW)] * 2) * n
        + [
            pltpu.HBM(x, LOW)
            for x in (
                (tokens, 2 * CHUNKS * units),
                (tokens, CHUNKS * units),
                (width, 2 * CHUNKS * units),
                (CHUNKS * units, width),
            )
        ],
        args,
        [
            pltpu.VMEM((tokens, width), LOW),
            pltpu.VMEM((tokens, width), LOW),
            pltpu.VMEM((n, width, 2 * units), LOW),
            pltpu.VMEM((n, units, width), LOW),
            pltpu.VMEM((tokens, units), LOW),
            pltpu.VMEM((tokens, 2 * units), LOW),
            pltpu.VMEM((width, 2 * units), LOW),
            pltpu.VMEM((width, units), LOW),
            pltpu.SemaphoreType.DMA((2 * slots * n_blocks,)),
            pltpu.SemaphoreType.DMA((2 * n_blocks,)),
            pltpu.SemaphoreType.DMA((3 * n_seq * n,)),
            pltpu.SemaphoreType.DMA((8 * n,)),
        ],
        aliases,
        mib=GLU_MIB,
        cost=LONG,
    )


def halves_product_kernel(cb, ids, rows_ref, weight, own, other):
    result = dot(rows_ref[...], weight[...], 1, cb)

    @pl.when(pl.program_id(0) < pl.num_programs(0) // 2)
    def _():
        other[...] = result.astype(LOW)

    @pl.when(pl.program_id(0) >= pl.num_programs(0) // 2)
    def _():
        own[...] = result


def halves_product(ids, values, weight, cb, rows=512):
    tokens, size = values.shape
    width = weight.shape[1 - cb]
    per = tokens // 2 // rows
    return call(
        functools.partial(halves_product_kernel, cb),
        (2 * per,),
        ids,
        [pl.BlockSpec((rows, size), lambda i, ids: ((i + per) % (2 * per), 0)), kept(weight.shape)],
        [
            pl.BlockSpec((rows, width), lambda i, ids: (jnp.maximum(i - per, 0), 0)),
            pl.BlockSpec((rows, width), lambda i, ids: (jnp.minimum(i, per - 1), 0)),
        ],
        [sds((tokens // 2, width), F32), sds((tokens // 2, width))],
        in_hbm((values, weight)),
        mib=32,
        cost=LONG,
    )


def combine_kernel(ids, own, other, residual, stay, later, send):
    span = stay.shape[1]
    second, first = 2 - ids[CORE], 1 + ids[CORE]
    for r, out, at in ((0, stay, 0), (second, later, 0), (first, send, 0), (3, send, 1)):
        value = (residual[0, r] + (own[r, 0] + other[r, 0].astype(F32))).astype(LOW)
        if out is send:
            send[at, 0] = value
        else:
            out[0] = value


def combine(ids, own, other, residual):
    slots, n_blocks, span, width = residual.shape
    rows = pl.BlockSpec((n_blocks, 1, span, width), lambda s, ids: (0, s, 0, 0))
    block = pl.BlockSpec((1, span, width), lambda s, ids: (s, 0, 0))
    own, other = [x.reshape(n_blocks, slots, span, width) for x in (own, other)]
    return call(
        combine_kernel,
        (slots,),
        ids,
        [rows, rows, pl.BlockSpec((1, n_blocks, span, width), lambda s, ids: (s, 0, 0, 0))],
        [block, block, pl.BlockSpec((2, 1, span, width), lambda s, ids: (0, s, 0, 0))],
        [sds((slots, span, width))] * 2 + [sds((2, slots, span, width))],
        (own, other, residual),
        mib=16,
    )


def place_halves(ids, grad, at, keep, send):
    size = grad.shape[0] // 8
    for q in range(4):
        to = ids[ROW_AT + q]
        for c in range(2):
            rows = grad[(2 * q + c) * size : (2 * q + c + 1) * size]

            @pl.when(ids[CORE] == c)
            def _(rows=rows, to=to):
                keep[to, at : at + size] = rows

            @pl.when(ids[CORE] != c)
            def _(rows=rows, to=(to % 2) * 2 + to // 2):
                send[to, at : at + size] = rows


def accumulate(step, ref, value):
    @pl.when(step == 0)
    def _():
        ref[...] = value

    @pl.when(step > 0)
    def _():
        ref[...] += value


def back_out_kernel(
    ids, n2g_own_hbm, n2g_other_hbm, residual_hbm, ct0, ct1, ct2, ct3, gated_hbm, conv_hbm, p_hbm, normed_hbm, w_hbm,
    taps, gain2, residual_grad_hbm, conv_grad_hbm, pg_hbm, small, keep, send,
    n2g_own, n2g_other, residual, cot, gated, conv, p, normed, w_out, branch, conv_grad, pg, sems_in, sems_out,
):
    slots, n_blocks, span, width = residual.shape
    count = n_blocks * span
    loads, stores = Copies(sems_in), Copies(sems_out)
    early, late = [], []
    for s in range(slots):
        here = pl.ds(s * count, count)
        early.append(
            [loads.start(residual_hbm.at[s], residual.at[s])]
            + [loads.start(ref.at[s], cot.at[s, r]) for r, ref in enumerate((ct0, ct1, ct2, ct3))]
            + [loads.start(n2g_own_hbm.at[:, s], n2g_own.at[s]), loads.start(n2g_other_hbm.at[:, s], n2g_other.at[s])]
        )
        late.append(
            ([loads.start(w_hbm, w_out)] if s == 0 else [])
            + [loads.start(p_hbm.at[s, :, pl.ds(0, width)], p.at[here]), loads.start(conv_hbm.at[s], conv.at[here])]
        )
    last = [
        loads.start(ref.at[s], to.at[pl.ds(s * count, count)])
        for s in range(slots)
        for ref, to in ((gated_hbm, gated), (normed_hbm, normed))
    ]
    gain_grad, tap_sums = jnp.zeros((1, width), F32), None
    for s in range(slots):
        here = slice(s * count, (s + 1) * count)
        for copy in early[s]:
            copy.wait()
        for r in range(n_blocks):
            at = pl.multiple_of(s * count + (ids[SEQ] ^ r) * span, span)
            grad = n2g_own[s, r] + n2g_other[s, r].astype(F32)
            unit, inverse = standardize(residual[s, r])
            gain_grad += jnp.sum(grad * unit, axis=0, keepdims=True)
            value = cot[s, r].astype(F32) + norm_back(grad, unit, inverse, gain2[...])
            residual[s, r] = value
            branch[pl.ds(at, span), :] = value.astype(LOW)
        stores.start(residual.at[s], residual_grad_hbm.at[s])
        live = live_mask(ids[LENGTH + s], count)
        for copy in late[s]:
            copy.wait()
        gated_grad = live * dot(branch[here], w_out[...], 1, 1)
        conv_grad[here] = (gated_grad * mix(p[here], taps[...])).astype(LOW)
        sums, pg[here] = mix_back(gated_grad * conv[here].astype(F32), p[here], taps[...])
        tap_sums = sums if s == 0 else [x + y for x, y in zip(tap_sums, sums)]
        stores.start(conv_grad.at[pl.ds(s * count, count)], conv_grad_hbm.at[s])
        stores.start(pg.at[pl.ds(s * count, count)], pg_hbm.at[s])
    small[...] = jnp.concatenate(tap_sums + [gain_grad], axis=0)
    for copy in last:
        copy.wait()
    place_halves(ids, dot(gated[...], branch[...], 0, 0).astype(LOW), 0, keep, send)
    place_halves(ids, dot(normed[...], pg[...], 0, 0).astype(LOW), width // 8, keep, send)
    stores.finish()


def back_out(ids, n2g_own, n2g_other, residual, cot, gated, conv, p_all, normed, w_out, taps, gain2):
    slots, n_blocks, span, width = residual.shape
    count = n_blocks * span
    n2g_own, n2g_other = [x.reshape(n_blocks, slots, span, width) for x in (n2g_own, n2g_other)]
    part = (4, 2 * width // 8, width)
    args = (n2g_own, n2g_other, *in_hbm([residual]), *cot, *in_hbm((gated, conv, p_all, normed, w_out)))
    n_loads = slots * (1 + n_blocks + 2 + 2 + 2) + 1
    flat = (slots * count, width)
    return call(
        back_out_kernel,
        (1,),
        ids,
        [ANY] * len(args) + [kept((3, width)), kept((1, width))],
        [ANY] * 3 + [whole((4, width))] + [pl.BlockSpec(memory_space=pltpu.VMEM)] * 2,
        [
            pltpu.HBM(residual.shape, F32),
            pltpu.HBM((slots, count, width), LOW),
            pltpu.HBM((slots, count, width), LOW),
            sds((4, width), F32),
            pltpu.VMEM(part, LOW),
            pltpu.VMEM(part, LOW),
        ],
        (*args, taps, gain2),
        [
            pltpu.VMEM(residual.shape, F32),
            pltpu.VMEM(residual.shape, LOW),
            pltpu.VMEM(residual.shape, F32),
            pltpu.VMEM(residual.shape, LOW),
            *[pltpu.VMEM(flat, LOW)] * 4,
            pltpu.VMEM((width, width), LOW),
            *[pltpu.VMEM(flat, LOW)] * 3,
            pltpu.SemaphoreType.DMA((n_loads,)),
            pltpu.SemaphoreType.DMA((3 * slots,)),
        ],
        mib=BACK_MIB,
        cost=LONG,
    )


def back_conv_kernel(
    ids, conv_grad_hbm, spec_hbm, p_hbm, normed_hbm, table_hbm, inverse_hbm, t_value, t_cond,
    pg_hbm, small, keep, send,
    conv_grad, spec, p, normed, table, inverse, pg, sems_in, sems_out,
):
    width = t_value.shape[1]
    count = table.shape[0]
    slots = conv_grad.shape[0] // count
    scale = count**-0.5
    loads, stores = Copies(sems_in), Copies(sems_out)
    here_of = lambda s: pl.ds(s * count, count)
    first = [loads.start(table_hbm, table)]
    parts = []
    for s in range(slots):
        parts.append([loads.start(conv_grad_hbm.at[s], conv_grad.at[here_of(s)])])
        parts.append([loads.start(spec_hbm.at[s], spec.at[here_of(s)])])
        if s == 0:
            parts[-1].append(loads.start(inverse_hbm, inverse))
        parts.append([loads.start(p_hbm.at[s, :, pl.ds(width, 2 * width)], p.at[here_of(s)])])
    last = [loads.start(normed_hbm.at[s], normed.at[here_of(s)]) for s in range(slots)]
    tap_sums = static_total = None
    for s in range(slots):
        here = slice(s * count, (s + 1) * count)
        live = live_mask(ids[LENGTH + s], count)
        for copy in (first if s == 0 else []) + parts[3 * s]:
            copy.wait()
        gs = dot(table[...], conv_grad[here])
        for copy in parts[3 * s + 1]:
            copy.wait()
        value_low = spectrum_product(gs, spec[here, width:].astype(F32), -1.0)
        cond_low = spectrum_product(gs, spec[here, :width].astype(F32), -1.0)
        value_grad = live * dot(inverse[...], value_low)
        back = dot(inverse[...], cond_low)
        static_total = back if s == 0 else static_total + back
        for copy in parts[3 * s + 2]:
            copy.wait()
        sums_v, pg[here, :width] = mix_back(value_grad, p[here, :width], t_value[...])
        cond_grad = (live * scale) * back * gelu_parts(mix(p[here, width:], t_cond[...]))[1]
        sums_c, pg[here, width:] = mix_back(cond_grad, p[here, width:], t_cond[...])
        sums = sums_v + sums_c
        tap_sums = sums if s == 0 else [x + y for x, y in zip(tap_sums, sums)]
        stores.start(pg.at[here_of(s)], pg_hbm.at[s])
    small[...] = jnp.concatenate(tap_sums, axis=0)
    place_halves(ids, static_total.astype(LOW), width // 4, keep, send)
    for copy in last:
        copy.wait()
    total = dot(normed[...], pg[...], 0, 0).astype(LOW)
    place_halves(ids, total[:, :width], 0, keep, send)
    place_halves(ids, total[:, width:], width // 8, keep, send)
    stores.finish()


def back_conv(ids, conv_grad, spec, p_all, normed, tables, taps):
    slots, count, width = conv_grad.shape
    tap = lambda m: pl.BlockSpec((3, width), lambda i, ids, m=m: (0, m))
    part = (4, (2 * width + count) // 8, width)
    args = in_hbm((conv_grad, spec, p_all, normed, *tables))
    rows = slots * count
    return call(
        back_conv_kernel,
        (1,),
        ids,
        [ANY] * len(args) + [tap(1), tap(2)],
        [ANY, whole((6, width))] + [pl.BlockSpec(memory_space=pltpu.VMEM)] * 2,
        [
            pltpu.HBM((slots, count, 2 * width), LOW),
            sds((6, width), F32),
            pltpu.VMEM(part, LOW),
            pltpu.VMEM(part, LOW),
        ],
        (*args, taps, taps),
        [
            pltpu.VMEM((rows, width), LOW),
            pltpu.VMEM((rows, 2 * width), LOW),
            pltpu.VMEM((rows, 2 * width), LOW),
            pltpu.VMEM((rows, width), LOW),
            pltpu.VMEM((count, count), LOW),
            pltpu.VMEM((count, count), LOW),
            pltpu.VMEM((rows, 2 * width), LOW),
            pltpu.SemaphoreType.DMA((4 * slots + 2,)),
            pltpu.SemaphoreType.DMA((slots,)),
        ],
        mib=BACK_MIB,
        cost=LONG,
    )


def back_in_kernel(ids, pg_gate, pg_rest, x, residual_grad, in_weight, gain1, gain_ref, *refs):
    outs, total = refs[:-1], refs[-1]
    s = pl.program_id(0)
    width = x.shape[2]
    span = residual_grad.shape[2]
    total[...] = dot(pg_gate[0], in_weight[:, :width], 1, 1) + dot(pg_rest[0], in_weight[:, width:], 1, 1)
    gain_grad = jnp.zeros((1, width), F32)
    for r, out in enumerate(outs):
        at = pl.ds(pl.multiple_of((ids[SEQ] ^ r) * span, span), span)
        standard, inverse = standardize(x[0, at, :].astype(F32))
        grad = total[at, :]
        gain_grad += jnp.sum(grad * standard, axis=0, keepdims=True)
        out[0] = (residual_grad[0, r] + norm_back(grad, standard, inverse, gain1[...])).astype(LOW)
    accumulate(s, gain_ref, gain_grad)


def back_in(ids, pg_gate, pg_rest, x, residual_grad, in_weight, gain1):
    slots, count, width = x.shape
    n_blocks, span = residual_grad.shape[1:3]
    seqs = lambda m: pl.BlockSpec((1, count, m * width), lambda s, ids: (s, 0, 0))
    rel = pl.BlockSpec((1, n_blocks, span, width), lambda s, ids: (s, 0, 0, 0))
    return call(
        back_in_kernel,
        (slots,),
        ids,
        [seqs(1), seqs(2), seqs(1), rel, kept(in_weight.shape), kept((1, width))],
        [whole((1, width))] + [pl.BlockSpec((1, span, width), lambda s, ids: (s, 0, 0))] * n_blocks,
        [sds((1, width), F32)] + [sds((slots, span, width))] * n_blocks,
        (pg_gate, pg_rest, x, residual_grad, in_weight, gain1),
        [pltpu.VMEM((count, width), F32)],
        mib=32,
        cost=LONG,
    )


def exchange(x, partner):
    n_seq, n_batch = lax.axis_size("seq"), lax.axis_size("batch")
    pairs = []
    for s in range(n_seq):
        for b in range(n_batch):
            to_s, to_b = partner(s, b)
            pairs.append((s * n_batch + b, to_s * n_batch + to_b))
    return lax.ppermute(x, ("seq", "batch"), pairs)


def across(s, b):
    return s, b ^ 1


def first_side(s, b):
    return s ^ (1 if b % 2 == 0 else 2), b


def second_side(s, b):
    return s ^ (2 if b % 2 == 0 else 1), b


def next_chip(s, b):
    return s, b ^ 2


def far_chip(s, b):
    return s, b ^ 4


def blocks_of(r):
    return lambda s, b: (s ^ r, b)


def tie(*groups):
    return lax.optimization_barrier(groups)


class Piece:
    def __init__(self, keep, send, steps, alone=False):
        self.keep, self.send, self.steps = keep, send, list(steps)
        self.arriving, self.place, self.got = None, 0, []
        if alone:
            self.arriving = exchange(send, self.steps[0][0])


def shape_after(shape, cut):
    rows, cols = shape
    if cut == "rows":
        return rows // 2, cols
    if cut == "lanes":
        return rows, cols // 2
    return rows, cols


def slabs(shape):
    return shape[0] * shape[1] // LANES


def put_slabs(to, at, value):
    rows = value.shape[0]
    for c in range(value.shape[1] // LANES):
        to[at + c * rows : at + (c + 1) * rows] = value[:, c * LANES : (c + 1) * LANES]


def engine_kernel(plan, n_in, *refs):
    ins, outs = refs[:n_in], refs[n_in:]
    for op, *rest in plan:
        if op == "fresh":
            src, row, (rows, cols), dst, at = rest
            put_slabs(outs[dst], at, ins[src][row : row + rows])
        elif op == "move":
            src, row, rows, dst, at = rest
            outs[dst][at : at + rows] = ins[src][row : row + rows]
        else:
            keep, src, row, (rows, cols), cut, stay, dst, at = rest
            held, arrived = ins[keep], ins[src]
            plain = arrived.shape == held.shape
            for c in range(cols // LANES):
                lanes = slice(c * LANES, (c + 1) * LANES)
                there = arrived[:, lanes] if plain else arrived[row + c * rows : row + (c + 1) * rows]
                total = (held[:, lanes].astype(F32) + there.astype(F32)).astype(LOW)
                if cut == "rows":
                    half = rows // 2
                    outs[stay][:, lanes] = total[:half]
                    outs[dst][at + c * half : at + (c + 1) * half] = total[half:]
                elif cut == "lanes" and c >= cols // LANES // 2:
                    to = at + (c - cols // LANES // 2) * rows
                    outs[dst][to : to + rows] = total
                else:
                    outs[stay][:, lanes] = total
                    if cut == "all":
                        outs[dst][at + c * rows : at + (c + 1) * rows] = total


def boundary(ids, pieces, guard):
    active = [p for p in pieces if p.steps]
    if not active:
        return guard
    arrivals = {id(p.arriving): p.arriving for p in active if p.arriving is not None}
    keys = list(arrivals)
    landed, guard = tie([arrivals[k] for k in keys], guard)
    landed = dict(zip(keys, landed))
    partners = []
    for p in active:
        upcoming = p.steps if p.arriving is None else p.steps[1:]
        if upcoming and upcoming[0][0] not in partners:
            partners.append(upcoming[0][0])
    ins, index, plan, stays, results = [], {}, [], [], []
    rows_of = dict.fromkeys(partners, 0)

    def source(x):
        if id(x) not in index:
            index[id(x)] = len(ins)
            ins.append(x)
        return index[id(x)]

    def message(partner, rows):
        at = rows_of[partner]
        rows_of[partner] += rows
        return partners.index(partner), at

    for p in active:
        partner, cut = p.steps[0]
        if p.arriving is None:
            parts = 2 if cut == "relay" else 1
            shape = (p.send.shape[0] // parts, p.send.shape[1])
            dst, at = message(partner, parts * slabs(shape))
            for i in range(parts):
                plan.append(("fresh", source(p.send), i * shape[0], shape, dst, at + i * slabs(shape)))
            results.append((p, False, None, dst, at))
            continue
        arrived, n = landed[id(p.arriving)], slabs(p.keep.shape)
        if cut == "relay":
            dst, at = message(p.steps[1][0], 2 * n)
            plan.append(("fresh", source(p.keep), 0, p.keep.shape, dst, at))
            plan.append(("move", source(arrived), p.place + n, n, dst, at + n))
            p.got.append((arrived, p.place))
            results.append((p, True, None, dst, at))
        elif cut == "land":
            p.got += [(arrived, p.place), (arrived, p.place + n)]
            results.append((p, True, None, None, None))
        else:
            after = shape_after(p.keep.shape, cut)
            dst, at = message(p.steps[1][0], slabs(after)) if cut != "done" else (None, None)
            stay = len(partners) + len(stays)
            stays.append(after)
            plan.append(("add", source(p.keep), source(arrived), p.place, p.keep.shape, cut, stay, dst, at))
            results.append((p, True, stay, dst, at))
    outs = []
    if plan:
        shapes = [(rows_of[q], LANES) for q in partners] + stays
        size = sum(x.size for x in ins) + sum(a * b for a, b in shapes)
        outs = pl.pallas_call(
            functools.partial(engine_kernel, plan, len(ins)),
            out_shape=[sds(x) for x in shapes],
            in_specs=[pl.BlockSpec(memory_space=pltpu.VMEM)] * len(ins),
            out_specs=[pl.BlockSpec(memory_space=pltpu.VMEM)] * len(shapes),
            compiler_params=pltpu.CompilerParams(vmem_limit_bytes=2 * size + 4 * MIB),
            cost_estimate=pl.CostEstimate(flops=LONG, bytes_accessed=COST, transcendentals=0),
        )(*ins)
        outs, guard = tie(outs, guard)
    sent = [exchange(outs[i], q) for i, q in enumerate(partners)]
    for p, stepped, stay, dst, at in results:
        if stepped:
            p.steps.pop(0)
        if stay is not None:
            p.keep = outs[stay]
        p.arriving, p.place = (sent[dst], at) if p.steps else (None, None)
    return guard


def wide_sum(keep, arrived, at):
    r, cols = keep.shape
    parts = [arrived[at + c * r : at + (c + 1) * r] for c in range(cols // LANES)]
    return keep[...].astype(F32) + jnp.concatenate(parts, axis=1).astype(F32)


def by_chip_kernel(places, ids, a_keep, b_keep, small_keep, arrived, *outs):
    a = a_keep[...].astype(F32)
    b, small = [wide_sum(ref, arrived, at) for ref, at in zip((b_keep, small_keep), places)]
    width = a.shape[1]
    half = a.shape[0] // 2
    n_chip = len(outs)
    rows = jnp.concatenate([a[half:], b[:half], b[half : 2 * half]], axis=1)
    size, part = 3 * width // n_chip, width // n_chip
    static = b[2 * half :]
    packed = static.shape[0] // n_chip
    count = half + packed
    for q in range(n_chip):
        top = jnp.concatenate([rows[:, q * size : (q + 1) * size], a[:half, q * part : (q + 1) * part]], axis=1)
        cols = static[:, q * part : (q + 1) * part]
        tail = jnp.concatenate([cols[m * packed : (m + 1) * packed] for m in range(n_chip)], axis=1)
        message = jnp.concatenate([top, tail], axis=0).astype(LOW)
        for rel, out in enumerate(outs):

            @pl.when(ids[PLACE] == (q ^ rel))
            def _(message=message, out=out):
                out[:count] = message

    for out in outs:
        out[count:] = small.astype(LOW)


def by_chip(ids, a, b, small):
    width = a.keep.shape[1]
    half = a.keep.shape[0] // 2
    rows = half + (b.keep.shape[0] - 2 * half) // 4 + small.keep.shape[0]
    args = (a.keep, b.keep, small.keep, b.arriving)
    return call(
        functools.partial(by_chip_kernel, (b.place, small.place)), (1,), ids, [whole(x.shape) for x in args],
        [whole((rows, width))] * 4, [sds((rows, width))] * 4, args, mib=24,
    )


def cut_cores_kernel(batches, n_small, ids, *refs):
    parts, glus, downs, own, send = refs[:4], refs[4 : 4 + CHUNKS], refs[4 + CHUNKS : 4 + 2 * CHUNKS], refs[-2], refs[-1]
    total = sum(ref[...].astype(F32) for ref in parts)
    rows, width = total.shape
    total, small = total[: rows - n_small], total[rows - n_small :]
    top = width // 8
    size, part = 3 * width // batches, width // batches
    first = ids[CORE] == 0

    def put(at, low, high):
        here = slice(at, at + low.shape[0])
        own[here, : low.shape[1]] = jnp.where(first, low, high).astype(LOW)
        send[here, : low.shape[1]] = jnp.where(first, high, low).astype(LOW)
        return at + low.shape[0]

    static = jnp.concatenate([total[top:, m * 2 * part : (m + 1) * 2 * part] for m in range(4)], axis=0)
    pair = [
        jnp.concatenate(
            [total[:top, c * size : (c + 1) * size], total[:top, 2 * size + c * part : 2 * size + (c + 1) * part]], axis=1
        )
        for c in range(2)
    ]
    at = put(0, *pair)
    glu = jnp.concatenate([g[...].astype(F32) for g in glus], axis=1)
    side = [
        jnp.concatenate([glu[:, (2 * k + c) * LANES : (2 * k + c + 1) * LANES] for k in range(CHUNKS)], axis=1)
        for c in range(2)
    ]
    at = put(at, *side)
    down = jnp.concatenate([d[...].astype(F32) for d in downs], axis=1)
    at = put(at, down[: down.shape[0] // 2], down[down.shape[0] // 2 :])
    tall = jnp.concatenate([small[:, : width // 2], small[:, width // 2 :]], axis=0)
    at = put(at, tall, tall)
    put(at, static[:, :part], static[:, part:])


def cut_cores(ids, parts, glus, downs, batches, n_small):
    rows, width = parts[0].shape
    top = width // 8
    shape = (
        top + glus[0].shape[0] + downs[0].shape[0] // 2 + 2 * n_small + 4 * (rows - n_small - top), CHUNKS * LANES
    )
    args = (*parts, *glus, *downs)
    return call(
        functools.partial(cut_cores_kernel, batches, n_small), (1,), ids, [whole(x.shape) for x in args], [whole(shape)] * 2,
        [sds(shape)] * 2, args, mib=16,
    )


def finish_kernel(n_small, ids, own, other, in_ref, out_ref, static_ref, glu_ref, down_ref, taps_ref, gain1_ref, gain2_ref):
    part, share = out_ref.shape[1], own.shape[1]
    top, half, tall = in_ref.shape[0] // 2, glu_ref.shape[0], 2 * n_small
    for ref, core in ((own, ids[CORE]), (other, 1 - ids[CORE])):
        rows = pl.ds(pl.multiple_of(core * top, 8), top)
        both = ref[:top].astype(F32)
        in_ref[rows, :] = both[:, : share - part]
        out_ref[rows, :] = both[:, share - part :]
        cols = pl.ds(pl.multiple_of(core * share, LANES), share)
        at = top
        glu_ref[:, cols] = ref[at : at + half].astype(F32)
        at += half
        down_ref[:, cols] = ref[at : at + part].astype(F32)
    at = top + half + part
    static = [ref[at + tall :, :part].astype(F32) for ref in (own, other)]
    first = ids[CORE] == 0
    static_ref[...] = jnp.concatenate(
        [jnp.where(first, static[0], static[1]), jnp.where(first, static[1], static[0])], axis=0
    ).T
    tall_sum = own[at : at + tall].astype(F32) + other[at : at + tall].astype(F32)
    small = jnp.concatenate([tall_sum[: tall // 2], tall_sum[tall // 2 :]], axis=1)
    gain1_ref[...], gain2_ref[...] = small[0], small[4]
    width = small.shape[1]
    for m, first in enumerate((1, 5, 8)):
        taps_ref[:, m * width : (m + 1) * width] = small[first : first + 3]


def finish(ids, own, other, width, count, batches, n_small):
    part = width // batches
    rows = width // 4
    shapes = [
        (rows, 3 * part), (rows, part), (part, count // 4), (rows, 2 * own.shape[1]), (part, 2 * own.shape[1]),
        (3, 3 * width), (width,), (width,),
    ]
    return call(
        functools.partial(finish_kernel, n_small), (1,), ids, [whole(own.shape)] * 2, [whole(x) for x in shapes], [sds(x, F32) for x in shapes],
        (own, other), mib=16,
    )


def add_low(a, b):
    return (a.astype(F32) + b.astype(F32)).astype(LOW)


def seq_sums(keep, send):
    part = add_low(keep, exchange(send, first_side))
    return add_low(part[0], exchange(part[1], second_side))


def spread_sum(x, core, rows, dim):
    x = x.astype(F32)
    zero = jnp.zeros_like(x)
    low, high = jnp.where(core == 0, x, zero), jnp.where(core == 0, zero, x)
    both = jnp.concatenate([low, high], axis=dim)
    return lax.psum_scatter(both, "batch", scatter_dimension=1 - rows, tiled=True)


def on_device(
    inputs,
    lengths,
    norm1_gain,
    in_weight,
    short_taps,
    static_kernel,
    out_weight,
    norm2_gain,
    glu_weight,
    down_weight,
    cotangent,
):
    span, n_slots, width = inputs.shape
    n_seq, n_batch = lax.axis_size("seq"), lax.axis_size("batch")
    seq, batch = lax.axis_index("seq"), lax.axis_index("batch")
    core, place = batch % 2, batch // 2
    paired = n_batch == 8
    total_pos = span * n_seq
    slots = n_slots // n_seq
    tokens = slots * total_pos
    tables = [jnp.asarray(t) for t in half_tables(total_pos)]
    gain1, gain2 = norm1_gain[None], norm2_gain[None]

    block = jnp.arange(4, dtype=jnp.int32)
    swap = lambda rel: (rel % 2) * 2 + rel // 2
    rel = block ^ seq
    row_at = jnp.where(core == 0, swap(rel), rel)
    chip_at = swap(block ^ place) if paired else block
    col_at = row_at if paired else block
    mine = jnp.arange(n_slots)[None, :] == (seq * slots + jnp.arange(slots))[:, None]
    own_lengths = jnp.sum(jnp.where(mine, lengths[None, :], 0), axis=1)
    head = jnp.stack([seq, core, place if paired else jnp.zeros_like(place)]).astype(jnp.int32)
    ids = jnp.concatenate([head, own_lengths, row_at, chip_at, col_at])

    x_turned = turn(ids, inputs, True)
    x_sent = [x_turned[s * n_seq : (s + 1) * n_seq] for s in range(slots)]
    x_blocks = [
        [sent[0]] + [exchange(sent[r], blocks_of(r)) for r in range(1, n_seq)] for sent in x_sent
    ]
    ct_turned = turn(ids, cotangent, False)
    weights = (in_weight, static_kernel, *tables, out_weight, short_taps, gain1, gain2)

    saved, n2_parts, n2_others = None, [], []
    flat = lambda a: a.reshape(-1, width)
    for s in range(slots):
        if s == 0:
            x_blocks[0], ct_turned = tie(x_blocks[0], ct_turned)
            ct_blocks = [ct_turned[0]] + [exchange(ct_turned[r], blocks_of(r)) for r in range(1, n_seq - 1)]
        if s == 1:
            x_blocks, ct_blocks, last, saved = tie(x_blocks, ct_blocks, ct_turned[n_seq - 1], saved)
            ct_blocks.append(exchange(last, blocks_of(n_seq - 1)))
            ct_others = [exchange(flat(c), across) for c in ct_blocks[:-1]]
        *saved, n2 = mixer_forward(ids, s, slots, x_blocks[s], weights, saved)
        n2_parts.append(n2.reshape(total_pos, width))
        n2_others.append(exchange(n2_parts[-1], across))
    ct_others.append(exchange(flat(ct_blocks[-1]), across))
    ct_parts = [flat(c) for c in ct_blocks] + ct_others
    p_all, spec, conv, gated, normed, x_whole, residual = saved
    n2_parts = n2_parts + n2_others

    pieces, chunks, shared = [], [], []
    chip_steps, seq_steps, cuts = (next_chip, far_chip), (first_side, second_side), ("rows", "lanes", "lanes", "done")
    for ks in GROUPS:
        out = glu_chunks(ids, ks, n2_parts, ct_parts, glu_weight, down_weight, shared, n_seq)
        shared = out[-4:]
        for i in range(len(ks)):
            parts = out[4 * i : 4 * i + 4]
            chunks.append(parts)
            if paired:
                pieces.append(Piece(*parts[:2], zip(seq_steps + chip_steps, cuts)))
                pieces.append(Piece(*parts[2:], zip(chip_steps + seq_steps, cuts)))
        ct_parts, shared = boundary(ids, pieces, (ct_parts, shared))
    ff_pieces = list(pieces)
    grads, hiddens, w_glus, w_downs = shared
    out_own, out_sent = halves_product(ids, hiddens, w_downs, 0)
    out_other = exchange(out_sent, across)
    grads, out_sent = tie(grads, out_sent)
    n2g_own, n2g_sent = halves_product(ids, grads, w_glus, 1)
    n2g_other = exchange(n2g_sent, across)
    out_other, n2g_sent = tie(out_other, n2g_sent)
    stay, later, sent = combine(ids, out_own, out_other, residual)
    moved = Piece(flat(later), flat(sent), [(first_side, "relay"), (second_side, "land")])
    pieces.append(moved)
    n2g_own = boundary(ids, pieces, n2g_own)
    residual_grad, conv_grad, pg_gate, small_out, a_keep, a_send = back_out(
        ids, n2g_own, n2g_other, residual, ct_blocks, gated, conv, p_all, normed, out_weight, short_taps, gain2
    )
    conv_grad, pg_gate = boundary(ids, pieces, (conv_grad, pg_gate))
    sum_steps = [(across, "rows"), (first_side, "rows"), (second_side, "done")]
    a = Piece(flat(a_keep), flat(a_send), sum_steps, alone=True)
    if paired:
        conv_grad, pg_gate = boundary(ids, [a], (conv_grad, pg_gate))
        pieces.append(a)
    pg_rest, small_conv, b_keep, b_send = back_conv(ids, conv_grad, spec, p_all, normed, tables, short_taps)
    pg_rest, pg_gate = boundary(ids, pieces, (pg_rest, pg_gate))
    b = Piece(flat(b_keep), flat(b_send), sum_steps, alone=True)
    if paired:
        pieces.append(b)
    gain_in, *x_sent = back_in(ids, pg_gate, pg_rest, x_whole, residual_grad, in_weight, gain1)
    x_sent = boundary(ids, pieces, x_sent)
    output = unturn(ids, [stay] + [ref for ref, _ in moved.got], LOW, tuple(at for _, at in moved.got))
    small = jnp.concatenate([gain_in, small_out, small_conv], axis=0)
    n_small = small.shape[0] + -small.shape[0] % 16
    if paired:
        small = jnp.pad(small, ((0, n_small - small.shape[0]), (0, 0))).astype(LOW)
        small = Piece(small, small, [(first_side, "all"), (second_side, "all")], alone=True)
        pieces.append(small)
        x_sent, output = boundary(ids, pieces, (x_sent, output))
        own, *sent = by_chip(ids, a, b, small)
        own, x_sent = tie(own, x_sent)
        got = [exchange(x, lambda s, b, rel=rel: (s, b ^ (2 * rel))) for rel, x in enumerate(sent, 1)]
        x_got = [x_sent[0]] + [exchange(x_sent[r], blocks_of(r)) for r in range(1, n_seq)]
        own, sent = cut_cores(
            ids, (own, *got), [p.keep for p in ff_pieces[0::2]], [p.keep for p in ff_pieces[1::2]], n_batch, n_small
        )
        sent, x_got = tie(sent, x_got)
        theirs = exchange(sent, across)
        input_grad = unturn(ids, x_got, F32)
        theirs, input_grad = tie(theirs, input_grad)
        total_in, total_out, total_static, total_glu, total_down, total_taps, *gains = finish(
            ids, own, theirs, width, total_pos, n_batch, n_small
        )
        total_static, total_down = total_static.T, total_down.T
    else:
        x_got = [x_sent[0]] + [exchange(x_sent[r], blocks_of(r)) for r in range(1, n_seq)]
        pieces = [a, b]
        while a.steps:
            boundary(ids, pieces, ())
        top = width // 8
        in_rows = jnp.concatenate([a.keep[top:], b.keep[:top], b.keep[top : 2 * top]], axis=1)
        total_in = spread_sum(in_rows, core, 0, 0)
        total_out = spread_sum(a.keep[:top], core, 0, 0)
        total_static = spread_sum(b.keep[2 * top :], core, 0, 0)
        side = n_seq // 2
        halves = lambda x: x.reshape(2, x.shape[0] // 2, x.shape[1])
        glu = jnp.stack(
            [seq_sums(halves(c[0]), halves(c[1])).reshape(-1, side, 2, side, LANES) for c in chunks], axis=4
        )
        glu = glu.transpose(0, 2, 1, 3, 4, 5).reshape(-1, 2 * n_seq, 1, CHUNKS * LANES)
        mine = (jnp.arange(2) == core)[:, None]
        glu = jnp.where(mine, glu, 0).astype(F32).reshape(glu.shape[0], -1)
        total_glu = lax.psum_scatter(glu, "batch", scatter_dimension=1, tiled=True)
        joined = [jnp.concatenate([c[2], c[3]], axis=int(c[2].shape[0] == width)) for c in chunks]
        down = jnp.stack([d.reshape(width, n_seq, LANES) for d in joined], axis=2)
        down = down.reshape(width, n_seq, 1, CHUNKS * LANES)
        down = jnp.where(mine, down, 0).astype(F32).reshape(width, -1)
        down = lax.psum_scatter(down, "batch", scatter_dimension=0, tiled=True)
        total_down = lax.psum_scatter(down, "seq", scatter_dimension=1, tiled=True).T

        small = lax.psum(small, ("seq", "batch"))
        gains = jnp.stack([small[0], small[4]])
        total_taps = jnp.concatenate([small[1:4], small[5:8], small[8:11]], axis=1)
        input_grad = unturn(ids, x_got, F32)
    return (
        output,
        input_grad,
        gains[0],
        total_in,
        total_taps,
        total_static,
        total_out,
        gains[1],
        total_glu,
        total_down,
    )


def solution(mesh):
    return jax.shard_map(
        on_device,
        mesh=mesh,
        in_specs=(
            P("seq", "batch", None),
            P("batch"),
            P(),
            P(),
            P(),
            P(),
            P(),
            P(),
            P(),
            P(),
            P("seq", "batch", None),
        ),
        out_specs=(
            P("seq", "batch", None),
            P("seq", "batch", None),
            P(),
            P("seq", "batch"),
            P(),
            P("seq", "batch"),
            P("seq", "batch"),
            P(),
            P("seq", "batch"),
            P("seq", "batch"),
        ),
        check_vma=False,
    )
```

```python
import functools
import math

import jax
import jax.numpy as jnp
import numpy as np
from jax import lax
from jax.experimental import pallas as pl
from jax.experimental.pallas import tpu as pltpu
from jax.sharding import PartitionSpec as P

F32 = jnp.float32
LOW = jnp.bfloat16
CHUNKS = 3
LANES = 128
ROOT = math.sqrt(2.0 / math.pi)
CUBE = 0.044715
MIB = 2**20
COST = 1000
LONG = 3 * 10**10
GLU_MIB = 50
GROUPS = ((0,), (1, 2))
MIX_MIB = 44
BACK_MIB = 46
ANY = pl.BlockSpec(memory_space=pl.ANY)

SEQ, CORE, PLACE, LENGTH, ROW_AT, CHIP_AT, COL_AT = 0, 1, 2, 3, 5, 9, 13


def half_tables(count):
    steps = np.arange(count)
    angle = (np.arange(count // 2)[:, None] * steps[None, :] % count) * (2.0 * math.pi / count)
    low_rows = np.cos(angle)
    high_rows = -np.sin(angle)
    high_rows[0] = np.where(steps % 2 == 0, 1.0, -1.0)
    table = np.concatenate([low_rows, high_rows], axis=0)
    weight = np.where(steps % (count // 2) == 0, 1.0, 2.0) / count
    return table.astype(LOW), (table * weight[:, None]).T.astype(LOW)


def dot(a, b, ca=1, cb=0):
    return lax.dot_general(a, b, (((ca,), (cb,)), ((), ())), preferred_element_type=F32)


def gelu_parts(z):
    square = z * z
    tanh = jnp.tanh(z * (ROOT + (ROOT * CUBE) * square))
    plus = 0.5 + 0.5 * tanh
    act = z * plus
    return act, plus + act * (1.0 - tanh) * (ROOT + (3.0 * ROOT * CUBE) * square)


def gelu(z):
    return z * (0.5 + 0.5 * jnp.tanh(z * (ROOT + (ROOT * CUBE) * (z * z))))


def standardize(values):
    centred = values - jnp.mean(values, axis=-1, keepdims=True)
    inverse = lax.rsqrt(jnp.mean(centred * centred, axis=-1, keepdims=True) + 1e-05)
    return centred * inverse, inverse


def norm_back(grad_in, standard, inverse, gain_vec):
    scaled = grad_in * gain_vec
    inner = (
        scaled
        - jnp.mean(scaled, axis=-1, keepdims=True)
        - standard * jnp.mean(scaled * standard, axis=-1, keepdims=True)
    )
    return inverse * inner


def shifts(a):
    count = a.shape[0]
    row = lax.broadcasted_iota(jnp.int32, a.shape, 0)
    before = jnp.where(row == 0, 0.0, pltpu.roll(a, 1, 0))
    after = jnp.where(row == count - 1, 0.0, pltpu.roll(a, count - 1, 0))
    return before, after


def mix(low, taps):
    wide = low.astype(F32)
    before, after = shifts(wide)
    return taps[0:1] * before + taps[1:2] * wide + taps[2:3] * after


def mix_back(grad, low, taps):
    wide = low.astype(F32)
    before, after = shifts(grad)
    sums = [jnp.sum(side * wide, axis=0, keepdims=True) for side in (after, grad, before)]
    return sums, (taps[0:1] * after + taps[1:2] * grad + taps[2:3] * before).astype(LOW)


def spectrum_product(a, b, sign):
    half = a.shape[0] // 2
    ar, ai, br, bi = a[:half], a[half:], b[:half], b[half:]
    first = lax.broadcasted_iota(jnp.int32, ar.shape, 0) == 0
    both = ai * bi
    re = ar * br - jnp.where(first, 0.0, sign * both)
    im = jnp.where(first, both, ai * br + sign * (ar * bi))
    return jnp.concatenate([re.astype(LOW), im.astype(LOW)], axis=0)


def live_mask(length, count):
    return (lax.broadcasted_iota(jnp.int32, (count, 1), 0) < length).astype(F32)


def whole(shape):
    return pl.BlockSpec(shape, lambda *at: (0,) * len(shape))


def kept(shape):
    return pl.BlockSpec(shape, lambda *at: (0,) * len(shape), pipeline_mode=pl.Buffered(1))


def in_hbm(arrays):
    return [pltpu.with_memory_space_constraint(a, pltpu.HBM) for a in arrays]


def sds(shape, dtype=LOW):
    return jax.ShapeDtypeStruct(shape, dtype)


def call(body, grid, ids, in_specs, out_specs, out_shape, args, scratch=(), aliases=None, mib=12, cost=COST):
    return pl.pallas_call(
        body,
        grid_spec=pltpu.PrefetchScalarGridSpec(
            num_scalar_prefetch=1, grid=grid, in_specs=in_specs, out_specs=out_specs, scratch_shapes=list(scratch)
        ),
        out_shape=out_shape,
        compiler_params=pltpu.CompilerParams(vmem_limit_bytes=mib * MIB),
        input_output_aliases=aliases or {},
        cost_estimate=pl.CostEstimate(flops=cost, bytes_accessed=COST, transcendentals=0),
    )(ids, *args)


def turn_kernel(by_slot, ids, x_ref, *refs):
    outs, held = refs[:-1], refs[-1]
    held[...] = jnp.swapaxes(x_ref[...].astype(F32), 0, 1).astype(LOW)
    n_seq = 4
    own = held.shape[0] // n_seq
    for r in range(n_seq):
        at = (ids[SEQ] ^ r) * own
        for s in range(own):
            if by_slot:
                outs[s * n_seq + r][...] = held[at + s]
            else:
                outs[r][s] = held[at + s]


def turn(ids, x, by_slot):
    span, slots, width = x.shape
    own = slots // 4
    shape = (span, width) if by_slot else (own, span, width)
    n_out = slots if by_slot else 4
    return call(
        functools.partial(turn_kernel, by_slot), (1,), ids, [whole(x.shape)], [whole(shape)] * n_out,
        [sds(shape)] * n_out, in_hbm([x]), [pltpu.VMEM((slots, span, width), LOW)], mib=20,
    )


def unturn_kernel(places, ids, *refs):
    blocks, out, held = refs[:-2], refs[-2], refs[-1]
    slots, span, width = held.shape
    own = slots // 4
    rels = range(4) if places is None else (0, 1 + ids[CORE], 2 - ids[CORE], 3)
    for i, (rel, block) in enumerate(zip(rels, blocks)):
        for s in range(own):
            to = (ids[SEQ] ^ rel) * own + s
            if places is None or i == 0:
                held[to] = block[s].astype(F32)
            else:
                for c in range(width // LANES):
                    row = places[i - 1] + (c * own + s) * span
                    held[to, :, c * LANES : (c + 1) * LANES] = block[row : row + span].astype(F32)
    out[...] = jnp.swapaxes(held[...], 0, 1).astype(out.dtype)


def unturn(ids, blocks, dtype, places=None):
    own, span, width = blocks[0].shape
    slots = own * 4
    return call(
        functools.partial(unturn_kernel, places),
        (1,),
        ids,
        [whole(b.shape) for b in blocks],
        whole((span, slots, width)),
        sds((span, slots, width), dtype),
        blocks,
        [pltpu.VMEM((slots, span, width), F32)],
        mib=32,
    )


class Copies:
    def __init__(self, sems):
        self.sems, self.made = sems, []

    def start(self, src, to):
        copy = pltpu.make_async_copy(src, to, self.sems.at[len(self.made)])
        copy.start()
        self.made.append(copy)
        return copy

    def finish(self):
        for copy in self.made:
            copy.wait()


def mixer_kernel(
    slot, ids, x0, x1, x2, x3, in_weight, static, table, inverse, w_out, taps, gain1, gain2, *refs
):
    p_hbm, spec_hbm, conv_hbm, gated_hbm, normed_hbm, x_hbm, residual_hbm, n2_hbm = refs[-22:-14]
    (x, w_in, static_low, tab, inv, w_o, p, spec, conv, gated, normed, total, sems_in, sems_out) = refs[-14:]
    blocks = (x0, x1, x2, x3)
    count, width = x.shape
    span = count // len(blocks)
    scale = count**-0.5
    loads, stores = Copies(sems_in), Copies(sems_out)
    place = [pl.ds(pl.multiple_of((ids[SEQ] ^ r) * span, span), span) for r in range(len(blocks))]
    x_copies = [loads.start(block, x.at[place[r]]) for r, block in enumerate(blocks)]
    w_copy, *t_copies = [
        loads.start(src, to)
        for src, to in ((in_weight, w_in), (table, tab), (static, static_low), (inverse, inv), (w_out, w_o))
    ]
    for copy in x_copies:
        copy.wait()
    stores.start(x, x_hbm.at[slot])
    for q in range(len(blocks)):
        rows = slice(q * span, (q + 1) * span)
        wide = x[rows].astype(F32)
        standard, _ = standardize(wide)
        normed[rows] = (standard * gain1[...]).astype(LOW)
        total[rows] = wide
    stores.start(normed, normed_hbm.at[slot])
    live = live_mask(ids[LENGTH + slot], count)
    w_copy.wait()
    p[...] = dot(normed[...], w_in[...]).astype(LOW)
    stores.start(p, p_hbm.at[slot])
    for copy in t_copies:
        copy.wait()
    static_spec = dot(tab[...], static_low[...].astype(LOW))
    value = (live * mix(p[:, width : 2 * width], taps[:, width : 2 * width])).astype(LOW)
    vs = dot(tab[...], value)
    cond = (live * gelu(mix(p[:, 2 * width :], taps[:, 2 * width :]))).astype(LOW)
    ks = static_spec + scale * dot(tab[...], cond)
    spec[:, :width], spec[:, width:] = vs.astype(LOW), ks.astype(LOW)
    stores.start(spec, spec_hbm.at[slot])
    conv[...] = dot(inv[...], spectrum_product(vs, ks, 1.0)).astype(LOW)
    stores.start(conv, conv_hbm.at[slot])
    gated[...] = (live * mix(p[:, :width], taps[:, :width]) * conv[...].astype(F32)).astype(LOW)
    stores.start(gated, gated_hbm.at[slot])
    total[...] += dot(gated[...], w_o[...])
    for r in range(len(blocks)):
        stores.start(total.at[place[r]], residual_hbm.at[slot, r])
    n2 = x
    stores.made[0].wait()
    for q in range(len(blocks)):
        rows = slice(q * span, (q + 1) * span)
        standard, _ = standardize(total[rows])
        n2[rows] = (standard * gain2[...]).astype(LOW)
    for r in range(len(blocks)):
        stores.start(n2.at[place[r]], n2_hbm.at[r])
    for copy in stores.made[1:]:
        copy.wait()


def mixer_forward(ids, slot, slots, x_blocks, weights, before):
    span, width = x_blocks[0].shape
    count = span * len(x_blocks)
    cols = (3, 2, 1, 1, 1, 1)
    rel = (len(x_blocks), span, width)
    *large, taps, gain1, gain2 = weights
    args = (*x_blocks, *in_hbm(large), taps, gain1, gain2)
    in_specs = [ANY] * (len(x_blocks) + len(large)) + [kept(a.shape) for a in (taps, gain1, gain2)]
    aliases = {}
    if before is not None:
        aliases = {1 + len(args) + i: i for i in range(len(before))}
        args, in_specs = args + tuple(before), in_specs + [ANY] * len(before)
    return call(
        functools.partial(mixer_kernel, slot),
        (1,),
        ids,
        in_specs,
        [ANY] * 8,
        [pltpu.HBM((slots, count, m * width), LOW) for m in cols] + [pltpu.HBM((slots, *rel), F32), sds(rel)],
        args,
        [
            pltpu.VMEM((count, width), LOW),
            pltpu.VMEM((width, 3 * width), LOW),
            pltpu.VMEM((count, width), F32),
            pltpu.VMEM((count, count), LOW),
            pltpu.VMEM((count, count), LOW),
            pltpu.VMEM((width, width), LOW),
            pltpu.VMEM((count, 3 * width), LOW),
            pltpu.VMEM((count, 2 * width), LOW),
            pltpu.VMEM((count, width), LOW),
            pltpu.VMEM((count, width), LOW),
            pltpu.VMEM((count, width), LOW),
            pltpu.VMEM((count, width), F32),
            pltpu.SemaphoreType.DMA((9,)),
            pltpu.SemaphoreType.DMA((14,)),
        ],
        aliases,
        mib=MIX_MIB,
        cost=LONG,
    )


def glu_kernel(ks, n_seq, slots, ids, *refs):
    n_blocks, n = 4, len(ks)
    n2_parts, ct_parts = refs[: 2 * slots], refs[2 * slots : 2 * slots + 2 * n_blocks]
    glu_hbm, down_hbm = refs[2 * (slots + n_blocks) :][:2]
    parts_out = refs[-16 - 4 * n : -16]
    (
        gu_hbm, hidden_hbm, w_glu_hbm, w_down_hbm,
        n2, ct, w_glus, w_downs, hidden, gu, g_low, d_low, n2_sems, ct_sems, w_sems, out_sems,
    ) = refs[-16:]
    rows = n2.shape[0] // 2
    span = rows // n_blocks // slots
    units = w_downs.shape[1]
    halves = [pl.ds(h * rows, rows) for h in range(2)]

    def load(h):
        copies = []
        for s in range(slots):
            for r in range(n_blocks):
                copies.append(
                    pltpu.make_async_copy(
                        n2_parts[h * slots + s].at[pl.ds(r * span, span)],
                        n2.at[pl.ds(h * rows + (r * slots + s) * span, span)],
                        n2_sems.at[(h * slots + s) * n_blocks + r],
                    )
                )
        return copies, [
            pltpu.make_async_copy(
                ct_parts[h * n_blocks + r],
                ct.at[pl.ds(h * rows + r * slots * span, slots * span)],
                ct_sems.at[h * n_blocks + r],
            )
            for r in range(n_blocks)
        ]

    loads = [load(h) for h in range(2)]
    glu_copies, down_copies = [], []
    for i, k in enumerate(ks):
        starts = [pl.multiple_of(((2 * m + ids[CORE]) * CHUNKS + k) * LANES, LANES) for m in range(2 * n_seq)]
        glu_copies.append(
            [
                pltpu.make_async_copy(
                    glu_hbm.at[:, pl.ds(col, LANES)],
                    w_glus.at[i, :, pl.ds(m * LANES, LANES)],
                    w_sems.at[3 * n_seq * i + m],
                )
                for m, col in enumerate(starts)
            ]
        )
        down_copies.append(
            [
                pltpu.make_async_copy(
                    down_hbm.at[pl.ds(row, LANES)],
                    w_downs.at[i, pl.ds(m * LANES, LANES)],
                    w_sems.at[3 * n_seq * i + 2 * n_seq + m],
                )
                for m, row in enumerate(starts[:n_seq])
            ]
        )
    for copy in loads[0][0] + glu_copies[0] + down_copies[0] + loads[0][1] + loads[1][0] + loads[1][1]:
        copy.start()
    for i in range(1, n):
        for copy in glu_copies[i] + down_copies[i]:
            copy.start()
    outs = []

    def store(src, to):
        copy = pltpu.make_async_copy(src, to, out_sems.at[len(outs)])
        copy.start()
        outs.append(copy)

    for i, k in enumerate(ks):
        glu_keep, glu_send, down_keep, down_send = parts_out[4 * i : 4 * i + 4]
        w_glu, w_down = w_glus.at[i], w_downs.at[i]
        for copy in (loads[0][0] if i == 0 else []) + glu_copies[i]:
            copy.wait()
        gate_ups = [dot(n2[halves[0]], w_glu[...])]
        for copy in down_copies[i] + (loads[0][1] + loads[1][0] + loads[1][1] if i == 0 else outs[8 * i - 8 : 8 * i]):
            copy.wait()
        gate_ups.append(dot(n2[halves[1]], w_glu[...]))
        for h, gate_up in enumerate(gate_ups):
            here = halves[h]
            gate, up = gate_up[:, :units], gate_up[:, units:]
            hidden_grad = dot(ct[here], w_down[...], 1, 1)
            act, slope = gelu_parts(gate)
            hidden[here] = (act * up).astype(LOW)
            gu[here, :units] = (hidden_grad * up * slope).astype(LOW)
            gu[here, units:] = (hidden_grad * act).astype(LOW)
        mine, wide = pl.ds(k * units, units), pl.ds(2 * k * units, 2 * units)
        store(w_glu, w_glu_hbm.at[:, wide])
        store(w_down, w_down_hbm.at[mine])
        store(hidden, hidden_hbm.at[:, mine])
        store(gu, gu_hbm.at[:, wide])
        g_sum = dot(n2[...], gu[...], 0, 0)
        side = units // 2
        size = g_sum.shape[0] // 4
        for q in range(4):
            here = pl.ds(pl.multiple_of(ids[ROW_AT + q] * size, size), size)
            for high in range(2):
                for g in range(2):
                    at = (high ^ (ids[PLACE] % 2)) * 2 + (g ^ (ids[PLACE] // 2 % 2))
                    from_col = g * units + high * side
                    part = g_sum[q * size : (q + 1) * size, from_col : from_col + side]
                    g_low[here, pl.ds(pl.multiple_of(at * side, side), side)] = part.astype(LOW)
        half = d_low.shape[0] // 2
        store(g_low.at[pl.ds(half, half)], glu_send)
        store(g_low.at[pl.ds(0, half)], glu_keep)
        d_sum = dot(ct[...], hidden[...], 0, 0)
        for q in range(4):
            here = pl.ds(pl.multiple_of(ids[CHIP_AT + q] * size, size), size)
            for s in range(4):
                part = d_sum[q * size : (q + 1) * size, s * LANES : (s + 1) * LANES]
                d_low[here, pl.ds(pl.multiple_of(ids[COL_AT + s] * LANES, LANES), LANES)] = part.astype(LOW)
        store(d_low.at[pl.ds(half, half)], down_send)
        store(d_low.at[pl.ds(0, half)], down_keep)
    for copy in outs[8 * n - 8 :]:
        copy.wait()


def glu_chunks(ids, ks, n2_parts, ct_parts, glu_weight, down_weight, shared, n_seq):
    width, units = glu_weight.shape[0], n_seq * LANES
    slots, n_blocks, n = len(n2_parts) // 2, 4, len(ks)
    tokens = sum(p.shape[0] for p in n2_parts)
    here = [pltpu.with_memory_space_constraint(x, pltpu.VMEM) for x in n2_parts[slots:]] if not shared else n2_parts[slots:]
    args = (*n2_parts[:slots], *here, *ct_parts, *in_hbm((glu_weight, down_weight)), *shared)
    aliases = {1 + len(args) - len(shared) + i: 4 * n + i for i in range(len(shared))}
    return call(
        functools.partial(glu_kernel, ks, n_seq, slots),
        (1,),
        ids,
        [ANY] * len(args),
        [ANY] * (4 * n + 4),
        ([pltpu.VMEM((width // 2, 2 * units), LOW)] * 2 + [pltpu.VMEM((width // 2, units), LOW)] * 2) * n
        + [
            pltpu.HBM(x, LOW)
            for x in (
                (tokens, 2 * CHUNKS * units),
                (tokens, CHUNKS * units),
                (width, 2 * CHUNKS * units),
                (CHUNKS * units, width),
            )
        ],
        args,
        [
            pltpu.VMEM((tokens, width), LOW),
            pltpu.VMEM((tokens, width), LOW),
            pltpu.VMEM((n, width, 2 * units), LOW),
            pltpu.VMEM((n, units, width), LOW),
            pltpu.VMEM((tokens, units), LOW),
            pltpu.VMEM((tokens, 2 * units), LOW),
            pltpu.VMEM((width, 2 * units), LOW),
            pltpu.VMEM((width, units), LOW),
            pltpu.SemaphoreType.DMA((2 * slots * n_blocks,)),
            pltpu.SemaphoreType.DMA((2 * n_blocks,)),
            pltpu.SemaphoreType.DMA((3 * n_seq * n,)),
            pltpu.SemaphoreType.DMA((8 * n,)),
        ],
        aliases,
        mib=GLU_MIB,
        cost=LONG,
    )


def halves_product_kernel(cb, ids, rows_ref, weight, own, other):
    result = dot(rows_ref[...], weight[...], 1, cb)

    @pl.when(pl.program_id(0) < pl.num_programs(0) // 2)
    def _():
        other[...] = result.astype(LOW)

    @pl.when(pl.program_id(0) >= pl.num_programs(0) // 2)
    def _():
        own[...] = result


def halves_product(ids, values, weight, cb, rows=512):
    tokens, size = values.shape
    width = weight.shape[1 - cb]
    per = tokens // 2 // rows
    return call(
        functools.partial(halves_product_kernel, cb),
        (2 * per,),
        ids,
        [pl.BlockSpec((rows, size), lambda i, ids: ((i + per) % (2 * per), 0)), kept(weight.shape)],
        [
            pl.BlockSpec((rows, width), lambda i, ids: (jnp.maximum(i - per, 0), 0)),
            pl.BlockSpec((rows, width), lambda i, ids: (jnp.minimum(i, per - 1), 0)),
        ],
        [sds((tokens // 2, width), F32), sds((tokens // 2, width))],
        in_hbm((values, weight)),
        mib=32,
        cost=LONG,
    )


def combine_kernel(ids, own, other, residual, stay, later, send):
    span = stay.shape[1]
    second, first = 2 - ids[CORE], 1 + ids[CORE]
    for r, out, at in ((0, stay, 0), (second, later, 0), (first, send, 0), (3, send, 1)):
        value = (residual[0, r] + (own[r, 0] + other[r, 0].astype(F32))).astype(LOW)
        if out is send:
            send[at, 0] = value
        else:
            out[0] = value


def combine(ids, own, other, residual):
    slots, n_blocks, span, width = residual.shape
    rows = pl.BlockSpec((n_blocks, 1, span, width), lambda s, ids: (0, s, 0, 0))
    block = pl.BlockSpec((1, span, width), lambda s, ids: (s, 0, 0))
    own, other = [x.reshape(n_blocks, slots, span, width) for x in (own, other)]
    return call(
        combine_kernel,
        (slots,),
        ids,
        [rows, rows, pl.BlockSpec((1, n_blocks, span, width), lambda s, ids: (s, 0, 0, 0))],
        [block, block, pl.BlockSpec((2, 1, span, width), lambda s, ids: (0, s, 0, 0))],
        [sds((slots, span, width))] * 2 + [sds((2, slots, span, width))],
        (own, other, residual),
        mib=16,
    )


def place_halves(ids, grad, at, keep, send):
    size = grad.shape[0] // 8
    for q in range(4):
        to = ids[ROW_AT + q]
        for c in range(2):
            rows = grad[(2 * q + c) * size : (2 * q + c + 1) * size]

            @pl.when(ids[CORE] == c)
            def _(rows=rows, to=to):
                keep[to, at : at + size] = rows

            @pl.when(ids[CORE] != c)
            def _(rows=rows, to=(to % 2) * 2 + to // 2):
                send[to, at : at + size] = rows


def accumulate(step, ref, value):
    @pl.when(step == 0)
    def _():
        ref[...] = value

    @pl.when(step > 0)
    def _():
        ref[...] += value


def back_out_kernel(
    ids, n2g_own_hbm, n2g_other_hbm, residual_hbm, ct0, ct1, ct2, ct3, gated_hbm, conv_hbm, p_hbm, normed_hbm, w_hbm,
    taps, gain2, residual_grad_hbm, conv_grad_hbm, pg_hbm, small, keep, send,
    n2g_own, n2g_other, residual, cot, gated, conv, p, normed, w_out, branch, conv_grad, pg, sems_in, sems_out,
):
    slots, n_blocks, span, width = residual.shape
    count = n_blocks * span
    loads, stores = Copies(sems_in), Copies(sems_out)
    early, late = [], []
    for s in range(slots):
        here = pl.ds(s * count, count)
        early.append(
            [loads.start(residual_hbm.at[s], residual.at[s])]
            + [loads.start(ref.at[s], cot.at[s, r]) for r, ref in enumerate((ct0, ct1, ct2, ct3))]
            + [loads.start(n2g_own_hbm.at[:, s], n2g_own.at[s]), loads.start(n2g_other_hbm.at[:, s], n2g_other.at[s])]
        )
        late.append(
            ([loads.start(w_hbm, w_out)] if s == 0 else [])
            + [loads.start(p_hbm.at[s, :, pl.ds(0, width)], p.at[here]), loads.start(conv_hbm.at[s], conv.at[here])]
        )
    last = [
        loads.start(ref.at[s], to.at[pl.ds(s * count, count)])
        for s in range(slots)
        for ref, to in ((gated_hbm, gated), (normed_hbm, normed))
    ]
    gain_grad, tap_sums = jnp.zeros((1, width), F32), None
    for s in range(slots):
        here = slice(s * count, (s + 1) * count)
        for copy in early[s]:
            copy.wait()
        for r in range(n_blocks):
            at = pl.multiple_of(s * count + (ids[SEQ] ^ r) * span, span)
            grad = n2g_own[s, r] + n2g_other[s, r].astype(F32)
            unit, inverse = standardize(residual[s, r])
            gain_grad += jnp.sum(grad * unit, axis=0, keepdims=True)
            value = cot[s, r].astype(F32) + norm_back(grad, unit, inverse, gain2[...])
            residual[s, r] = value
            branch[pl.ds(at, span), :] = value.astype(LOW)
        stores.start(residual.at[s], residual_grad_hbm.at[s])
        live = live_mask(ids[LENGTH + s], count)
        for copy in late[s]:
            copy.wait()
        gated_grad = live * dot(branch[here], w_out[...], 1, 1)
        conv_grad[here] = (gated_grad * mix(p[here], taps[...])).astype(LOW)
        sums, pg[here] = mix_back(gated_grad * conv[here].astype(F32), p[here], taps[...])
        tap_sums = sums if s == 0 else [x + y for x, y in zip(tap_sums, sums)]
        stores.start(conv_grad.at[pl.ds(s * count, count)], conv_grad_hbm.at[s])
        stores.start(pg.at[pl.ds(s * count, count)], pg_hbm.at[s])
    small[...] = jnp.concatenate(tap_sums + [gain_grad], axis=0)
    for copy in last:
        copy.wait()
    place_halves(ids, dot(gated[...], branch[...], 0, 0).astype(LOW), 0, keep, send)
    place_halves(ids, dot(normed[...], pg[...], 0, 0).astype(LOW), width // 8, keep, send)
    stores.finish()


def back_out(ids, n2g_own, n2g_other, residual, cot, gated, conv, p_all, normed, w_out, taps, gain2):
    slots, n_blocks, span, width = residual.shape
    count = n_blocks * span
    n2g_own, n2g_other = [x.reshape(n_blocks, slots, span, width) for x in (n2g_own, n2g_other)]
    part = (4, 2 * width // 8, width)
    args = (n2g_own, n2g_other, *in_hbm([residual]), *cot, *in_hbm((gated, conv, p_all, normed, w_out)))
    n_loads = slots * (1 + n_blocks + 2 + 2 + 2) + 1
    flat = (slots * count, width)
    return call(
        back_out_kernel,
        (1,),
        ids,
        [ANY] * len(args) + [kept((3, width)), kept((1, width))],
        [ANY] * 3 + [whole((4, width))] + [pl.BlockSpec(memory_space=pltpu.VMEM)] * 2,
        [
            pltpu.HBM(residual.shape, F32),
            pltpu.HBM((slots, count, width), LOW),
            pltpu.HBM((slots, count, width), LOW),
            sds((4, width), F32),
            pltpu.VMEM(part, LOW),
            pltpu.VMEM(part, LOW),
        ],
        (*args, taps, gain2),
        [
            pltpu.VMEM(residual.shape, F32),
            pltpu.VMEM(residual.shape, LOW),
            pltpu.VMEM(residual.shape, F32),
            pltpu.VMEM(residual.shape, LOW),
            *[pltpu.VMEM(flat, LOW)] * 4,
            pltpu.VMEM((width, width), LOW),
            *[pltpu.VMEM(flat, LOW)] * 3,
            pltpu.SemaphoreType.DMA((n_loads,)),
            pltpu.SemaphoreType.DMA((3 * slots,)),
        ],
        mib=BACK_MIB,
        cost=LONG,
    )


def back_conv_kernel(
    ids, conv_grad_hbm, spec_hbm, p_hbm, normed_hbm, table_hbm, inverse_hbm, t_value, t_cond,
    pg_hbm, small, keep, send,
    conv_grad, spec, p, normed, table, inverse, pg, sems_in, sems_out,
):
    width = t_value.shape[1]
    count = table.shape[0]
    slots = conv_grad.shape[0] // count
    scale = count**-0.5
    loads, stores = Copies(sems_in), Copies(sems_out)
    here_of = lambda s: pl.ds(s * count, count)
    first = [loads.start(table_hbm, table)]
    parts = []
    for s in range(slots):
        parts.append([loads.start(conv_grad_hbm.at[s], conv_grad.at[here_of(s)])])
        parts.append([loads.start(spec_hbm.at[s], spec.at[here_of(s)])])
        if s == 0:
            parts[-1].append(loads.start(inverse_hbm, inverse))
        parts.append([loads.start(p_hbm.at[s, :, pl.ds(width, 2 * width)], p.at[here_of(s)])])
    last = [loads.start(normed_hbm.at[s], normed.at[here_of(s)]) for s in range(slots)]
    tap_sums = static_total = None
    for s in range(slots):
        here = slice(s * count, (s + 1) * count)
        live = live_mask(ids[LENGTH + s], count)
        for copy in (first if s == 0 else []) + parts[3 * s]:
            copy.wait()
        gs = dot(table[...], conv_grad[here])
        for copy in parts[3 * s + 1]:
            copy.wait()
        value_low = spectrum_product(gs, spec[here, width:].astype(F32), -1.0)
        cond_low = spectrum_product(gs, spec[here, :width].astype(F32), -1.0)
        value_grad = live * dot(inverse[...], value_low)
        back = dot(inverse[...], cond_low)
        static_total = back if s == 0 else static_total + back
        for copy in parts[3 * s + 2]:
            copy.wait()
        sums_v, pg[here, :width] = mix_back(value_grad, p[here, :width], t_value[...])
        cond_grad = (live * scale) * back * gelu_parts(mix(p[here, width:], t_cond[...]))[1]
        sums_c, pg[here, width:] = mix_back(cond_grad, p[here, width:], t_cond[...])
        sums = sums_v + sums_c
        tap_sums = sums if s == 0 else [x + y for x, y in zip(tap_sums, sums)]
        stores.start(pg.at[here_of(s)], pg_hbm.at[s])
    small[...] = jnp.concatenate(tap_sums, axis=0)
    place_halves(ids, static_total.astype(LOW), width // 4, keep, send)
    for copy in last:
        copy.wait()
    total = dot(normed[...], pg[...], 0, 0).astype(LOW)
    place_halves(ids, total[:, :width], 0, keep, send)
    place_halves(ids, total[:, width:], width // 8, keep, send)
    stores.finish()


def back_conv(ids, conv_grad, spec, p_all, normed, tables, taps):
    slots, count, width = conv_grad.shape
    tap = lambda m: pl.BlockSpec((3, width), lambda i, ids, m=m: (0, m))
    part = (4, (2 * width + count) // 8, width)
    args = in_hbm((conv_grad, spec, p_all, normed, *tables))
    rows = slots * count
    return call(
        back_conv_kernel,
        (1,),
        ids,
        [ANY] * len(args) + [tap(1), tap(2)],
        [ANY, whole((6, width))] + [pl.BlockSpec(memory_space=pltpu.VMEM)] * 2,
        [
            pltpu.HBM((slots, count, 2 * width), LOW),
            sds((6, width), F32),
            pltpu.VMEM(part, LOW),
            pltpu.VMEM(part, LOW),
        ],
        (*args, taps, taps),
        [
            pltpu.VMEM((rows, width), LOW),
            pltpu.VMEM((rows, 2 * width), LOW),
            pltpu.VMEM((rows, 2 * width), LOW),
            pltpu.VMEM((rows, width), LOW),
            pltpu.VMEM((count, count), LOW),
            pltpu.VMEM((count, count), LOW),
            pltpu.VMEM((rows, 2 * width), LOW),
            pltpu.SemaphoreType.DMA((4 * slots + 2,)),
            pltpu.SemaphoreType.DMA((slots,)),
        ],
        mib=BACK_MIB,
        cost=LONG,
    )


def back_in_kernel(ids, pg_gate, pg_rest, x, residual_grad, in_weight, gain1, gain_ref, *refs):
    outs, total = refs[:-1], refs[-1]
    s = pl.program_id(0)
    width = x.shape[2]
    span = residual_grad.shape[2]
    total[...] = dot(pg_gate[0], in_weight[:, :width], 1, 1) + dot(pg_rest[0], in_weight[:, width:], 1, 1)
    gain_grad = jnp.zeros((1, width), F32)
    for r, out in enumerate(outs):
        at = pl.ds(pl.multiple_of((ids[SEQ] ^ r) * span, span), span)
        standard, inverse = standardize(x[0, at, :].astype(F32))
        grad = total[at, :]
        gain_grad += jnp.sum(grad * standard, axis=0, keepdims=True)
        out[0] = (residual_grad[0, r] + norm_back(grad, standard, inverse, gain1[...])).astype(LOW)
    accumulate(s, gain_ref, gain_grad)


def back_in(ids, pg_gate, pg_rest, x, residual_grad, in_weight, gain1):
    slots, count, width = x.shape
    n_blocks, span = residual_grad.shape[1:3]
    seqs = lambda m: pl.BlockSpec((1, count, m * width), lambda s, ids: (s, 0, 0))
    rel = pl.BlockSpec((1, n_blocks, span, width), lambda s, ids: (s, 0, 0, 0))
    return call(
        back_in_kernel,
        (slots,),
        ids,
        [seqs(1), seqs(2), seqs(1), rel, kept(in_weight.shape), kept((1, width))],
        [whole((1, width))] + [pl.BlockSpec((1, span, width), lambda s, ids: (s, 0, 0))] * n_blocks,
        [sds((1, width), F32)] + [sds((slots, span, width))] * n_blocks,
        (pg_gate, pg_rest, x, residual_grad, in_weight, gain1),
        [pltpu.VMEM((count, width), F32)],
        mib=32,
        cost=LONG,
    )


def exchange(x, partner):
    n_seq, n_batch = lax.axis_size("seq"), lax.axis_size("batch")
    pairs = []
    for s in range(n_seq):
        for b in range(n_batch):
            to_s, to_b = partner(s, b)
            pairs.append((s * n_batch + b, to_s * n_batch + to_b))
    return lax.ppermute(x, ("seq", "batch"), pairs)


def across(s, b):
    return s, b ^ 1


def first_side(s, b):
    return s ^ (1 if b % 2 == 0 else 2), b


def second_side(s, b):
    return s ^ (2 if b % 2 == 0 else 1), b


def next_chip(s, b):
    return s, b ^ 2


def far_chip(s, b):
    return s, b ^ 4


def blocks_of(r):
    return lambda s, b: (s ^ r, b)


def tie(*groups):
    return lax.optimization_barrier(groups)


class Piece:
    def __init__(self, keep, send, steps, alone=False):
        self.keep, self.send, self.steps = keep, send, list(steps)
        self.arriving, self.place, self.got = None, 0, []
        if alone:
            self.arriving = exchange(send, self.steps[0][0])


def shape_after(shape, cut):
    rows, cols = shape
    if cut == "rows":
        return rows // 2, cols
    if cut == "lanes":
        return rows, cols // 2
    return rows, cols


def slabs(shape):
    return shape[0] * shape[1] // LANES


def put_slabs(to, at, value):
    rows = value.shape[0]
    for c in range(value.shape[1] // LANES):
        to[at + c * rows : at + (c + 1) * rows] = value[:, c * LANES : (c + 1) * LANES]


def engine_kernel(plan, n_in, *refs):
    ins, outs = refs[:n_in], refs[n_in:]
    for op, *rest in plan:
        if op == "fresh":
            src, row, (rows, cols), dst, at = rest
            put_slabs(outs[dst], at, ins[src][row : row + rows])
        elif op == "move":
            src, row, rows, dst, at = rest
            outs[dst][at : at + rows] = ins[src][row : row + rows]
        else:
            keep, src, row, (rows, cols), cut, stay, dst, at = rest
            held, arrived = ins[keep], ins[src]
            plain = arrived.shape == held.shape
            for c in range(cols // LANES):
                lanes = slice(c * LANES, (c + 1) * LANES)
                there = arrived[:, lanes] if plain else arrived[row + c * rows : row + (c + 1) * rows]
                total = (held[:, lanes].astype(F32) + there.astype(F32)).astype(LOW)
                if cut == "rows":
                    half = rows // 2
                    outs[stay][:, lanes] = total[:half]
                    outs[dst][at + c * half : at + (c + 1) * half] = total[half:]
                elif cut == "lanes" and c >= cols // LANES // 2:
                    to = at + (c - cols // LANES // 2) * rows
                    outs[dst][to : to + rows] = total
                else:
                    outs[stay][:, lanes] = total
                    if cut == "all":
                        outs[dst][at + c * rows : at + (c + 1) * rows] = total


def boundary(ids, pieces, guard):
    active = [p for p in pieces if p.steps]
    if not active:
        return guard
    arrivals = {id(p.arriving): p.arriving for p in active if p.arriving is not None}
    keys = list(arrivals)
    landed, guard = tie([arrivals[k] for k in keys], guard)
    landed = dict(zip(keys, landed))
    partners = []
    for p in active:
        upcoming = p.steps if p.arriving is None else p.steps[1:]
        if upcoming and upcoming[0][0] not in partners:
            partners.append(upcoming[0][0])
    ins, index, plan, stays, results = [], {}, [], [], []
    rows_of = dict.fromkeys(partners, 0)

    def source(x):
        if id(x) not in index:
            index[id(x)] = len(ins)
            ins.append(x)
        return index[id(x)]

    def message(partner, rows):
        at = rows_of[partner]
        rows_of[partner] += rows
        return partners.index(partner), at

    for p in active:
        partner, cut = p.steps[0]
        if p.arriving is None:
            parts = 2 if cut == "relay" else 1
            shape = (p.send.shape[0] // parts, p.send.shape[1])
            dst, at = message(partner, parts * slabs(shape))
            for i in range(parts):
                plan.append(("fresh", source(p.send), i * shape[0], shape, dst, at + i * slabs(shape)))
            results.append((p, False, None, dst, at))
            continue
        arrived, n = landed[id(p.arriving)], slabs(p.keep.shape)
        if cut == "relay":
            dst, at = message(p.steps[1][0], 2 * n)
            plan.append(("fresh", source(p.keep), 0, p.keep.shape, dst, at))
            plan.append(("move", source(arrived), p.place + n, n, dst, at + n))
            p.got.append((arrived, p.place))
            results.append((p, True, None, dst, at))
        elif cut == "land":
            p.got += [(arrived, p.place), (arrived, p.place + n)]
            results.append((p, True, None, None, None))
        else:
            after = shape_after(p.keep.shape, cut)
            dst, at = message(p.steps[1][0], slabs(after)) if cut != "done" else (None, None)
            stay = len(partners) + len(stays)
            stays.append(after)
            plan.append(("add", source(p.keep), source(arrived), p.place, p.keep.shape, cut, stay, dst, at))
            results.append((p, True, stay, dst, at))
    outs = []
    if plan:
        shapes = [(rows_of[q], LANES) for q in partners] + stays
        size = sum(x.size for x in ins) + sum(a * b for a, b in shapes)
        outs = pl.pallas_call(
            functools.partial(engine_kernel, plan, len(ins)),
            out_shape=[sds(x) for x in shapes],
            in_specs=[pl.BlockSpec(memory_space=pltpu.VMEM)] * len(ins),
            out_specs=[pl.BlockSpec(memory_space=pltpu.VMEM)] * len(shapes),
            compiler_params=pltpu.CompilerParams(vmem_limit_bytes=2 * size + 4 * MIB),
            cost_estimate=pl.CostEstimate(flops=LONG, bytes_accessed=COST, transcendentals=0),
        )(*ins)
        outs, guard = tie(outs, guard)
    sent = [exchange(outs[i], q) for i, q in enumerate(partners)]
    for p, stepped, stay, dst, at in results:
        if stepped:
            p.steps.pop(0)
        if stay is not None:
            p.keep = outs[stay]
        p.arriving, p.place = (sent[dst], at) if p.steps else (None, None)
    return guard


def wide_sum(keep, arrived, at):
    r, cols = keep.shape
    parts = [arrived[at + c * r : at + (c + 1) * r] for c in range(cols // LANES)]
    return keep[...].astype(F32) + jnp.concatenate(parts, axis=1).astype(F32)


def by_chip_kernel(places, ids, a_keep, b_keep, small_keep, arrived, *outs):
    a = a_keep[...].astype(F32)
    b, small = [wide_sum(ref, arrived, at) for ref, at in zip((b_keep, small_keep), places)]
    width = a.shape[1]
    half = a.shape[0] // 2
    n_chip = len(outs)
    rows = jnp.concatenate([a[half:], b[:half], b[half : 2 * half]], axis=1)
    size, part = 3 * width // n_chip, width // n_chip
    static = b[2 * half :]
    packed = static.shape[0] // n_chip
    count = half + packed
    for q in range(n_chip):
        top = jnp.concatenate([rows[:, q * size : (q + 1) * size], a[:half, q * part : (q + 1) * part]], axis=1)
        cols = static[:, q * part : (q + 1) * part]
        tail = jnp.concatenate([cols[m * packed : (m + 1) * packed] for m in range(n_chip)], axis=1)
        message = jnp.concatenate([top, tail], axis=0).astype(LOW)
        for rel, out in enumerate(outs):

            @pl.when(ids[PLACE] == (q ^ rel))
            def _(message=message, out=out):
                out[:count] = message

    for out in outs:
        out[count:] = small.astype(LOW)


def by_chip(ids, a, b, small):
    width = a.keep.shape[1]
    half = a.keep.shape[0] // 2
    rows = half + (b.keep.shape[0] - 2 * half) // 4 + small.keep.shape[0]
    args = (a.keep, b.keep, small.keep, b.arriving)
    return call(
        functools.partial(by_chip_kernel, (b.place, small.place)), (1,), ids, [whole(x.shape) for x in args],
        [whole((rows, width))] * 4, [sds((rows, width))] * 4, args, mib=24,
    )


def cut_cores_kernel(batches, n_small, ids, *refs):
    parts, glus, downs, own, send = refs[:4], refs[4 : 4 + CHUNKS], refs[4 + CHUNKS : 4 + 2 * CHUNKS], refs[-2], refs[-1]
    total = sum(ref[...].astype(F32) for ref in parts)
    rows, width = total.shape
    total, small = total[: rows - n_small], total[rows - n_small :]
    top = width // 8
    size, part = 3 * width // batches, width // batches
    first = ids[CORE] == 0

    def put(at, low, high):
        here = slice(at, at + low.shape[0])
        own[here, : low.shape[1]] = jnp.where(first, low, high).astype(LOW)
        send[here, : low.shape[1]] = jnp.where(first, high, low).astype(LOW)
        return at + low.shape[0]

    static = jnp.concatenate([total[top:, m * 2 * part : (m + 1) * 2 * part] for m in range(4)], axis=0)
    pair = [
        jnp.concatenate(
            [total[:top, c * size : (c + 1) * size], total[:top, 2 * size + c * part : 2 * size + (c + 1) * part]], axis=1
        )
        for c in range(2)
    ]
    at = put(0, *pair)
    glu = jnp.concatenate([g[...].astype(F32) for g in glus], axis=1)
    side = [
        jnp.concatenate([glu[:, (2 * k + c) * LANES : (2 * k + c + 1) * LANES] for k in range(CHUNKS)], axis=1)
        for c in range(2)
    ]
    at = put(at, *side)
    down = jnp.concatenate([d[...].astype(F32) for d in downs], axis=1)
    at = put(at, down[: down.shape[0] // 2], down[down.shape[0] // 2 :])
    tall = jnp.concatenate([small[:, : width // 2], small[:, width // 2 :]], axis=0)
    at = put(at, tall, tall)
    put(at, static[:, :part], static[:, part:])


def cut_cores(ids, parts, glus, downs, batches, n_small):
    rows, width = parts[0].shape
    top = width // 8
    shape = (
        top + glus[0].shape[0] + downs[0].shape[0] // 2 + 2 * n_small + 4 * (rows - n_small - top), CHUNKS * LANES
    )
    args = (*parts, *glus, *downs)
    return call(
        functools.partial(cut_cores_kernel, batches, n_small), (1,), ids, [whole(x.shape) for x in args], [whole(shape)] * 2,
        [sds(shape)] * 2, args, mib=16,
    )


def finish_kernel(n_small, ids, own, other, in_ref, out_ref, static_ref, glu_ref, down_ref, taps_ref, gain1_ref, gain2_ref):
    part, share = out_ref.shape[1], own.shape[1]
    top, half, tall = in_ref.shape[0] // 2, glu_ref.shape[0], 2 * n_small
    for ref, core in ((own, ids[CORE]), (other, 1 - ids[CORE])):
        rows = pl.ds(pl.multiple_of(core * top, 8), top)
        both = ref[:top].astype(F32)
        in_ref[rows, :] = both[:, : share - part]
        out_ref[rows, :] = both[:, share - part :]
        cols = pl.ds(pl.multiple_of(core * share, LANES), share)
        at = top
        glu_ref[:, cols] = ref[at : at + half].astype(F32)
        at += half
        down_ref[:, cols] = ref[at : at + part].astype(F32)
    at = top + half + part
    static = [ref[at + tall :, :part].astype(F32) for ref in (own, other)]
    first = ids[CORE] == 0
    static_ref[...] = jnp.concatenate(
        [jnp.where(first, static[0], static[1]), jnp.where(first, static[1], static[0])], axis=0
    ).T
    tall_sum = own[at : at + tall].astype(F32) + other[at : at + tall].astype(F32)
    small = jnp.concatenate([tall_sum[: tall // 2], tall_sum[tall // 2 :]], axis=1)
    gain1_ref[...], gain2_ref[...] = small[0], small[4]
    width = small.shape[1]
    for m, first in enumerate((1, 5, 8)):
        taps_ref[:, m * width : (m + 1) * width] = small[first : first + 3]


def finish(ids, own, other, width, count, batches, n_small):
    part = width // batches
    rows = width // 4
    shapes = [
        (rows, 3 * part), (rows, part), (part, count // 4), (rows, 2 * own.shape[1]), (part, 2 * own.shape[1]),
        (3, 3 * width), (width,), (width,),
    ]
    return call(
        functools.partial(finish_kernel, n_small), (1,), ids, [whole(own.shape)] * 2, [whole(x) for x in shapes], [sds(x, F32) for x in shapes],
        (own, other), mib=16,
    )


def add_low(a, b):
    return (a.astype(F32) + b.astype(F32)).astype(LOW)


def seq_sums(keep, send):
    part = add_low(keep, exchange(send, first_side))
    return add_low(part[0], exchange(part[1], second_side))


def spread_sum(x, core, rows, dim):
    x = x.astype(F32)
    zero = jnp.zeros_like(x)
    low, high = jnp.where(core == 0, x, zero), jnp.where(core == 0, zero, x)
    both = jnp.concatenate([low, high], axis=dim)
    return lax.psum_scatter(both, "batch", scatter_dimension=1 - rows, tiled=True)


def on_device(
    inputs,
    lengths,
    norm1_gain,
    in_weight,
    short_taps,
    static_kernel,
    out_weight,
    norm2_gain,
    glu_weight,
    down_weight,
    cotangent,
):
    span, n_slots, width = inputs.shape
    n_seq, n_batch = lax.axis_size("seq"), lax.axis_size("batch")
    seq, batch = lax.axis_index("seq"), lax.axis_index("batch")
    core, place = batch % 2, batch // 2
    paired = n_batch == 8
    total_pos = span * n_seq
    slots = n_slots // n_seq
    tokens = slots * total_pos
    tables = [jnp.asarray(t) for t in half_tables(total_pos)]
    gain1, gain2 = norm1_gain[None], norm2_gain[None]

    block = jnp.arange(4, dtype=jnp.int32)
    swap = lambda rel: (rel % 2) * 2 + rel // 2
    rel = block ^ seq
    row_at = jnp.where(core == 0, swap(rel), rel)
    chip_at = swap(block ^ place) if paired else block
    col_at = row_at if paired else block
    mine = jnp.arange(n_slots)[None, :] == (seq * slots + jnp.arange(slots))[:, None]
    own_lengths = jnp.sum(jnp.where(mine, lengths[None, :], 0), axis=1)
    head = jnp.stack([seq, core, place if paired else jnp.zeros_like(place)]).astype(jnp.int32)
    ids = jnp.concatenate([head, own_lengths, row_at, chip_at, col_at])

    x_turned = turn(ids, inputs, True)
    x_sent = [x_turned[s * n_seq : (s + 1) * n_seq] for s in range(slots)]
    x_blocks = [
        [sent[0]] + [exchange(sent[r], blocks_of(r)) for r in range(1, n_seq)] for sent in x_sent
    ]
    ct_turned = turn(ids, cotangent, False)
    weights = (in_weight, static_kernel, *tables, out_weight, short_taps, gain1, gain2)

    saved, n2_parts, n2_others = None, [], []
    flat = lambda a: a.reshape(-1, width)
    for s in range(slots):
        if s == 0:
            x_blocks[0], ct_turned = tie(x_blocks[0], ct_turned)
            ct_blocks = [ct_turned[0]] + [exchange(ct_turned[r], blocks_of(r)) for r in range(1, n_seq - 1)]
        if s == 1:
            x_blocks, ct_blocks, last, saved = tie(x_blocks, ct_blocks, ct_turned[n_seq - 1], saved)
            ct_blocks.append(exchange(last, blocks_of(n_seq - 1)))
            ct_others = [exchange(flat(c), across) for c in ct_blocks[:-1]]
        *saved, n2 = mixer_forward(ids, s, slots, x_blocks[s], weights, saved)
        n2_parts.append(n2.reshape(total_pos, width))
        n2_others.append(exchange(n2_parts[-1], across))
    ct_others.append(exchange(flat(ct_blocks[-1]), across))
    ct_parts = [flat(c) for c in ct_blocks] + ct_others
    p_all, spec, conv, gated, normed, x_whole, residual = saved
    n2_parts = n2_parts + n2_others

    pieces, chunks, shared = [], [], []
    chip_steps, seq_steps, cuts = (next_chip, far_chip), (first_side, second_side), ("rows", "lanes", "lanes", "done")
    for ks in GROUPS:
        out = glu_chunks(ids, ks, n2_parts, ct_parts, glu_weight, down_weight, shared, n_seq)
        shared = out[-4:]
        for i in range(len(ks)):
            parts = out[4 * i : 4 * i + 4]
            chunks.append(parts)
            if paired:
                pieces.append(Piece(*parts[:2], zip(seq_steps + chip_steps, cuts)))
                pieces.append(Piece(*parts[2:], zip(chip_steps + seq_steps, cuts)))
        ct_parts, shared = boundary(ids, pieces, (ct_parts, shared))
    ff_pieces = list(pieces)
    grads, hiddens, w_glus, w_downs = shared
    out_own, out_sent = halves_product(ids, hiddens, w_downs, 0)
    out_other = exchange(out_sent, across)
    grads, out_sent = tie(grads, out_sent)
    n2g_own, n2g_sent = halves_product(ids, grads, w_glus, 1)
    n2g_other = exchange(n2g_sent, across)
    out_other, n2g_sent = tie(out_other, n2g_sent)
    stay, later, sent = combine(ids, out_own, out_other, residual)
    moved = Piece(flat(later), flat(sent), [(first_side, "relay"), (second_side, "land")])
    pieces.append(moved)
    n2g_own = boundary(ids, pieces, n2g_own)
    residual_grad, conv_grad, pg_gate, small_out, a_keep, a_send = back_out(
        ids, n2g_own, n2g_other, residual, ct_blocks, gated, conv, p_all, normed, out_weight, short_taps, gain2
    )
    conv_grad, pg_gate = boundary(ids, pieces, (conv_grad, pg_gate))
    sum_steps = [(across, "rows"), (first_side, "rows"), (second_side, "done")]
    a = Piece(flat(a_keep), flat(a_send), sum_steps, alone=True)
    if paired:
        conv_grad, pg_gate = boundary(ids, [a], (conv_grad, pg_gate))
        pieces.append(a)
    pg_rest, small_conv, b_keep, b_send = back_conv(ids, conv_grad, spec, p_all, normed, tables, short_taps)
    pg_rest, pg_gate = boundary(ids, pieces, (pg_rest, pg_gate))
    b = Piece(flat(b_keep), flat(b_send), sum_steps, alone=True)
    if paired:
        pieces.append(b)
    gain_in, *x_sent = back_in(ids, pg_gate, pg_rest, x_whole, residual_grad, in_weight, gain1)
    x_sent = boundary(ids, pieces, x_sent)
    output = unturn(ids, [stay] + [ref for ref, _ in moved.got], LOW, tuple(at for _, at in moved.got))
    small = jnp.concatenate([gain_in, small_out, small_conv], axis=0)
    n_small = small.shape[0] + -small.shape[0] % 16
    if paired:
        small = jnp.pad(small, ((0, n_small - small.shape[0]), (0, 0))).astype(LOW)
        small = Piece(small, small, [(first_side, "all"), (second_side, "all")], alone=True)
        pieces.append(small)
        x_sent, output = boundary(ids, pieces, (x_sent, output))
        own, *sent = by_chip(ids, a, b, small)
        own, x_sent = tie(own, x_sent)
        got = [exchange(x, lambda s, b, rel=rel: (s, b ^ (2 * rel))) for rel, x in enumerate(sent, 1)]
        x_got = [x_sent[0]] + [exchange(x_sent[r], blocks_of(r)) for r in range(1, n_seq)]
        own, sent = cut_cores(
            ids, (own, *got), [p.keep for p in ff_pieces[0::2]], [p.keep for p in ff_pieces[1::2]], n_batch, n_small
        )
        sent, x_got = tie(sent, x_got)
        theirs = exchange(sent, across)
        input_grad = unturn(ids, x_got, F32)
        theirs, input_grad = tie(theirs, input_grad)
        total_in, total_out, total_static, total_glu, total_down, total_taps, *gains = finish(
            ids, own, theirs, width, total_pos, n_batch, n_small
        )
        total_static, total_down = total_static.T, total_down.T
    else:
        x_got = [x_sent[0]] + [exchange(x_sent[r], blocks_of(r)) for r in range(1, n_seq)]
        pieces = [a, b]
        while a.steps:
            boundary(ids, pieces, ())
        top = width // 8
        in_rows = jnp.concatenate([a.keep[top:], b.keep[:top], b.keep[top : 2 * top]], axis=1)
        total_in = spread_sum(in_rows, core, 0, 0)
        total_out = spread_sum(a.keep[:top], core, 0, 0)
        total_static = spread_sum(b.keep[2 * top :], core, 0, 0)
        side = n_seq // 2
        halves = lambda x: x.reshape(2, x.shape[0] // 2, x.shape[1])
        glu = jnp.stack(
            [seq_sums(halves(c[0]), halves(c[1])).reshape(-1, side, 2, side, LANES) for c in chunks], axis=4
        )
        glu = glu.transpose(0, 2, 1, 3, 4, 5).reshape(-1, 2 * n_seq, 1, CHUNKS * LANES)
        mine = (jnp.arange(2) == core)[:, None]
        glu = jnp.where(mine, glu, 0).astype(F32).reshape(glu.shape[0], -1)
        total_glu = lax.psum_scatter(glu, "batch", scatter_dimension=1, tiled=True)
        joined = [jnp.concatenate([c[2], c[3]], axis=int(c[2].shape[0] == width)) for c in chunks]
        down = jnp.stack([d.reshape(width, n_seq, LANES) for d in joined], axis=2)
        down = down.reshape(width, n_seq, 1, CHUNKS * LANES)
        down = jnp.where(mine, down, 0).astype(F32).reshape(width, -1)
        down = lax.psum_scatter(down, "batch", scatter_dimension=0, tiled=True)
        total_down = lax.psum_scatter(down, "seq", scatter_dimension=1, tiled=True).T

        small = lax.psum(small, ("seq", "batch"))
        gains = jnp.stack([small[0], small[4]])
        total_taps = jnp.concatenate([small[1:4], small[5:8], small[8:11]], axis=1)
        input_grad = unturn(ids, x_got, F32)
    return (
        output,
        input_grad,
        gains[0],
        total_in,
        total_taps,
        total_static,
        total_out,
        gains[1],
        total_glu,
        total_down,
    )


def solution(mesh):
    return jax.shard_map(
        on_device,
        mesh=mesh,
        in_specs=(
            P("seq", "batch", None),
            P("batch"),
            P(),
            P(),
            P(),
            P(),
            P(),
            P(),
            P(),
            P(),
            P("seq", "batch", None),
        ),
        out_specs=(
            P("seq", "batch", None),
            P("seq", "batch", None),
            P(),
            P("seq", "batch"),
            P(),
            P("seq", "batch"),
            P("seq", "batch"),
            P(),
            P("seq", "batch"),
            P("seq", "batch"),
        ),
        check_vma=False,
    )
```
